32 devices in a mesh: vintage: 2 (over core), tile: 16 (over z, y, x).
Axes of the slice: x: 2, y: 2, z: 4, core: 2. Of those that a mesh axis runs over, the one named last changes fastest.
Arguments:
- patches: bfloat16 [2, 8192, 768], P('vintage', 'tile'), may hold values from -16 to 16, as said below
- out_grad: bfloat16 [2, 8192, 768], P('vintage', 'tile'), may hold values from -6 to 6
- w_query: bfloat16 [768, 768], replicated, may hold values from -0.21875 to 0.21875
- w_key: bfloat16 [768, 256], replicated, may hold values from -0.21875 to 0.21875
- w_value: bfloat16 [768, 256], replicated, may hold values from -0.21875 to 0.21875
- w_out: bfloat16 [768, 768], replicated, may hold values from -0.21875 to 0.21875
- key_tiles: int32 [2, 64, 4], P('vintage'), may hold values from 0 to 15, all different within a row; in each aligned block of 4 rows (0 to 3, 4 to 7, ..., all dimensions but the last counted through in order) at most 2 rows name the same one
- key_blocks: int32 [2, 64, 4], P('vintage'), may hold values from 0 to 3
Outputs:
- layer_out: bfloat16 [2, 8192, 768], P('vintage', 'tile')
- input_grad: bfloat16 [2, 8192, 768], P('vintage', 'tile')
The draws below stay inside these ranges and needn't reach their ends.
Inputs may be any that keep to these rules, and one draw needn't show every extreme that they name: `patches`: patch features of order one, rows of differing scale possible. `key_tiles`: the 4 tiles of one query block's list differ; over the 4 query blocks of one tile no key tile is named more than 2 times, and in every draw some tile is named exactly 2 times by some tile's blocks.
All inputs are finite; a program needn't handle non-finite values.
Results may differ from the reference program's by a relative error of at most 0.012.
The reference program's roundings to bfloat16 on the way count: a program that leaves them out, or rounds other values in their place, can miss the bound.
Values may be sent and summed in bfloat16 or wider, within the bound.
No kernel may reach another device: no remote copies, remote signals or barrier semaphores. Data moves between devices by JAX's collectives and lax.ppermute only.
A program may use at most 128 MiB of HBM per device.

```python
import math
import jax
import jax.numpy as jnp
import numpy as np
from jax import lax

D = 768
HEADS = 12
KV_HEADS = 4
HEAD_DIM = 64
BLK = 128
CAP = 2
QB = 4
LIST_LEN = 4
PATCHES = 8192
QBLOCKS = 64
N_TILE = 16


def draw_patches(key, part):
    first_key = jax.random.fold_in(jax.random.fold_in(key, 17), 0)
    base = jax.random.normal(first_key, (2, PATCHES, D), jnp.float32)
    return jnp.clip(base, -6.0, 6.0).astype(jnp.bfloat16)


def touch_ends(drawn, rng, low, top_value):
    spot = [jax.random.randint(jax.random.fold_in(rng, axis), (), 0, length) for axis, length in enumerate(drawn.shape)]
    main_axis = drawn.shape.index(max(drawn.shape))
    beside = spot[:main_axis] + [(spot[main_axis] + 1) % drawn.shape[main_axis]] + spot[main_axis + 1:]
    return drawn.at[tuple(spot)].set(low).at[tuple(beside)].set(top_value)


def levels(rng, shape, shards, smallest, largest):
    level = 1.0
    for position, blocks in shards:
        draws = jax.random.uniform(jax.random.fold_in(jax.random.fold_in(rng, 6), position), (blocks,), jnp.float32, smallest / len(shards), largest / len(shards))
        level = level * jnp.repeat(jnp.exp(draws), shape[position] // blocks).reshape((-1,) + (1,) * (len(shape) - 1 - position))
    return level


def deal_out(key, own, number, rows, number_of, top, reach, lean):
    order = jax.random.permutation(key, number_of)
    heavy_load, usual = load_shares(number_of, rows * top, reach, lean, True), load_shares(number_of, rows * top, reach, lean, False)
    places = jnp.arange(number_of)

    def named(sizes, rotation):
        used = int((sizes > 0).sum())
        fixed = max(1, used // 4)
        shifted = fixed + (places - fixed + rotation * (used - fixed)) % max(1, number_of - fixed)
        return jnp.zeros((number_of,), jnp.int32).at[order[jnp.where(places < fixed, places, shifted)]].set(jnp.asarray(sizes, jnp.int32))

    sizes = jnp.where(number % 4 == 0, named(heavy_load, number // 4), named(usual, number - number // 4 - 1))
    mixed = jax.random.permutation(jax.random.fold_in(own, 3), number_of)
    source_of, taker = mixed[0:number_of // 2 * 2:2], mixed[1:number_of // 2 * 2:2]
    margin = jnp.minimum(sizes[source_of] - 1, reach - sizes[taker]) // 2
    margin = jnp.where((source_of == order[0]) | (taker == order[0]) | (sizes[taker] == 0), 0, jnp.maximum(margin, 0))
    shifted = jax.random.randint(jax.random.fold_in(own, 4), (number_of // 2,), 0, 1 << 20) % (margin + 1)
    sizes = sizes.at[source_of].add(-shifted).at[taker].add(shifted)
    labels = jnp.searchsorted(jnp.cumsum(sizes), jnp.arange(rows * top), side="right").astype(jnp.int32)
    table = labels.reshape(top, rows).T
    table = table[jax.random.permutation(jax.random.fold_in(own, 1), rows)]
    rotation = jax.random.randint(jax.random.fold_in(own, 2), (rows, 1), 0, top)
    return jnp.take_along_axis(table, (jnp.arange(top)[None, :] + rotation) % top, axis=1)


def load_shares(number_of, total, reach, skew, full):
    loads = [(1 << 20) // math.isqrt(rank ** skew) + 1 for rank in range(1, number_of + 1)]
    largest = reach if full else min(reach, max(-(-total // number_of), total * loads[0] // sum(loads)))
    least = 1 if total - largest >= number_of - 1 else 0
    holding, rest = [largest] + [least] * (number_of - 1), total - largest - least * (number_of - 1)
    while rest > 0:
        free = [i for i in range(1, number_of) if holding[i] < largest] or [i for i in range(1, number_of) if holding[i] < reach]
        mass, remaining = sum([loads[i] for i in free]), rest
        for i in free:
            extra = min(reach - holding[i], max(1, remaining * loads[i] // mass), rest)
            holding[i] = holding[i] + extra
            rest = rest - extra
    return np.array(holding)


def centred(key, dims, scale, bound, shards=(), kind=jnp.bfloat16):
    result = jax.random.normal(key, dims, jnp.float32) * scale
    if len(shards) > 0:
        result = levels(key, dims, shards, -0.22, 0.18) * result
    return jnp.clip(result, min=-bound, max=bound).astype(kind)


def setup_inputs(seed: int = 0) -> dict:
    key_of = jax.random.split(jax.random.key(seed), 9)
    patches = draw_patches(jax.random.fold_in(key_of[8], 71), 0)
    out_grad = centred(key_of[1], (2, PATCHES, D), 1.0, 6.0, ((0, 2), (1, 16)))
    w_query = centred(key_of[2], (D, HEADS * HEAD_DIM), D ** -0.5, 0.21875)
    w_key = centred(key_of[3], (D, KV_HEADS * HEAD_DIM), D ** -0.5, 0.21875)
    w_value = centred(key_of[4], (D, KV_HEADS * HEAD_DIM), D ** -0.5, 0.21875)
    w_out = centred(key_of[5], (HEADS * HEAD_DIM, D), (HEADS * HEAD_DIM) ** -0.5, 0.21875)
    key_tiles_keys = jax.random.split(jax.random.fold_in(key_of[6], 1), 2 * QBLOCKS // QB)
    key_tiles_turns = jax.random.permutation(jax.random.fold_in(key_of[6], 3), 2 * QBLOCKS // QB)
    key_tiles = jax.vmap(lambda own, number: deal_out(jax.random.fold_in(key_of[6], 2), own, number, QB, N_TILE, LIST_LEN, CAP, 2))(key_tiles_keys, key_tiles_turns).reshape((2, QBLOCKS, LIST_LEN))
    key_blocks = touch_ends(jax.random.randint(key_of[7], (2, QBLOCKS, LIST_LEN), 0, QB), jax.random.fold_in(key_of[7], 1), 0, QB - 1).astype(jnp.int32)
    return dict(patches=patches, out_grad=out_grad, w_query=w_query, w_key=w_key, w_value=w_value, w_out=w_out, key_tiles=key_tiles, key_blocks=key_blocks)


EPSILON = 1e-06

def attend_block(query_rows, grad_rows, key_value, w_out):
    kv_width = KV_HEADS * HEAD_DIM
    group_size = HEADS // KV_HEADS
    temper = HEAD_DIM ** (-0.5)
    row_count = query_rows.shape[0]
    keys_f = key_value[:, :kv_width].astype(jnp.float32).reshape(-1, KV_HEADS, HEAD_DIM)
    values_f = key_value[:, kv_width:].astype(jnp.float32).reshape(-1, KV_HEADS, HEAD_DIM)
    query_f = query_rows.astype(jnp.float32).reshape(row_count, KV_HEADS, group_size, HEAD_DIM)
    scores = jnp.einsum('igrd,ngd->grin', query_f, keys_f) * temper
    peak = lax.optimization_barrier(jnp.max(scores, axis=-1, keepdims=True))
    expo = jnp.exp(scores - peak)
    probs = expo / lax.optimization_barrier(jnp.sum(expo, axis=-1, keepdims=True))
    probs_low = lax.optimization_barrier(probs.astype(jnp.bfloat16))
    probs_lf = probs_low.astype(jnp.float32)
    attended = jnp.einsum('grin,ngd->igrd', probs_lf, values_f).reshape(row_count, HEADS * HEAD_DIM)
    attended = lax.optimization_barrier(attended.astype(jnp.bfloat16))
    attended_f = attended.astype(jnp.float32)
    root_mean = jnp.sqrt(lax.optimization_barrier(jnp.mean(attended_f * attended_f, axis=-1, keepdims=True)) + EPSILON)
    normed = attended_f / root_mean
    layer_rows = jnp.dot(normed.astype(jnp.bfloat16), w_out, preferred_element_type=jnp.float32).astype(jnp.bfloat16)
    normed_grad = jnp.dot(grad_rows, w_out.T, preferred_element_type=jnp.float32)
    attended_grad = (normed_grad - normed * lax.optimization_barrier(jnp.mean(normed_grad * normed, axis=-1, keepdims=True))) / root_mean
    attended_grad = lax.optimization_barrier(attended_grad.astype(jnp.bfloat16))
    grad_f = attended_grad.astype(jnp.float32).reshape(row_count, KV_HEADS, group_size, HEAD_DIM)
    prob_grad = jnp.einsum('igrd,ngd->grin', grad_f, values_f)
    row_dot = lax.optimization_barrier(jnp.sum(probs * prob_grad, axis=-1, keepdims=True))
    score_grad = lax.optimization_barrier((probs * (prob_grad - row_dot) * temper).astype(jnp.bfloat16))
    score_f = score_grad.astype(jnp.float32)
    query_grad = jnp.einsum('grin,ngd->igrd', score_f, keys_f).reshape(row_count, HEADS * HEAD_DIM).astype(jnp.bfloat16)
    key_part = jnp.einsum('grin,igrd->ngd', score_f, query_f).reshape(-1, kv_width)
    value_part = jnp.einsum('grin,igrd->ngd', probs_lf, grad_f).reshape(-1, kv_width)
    parts = jnp.concatenate([key_part, value_part], axis=-1).astype(jnp.bfloat16)
    return (layer_rows, query_grad, parts.reshape(-1, row_count, 2 * kv_width))

def reference(patches, out_grad, w_query, w_key, w_value, w_out, key_tiles, key_blocks):
    kv_width = KV_HEADS * HEAD_DIM
    kv_cubes = []
    for vintage in range(2):
        keys = jnp.dot(patches[vintage], w_key, preferred_element_type=jnp.float32).astype(jnp.bfloat16)
        values = jnp.dot(patches[vintage], w_value, preferred_element_type=jnp.float32).astype(jnp.bfloat16)
        kv_cubes.append(jnp.concatenate([keys, values], axis=-1).reshape(QBLOCKS, BLK, 2 * kv_width))
    kv_terms = [None, None]
    layer_outs = []
    query_grads = []
    for vintage in range(2):
        other = 1 - vintage
        queries = jnp.dot(patches[vintage], w_query, preferred_element_type=jnp.float32).astype(jnp.bfloat16)
        queries = queries.reshape(QBLOCKS, BLK, HEADS * HEAD_DIM)
        grads = out_grad[vintage].reshape(QBLOCKS, BLK, D)
        block_ids = (key_tiles[vintage].astype(jnp.int32) * QB + key_blocks[vintage].astype(jnp.int32)).astype(jnp.int32)
        source = kv_cubes[other]

        def step(summed, item):
            query_rows, grad_rows, entry_ids = item
            key_value = source[entry_ids].reshape(-1, 2 * kv_width)
            layer_rows, query_grad, parts = attend_block(query_rows, grad_rows, key_value, w_out)
            summed = summed.at[entry_ids].add(parts.astype(jnp.float32))
            return (summed, (layer_rows, query_grad))
        start = jnp.zeros((QBLOCKS, BLK, 2 * kv_width), jnp.float32)
        summed, (layer_rows, query_grad) = lax.scan(step, start, (queries, grads, block_ids))
        kv_grad = summed.astype(jnp.bfloat16).reshape(PATCHES, 2 * kv_width)
        kv_terms[other] = jnp.dot(kv_grad[:, :kv_width], w_key.T, preferred_element_type=jnp.float32) + jnp.dot(kv_grad[:, kv_width:], w_value.T, preferred_element_type=jnp.float32)
        layer_outs.append(layer_rows.reshape(PATCHES, D))
        query_grads.append(query_grad.reshape(PATCHES, HEADS * HEAD_DIM))
    input_grads = []
    for vintage in range(2):
        total = jnp.dot(query_grads[vintage], w_query.T, preferred_element_type=jnp.float32) + kv_terms[vintage]
        input_grads.append(total.astype(jnp.bfloat16))
    return (jnp.stack(layer_outs), jnp.stack(input_grads))
```

```python
import functools

import jax
import jax.numpy as jnp
from jax import lax
from jax.experimental import pallas as pl
from jax.experimental.pallas import tpu as pltpu
from jax.sharding import PartitionSpec as P

HEADS = 12
KV_HEADS = 4
HEAD_DIM = 64
BLK = 128
CAP = 2
GROUP = HEADS // KV_HEADS
KV = KV_HEADS * HEAD_DIM
TEMPER = HEAD_DIM ** (-0.5)
EPSILON = 1e-06
F32 = jnp.float32
BF16 = jnp.bfloat16


def dot_nt(a, b):
    return lax.dot_general(a, b, (((1,), (1,)), ((), ())), preferred_element_type=F32)


def dot_tn(a, b):
    return lax.dot_general(a, b, (((0,), (0,)), ((), ())), preferred_element_type=F32)


def stack_heads(rows, g):
    first = g * GROUP * HEAD_DIM
    return jnp.concatenate(
        [rows[:, first + r * HEAD_DIM : first + (r + 1) * HEAD_DIM] for r in range(GROUP)], axis=0
    )


def spread_heads(stacked):
    return jnp.concatenate([stacked[r * BLK : (r + 1) * BLK] for r in range(GROUP)], axis=1)


def attention_kernel(list_len, slot_ref, q_ref, ng_ref, *refs):
    kv_refs = refs[:list_len]
    normed_ref, qg_ref, back_ref, probs_scr, parts_scr, sems = refs[list_len:]
    step = pl.program_id(0)
    keys = jnp.concatenate([ref[0, :, :KV] for ref in kv_refs], axis=0)
    values = jnp.concatenate([ref[0, :, KV:] for ref in kv_refs], axis=0)
    queries = q_ref[...] * jnp.asarray(TEMPER, BF16)
    attended = []
    for g in range(KV_HEADS):
        cols = slice(g * HEAD_DIM, (g + 1) * HEAD_DIM)
        scores = dot_nt(stack_heads(queries, g), keys[:, cols])
        expo = jnp.exp(scores - jnp.max(scores, axis=-1, keepdims=True))
        probs = expo * (1.0 / jnp.sum(expo, axis=-1, keepdims=True))
        probs_scr[g] = probs
        out = jnp.dot(probs.astype(BF16), values[:, cols], preferred_element_type=F32)
        attended.append(spread_heads(out.astype(BF16)))
    attended = jnp.concatenate(attended, axis=1).astype(F32)
    width = attended.shape[1]
    inverse = lax.rsqrt(jnp.sum(attended * attended, axis=-1, keepdims=True) / width + EPSILON)
    normed = attended * inverse
    normed_ref[...] = normed.astype(BF16)
    normed_grad = ng_ref[...]
    shared = jnp.sum(normed_grad * normed, axis=-1, keepdims=True) / width
    attended_grad = ((normed_grad - normed * shared) * inverse).astype(BF16)
    for g in range(KV_HEADS):
        cols = slice(g * HEAD_DIM, (g + 1) * HEAD_DIM)
        out_grad = stack_heads(attended_grad, g)
        prob_grad = dot_nt(out_grad, values[:, cols])
        probs = probs_scr[g]
        row_dot = jnp.sum(probs * prob_grad, axis=-1, keepdims=True)
        score_grad = (probs * (prob_grad - row_dot)).astype(BF16)
        query_grad = jnp.dot(score_grad, keys[:, cols], preferred_element_type=F32) * TEMPER
        first = g * GROUP * HEAD_DIM
        qg_ref[:, first : first + GROUP * HEAD_DIM] = spread_heads(query_grad.astype(BF16))
        key_part = dot_tn(score_grad, stack_heads(queries, g)).astype(BF16)
        value_part = dot_tn(probs.astype(BF16), out_grad).astype(BF16)
        for l in range(list_len):
            rows = slice(l * BLK, (l + 1) * BLK)
            parts_scr[step, l, :, g * HEAD_DIM : (g + 1) * HEAD_DIM] = key_part[rows]
            parts_scr[step, l, :, KV + g * HEAD_DIM : KV + (g + 1) * HEAD_DIM] = value_part[rows]

    def copy(s, l):
        return pltpu.make_async_copy(
            parts_scr.at[s, l], back_ref.at[slot_ref[s * list_len + l]], sems.at[s, l]
        )

    for l in range(list_len):
        copy(step, l).start()

    @pl.when(step == pl.num_programs(0) - 1)
    def _():
        for s in range(sems.shape[0]):
            for l in range(list_len):
                copy(s, l).wait()


def attention(slots, queries, normed_grad, arrived, list_len):
    rows, width = queries.shape
    blocks = rows // BLK
    row_spec = pl.BlockSpec((BLK, width), lambda r, s: (r, 0))

    def entry_spec(l):
        return pl.BlockSpec((1, BLK, 2 * KV), lambda r, s: (s[r * list_len + l], 0, 0))

    keys = list_len * BLK
    pairs = HEADS * rows * keys
    return pl.pallas_call(
        functools.partial(attention_kernel, list_len),
        grid_spec=pltpu.PrefetchScalarGridSpec(
            num_scalar_prefetch=1,
            grid=(blocks,),
            in_specs=[row_spec, row_spec] + [entry_spec(l) for l in range(list_len)],
            out_specs=[row_spec, row_spec, pl.BlockSpec(memory_space=pl.ANY)],
            scratch_shapes=[
                pltpu.VMEM((KV_HEADS, GROUP * BLK, keys), F32),
                pltpu.VMEM((blocks, list_len, BLK, 2 * KV), BF16),
                pltpu.SemaphoreType.DMA((blocks, list_len)),
            ],
        ),
        out_shape=[
            jax.ShapeDtypeStruct((rows, width), BF16),
            jax.ShapeDtypeStruct((rows, width), BF16),
            jax.ShapeDtypeStruct(arrived.shape, BF16),
        ],
        compiler_params=pltpu.CompilerParams(vmem_limit_bytes=56 * 1024 * 1024),
        cost_estimate=pl.CostEstimate(
            flops=12 * pairs * HEAD_DIM, bytes_accessed=16 * rows * width, transcendentals=pairs
        ),
        name="attention",
    )(slots, queries, normed_grad, *([arrived] * list_len))


def owner_kernel(chunk, wanted_ref, parts_ref, out_ref, total):
    step = pl.program_id(0)

    @pl.when(step == 0)
    def _():
        total[...] = jnp.zeros_like(total)

    for s in range(chunk):
        block = wanted_ref[step * chunk + s]

        @pl.when(block >= 0)
        def _():
            total[block] += parts_ref[s].astype(F32)

    @pl.when(step == pl.num_programs(0) - 1)
    def _():
        out_ref[...] = total[...].astype(BF16)


def owner_sum(wanted, returned, blocks):
    slots = returned.shape[0]
    chunk = 4
    return pl.pallas_call(
        functools.partial(owner_kernel, chunk),
        grid_spec=pltpu.PrefetchScalarGridSpec(
            num_scalar_prefetch=1,
            grid=(slots // chunk,),
            in_specs=[pl.BlockSpec((chunk, BLK, 2 * KV), lambda s, w: (s, 0, 0))],
            out_specs=pl.BlockSpec((blocks, BLK, 2 * KV), lambda s, w: (0, 0, 0)),
            scratch_shapes=[pltpu.VMEM((blocks, BLK, 2 * KV), F32)],
        ),
        out_shape=jax.ShapeDtypeStruct((blocks, BLK, 2 * KV), BF16),
        compiler_params=pltpu.CompilerParams(vmem_limit_bytes=24 * 1024 * 1024),
        name="owner_sum",
    )(wanted, returned)


def slot_index(entry_tiles, tile_count):
    one_hot = (entry_tiles[:, None] == jnp.arange(tile_count, dtype=jnp.int32)[None, :]).astype(
        jnp.int32
    )
    ranks = jnp.cumsum(one_hot, axis=0) - 1
    return jnp.sum(one_hot * ranks, axis=1)


def from_partner(value):
    return lax.ppermute(value, "vintage", [(0, 1), (1, 0)])


def shards(patches, out_grad, w_query, w_key, w_value, w_out, key_tiles, key_blocks):
    tokens = patches[0]
    rows = tokens.shape[0]
    tile_count = lax.axis_size("tile")
    my_tile = lax.axis_index("tile")
    block_count = rows // BLK
    list_len = key_tiles.shape[2]
    entry_count = block_count * list_len
    keys = jnp.dot(tokens, w_key, preferred_element_type=F32).astype(BF16)
    values = jnp.dot(tokens, w_value, preferred_element_type=F32).astype(BF16)
    partner = from_partner(jnp.concatenate([keys, values], axis=-1))
    partner_blocks = partner.reshape(block_count, BLK, 2 * KV)
    my_tiles = lax.dynamic_slice_in_dim(
        key_tiles[0], my_tile * block_count, block_count, 0
    ).reshape(-1)
    flat_slot = my_tiles * CAP + slot_index(my_tiles, tile_count)
    all_tiles = key_tiles[0].reshape(tile_count, entry_count)
    all_blocks = key_blocks[0].reshape(tile_count, entry_count)
    asking = (all_tiles == my_tile).astype(jnp.int32)
    ranks = jnp.cumsum(asking, axis=1) - 1
    slot_range = jnp.arange(CAP, dtype=jnp.int32)
    hits = (asking[:, :, None] == 1) & (ranks[:, :, None] == slot_range[None, None, :])
    wanted = (jnp.sum(jnp.where(hits, all_blocks[:, :, None] + 1, 0), axis=1) - 1).reshape(-1)
    send = partner_blocks[jnp.clip(wanted, 0, block_count - 1)]
    arrived = lax.all_to_all(send, "tile", split_axis=0, concat_axis=0, tiled=True)
    queries = jnp.dot(tokens, w_query, preferred_element_type=F32).astype(BF16)
    normed_grad = dot_nt(out_grad[0], w_out)
    normed_low, query_grad, back = attention(flat_slot, queries, normed_grad, arrived, list_len)
    returned = lax.all_to_all(back, "tile", split_axis=0, concat_axis=0, tiled=True)
    layer_out = jnp.dot(normed_low, w_out, preferred_element_type=F32).astype(BF16)
    query_term = dot_nt(query_grad, w_query)
    kv_grad = owner_sum(wanted, returned, block_count).reshape(rows, 2 * KV)
    kv_grad = from_partner(kv_grad)
    kv_term = dot_nt(kv_grad[:, :KV], w_key) + dot_nt(kv_grad[:, KV:], w_value)
    input_grad = (query_term + kv_term).astype(BF16)
    return (layer_out[None], input_grad[None])


def solution(mesh):
    in_specs = (
        P("vintage", "tile", None),
        P("vintage", "tile", None),
        P(),
        P(),
        P(),
        P(),
        P("vintage", None, None),
        P("vintage", None, None),
    )
    out_specs = (P("vintage", "tile", None), P("vintage", "tile", None))
    return jax.shard_map(shards, mesh=mesh, in_specs=in_specs, out_specs=out_specs, check_vma=False)
```

```python
import functools

import jax
import jax.numpy as jnp
from jax import lax
from jax.experimental import pallas as pl
from jax.experimental.pallas import tpu as pltpu
from jax.sharding import PartitionSpec as P

HEADS = 12
KV_HEADS = 4
HEAD_DIM = 64
BLK = 128
CAP = 2
MAJOR = 4
CHUNKS = 2
GROUP = HEADS // KV_HEADS
KV = KV_HEADS * HEAD_DIM
TEMPER = HEAD_DIM ** (-0.5)
EPSILON = 1e-06
PER_CHUNK = KV_HEADS // CHUNKS
HALF = PER_CHUNK * HEAD_DIM
F32 = jnp.float32
BF16 = jnp.bfloat16


def dot_nt(a, b):
    return lax.dot_general(a, b, (((1,), (1,)), ((), ())), preferred_element_type=F32)


def dot_tn(a, b):
    return lax.dot_general(a, b, (((0,), (0,)), ((), ())), preferred_element_type=F32)


def stack_heads(rows, g):
    first = g * GROUP * HEAD_DIM
    return jnp.concatenate(
        [rows[:, first + r * HEAD_DIM : first + (r + 1) * HEAD_DIM] for r in range(GROUP)], axis=0
    )


def spread_heads(stacked):
    return jnp.concatenate([stacked[r * BLK : (r + 1) * BLK] for r in range(GROUP)], axis=1)


def attention_kernel(list_len, slot_ref, q_ref, ng_ref, *refs):
    kv_refs = refs[: CHUNKS * list_len]
    normed_ref, qg_ref = refs[CHUNKS * list_len : CHUNKS * list_len + 2]
    back_refs = refs[CHUNKS * list_len + 2 : CHUNKS * list_len + 2 + CHUNKS]
    probs_scr, parts_scr, sems = refs[-3:]
    step = pl.program_id(0)
    queries = q_ref[...] * jnp.asarray(TEMPER, BF16)
    keys, values, attended = [], [], []
    for c in range(CHUNKS):
        entries = kv_refs[c * list_len : (c + 1) * list_len]
        rows = jnp.concatenate([ref[0] for ref in entries], axis=0)
        for k in range(PER_CHUNK):
            keys.append(rows[:, k * HEAD_DIM : (k + 1) * HEAD_DIM])
            values.append(rows[:, HALF + k * HEAD_DIM : HALF + (k + 1) * HEAD_DIM])
    for g in range(KV_HEADS):
        scores = dot_nt(stack_heads(queries, g), keys[g])
        expo = jnp.exp(scores - jnp.max(scores, axis=-1, keepdims=True))
        probs = expo * (1.0 / jnp.sum(expo, axis=-1, keepdims=True))
        probs_scr[g] = probs
        out = jnp.dot(probs.astype(BF16), values[g], preferred_element_type=F32)
        attended.append(spread_heads(out.astype(BF16)))
    attended = jnp.concatenate(attended, axis=1).astype(F32)
    width = attended.shape[1]
    inverse = lax.rsqrt(jnp.sum(attended * attended, axis=-1, keepdims=True) / width + EPSILON)
    normed = attended * inverse
    normed_ref[...] = normed.astype(BF16)
    normed_grad = ng_ref[...]
    shared = jnp.sum(normed_grad * normed, axis=-1, keepdims=True) / width
    attended_grad = ((normed_grad - normed * shared) * inverse).astype(BF16)
    for g in range(KV_HEADS):
        out_grad = stack_heads(attended_grad, g)
        prob_grad = dot_nt(out_grad, values[g])
        probs = probs_scr[g]
        row_dot = jnp.sum(probs * prob_grad, axis=-1, keepdims=True)
        score_grad = (probs * (prob_grad - row_dot)).astype(BF16)
        query_grad = jnp.dot(score_grad, keys[g], preferred_element_type=F32) * TEMPER
        first = g * GROUP * HEAD_DIM
        qg_ref[:, first : first + GROUP * HEAD_DIM] = spread_heads(query_grad.astype(BF16))
        key_part = dot_tn(score_grad, stack_heads(queries, g)).astype(BF16)
        value_part = dot_tn(probs.astype(BF16), out_grad).astype(BF16)
        c, k = g // PER_CHUNK, (g % PER_CHUNK) * HEAD_DIM
        for l in range(list_len):
            rows = slice(l * BLK, (l + 1) * BLK)
            parts_scr[c, step, l, :, k : k + HEAD_DIM] = key_part[rows]
            parts_scr[c, step, l, :, HALF + k : HALF + k + HEAD_DIM] = value_part[rows]

    def copy(c, s, l):
        return pltpu.make_async_copy(
            parts_scr.at[c, s, l],
            back_refs[c].at[slot_ref[s * list_len + l]],
            sems.at[c, s, l],
        )

    for c in range(CHUNKS):
        for l in range(list_len):
            copy(c, step, l).start()

    @pl.when(step == pl.num_programs(0) - 1)
    def _():
        for c in range(CHUNKS):
            for s in range(sems.shape[1]):
                for l in range(list_len):
                    copy(c, s, l).wait()


def attention(slots, queries, normed_grad, arrived, list_len):
    rows, width = queries.shape
    blocks = rows // BLK
    row_spec = pl.BlockSpec((BLK, width), lambda r, s: (r, 0))

    def entry_spec(l):
        return pl.BlockSpec((1, BLK, 2 * HALF), lambda r, s: (s[r * list_len + l], 0, 0))

    keys = list_len * BLK
    pairs = HEADS * rows * keys
    entry_specs = [entry_spec(l) for _ in range(CHUNKS) for l in range(list_len)]
    entry_args = [chunk for chunk in arrived for _ in range(list_len)]
    return pl.pallas_call(
        functools.partial(attention_kernel, list_len),
        grid_spec=pltpu.PrefetchScalarGridSpec(
            num_scalar_prefetch=1,
            grid=(blocks,),
            in_specs=[row_spec, row_spec] + entry_specs,
            out_specs=[row_spec, row_spec] + [pl.BlockSpec(memory_space=pl.ANY)] * CHUNKS,
            scratch_shapes=[
                pltpu.VMEM((KV_HEADS, GROUP * BLK, keys), F32),
                pltpu.VMEM((CHUNKS, blocks, list_len, BLK, 2 * HALF), BF16),
                pltpu.SemaphoreType.DMA((CHUNKS, blocks, list_len)),
            ],
        ),
        out_shape=[
            jax.ShapeDtypeStruct((rows, width), BF16),
            jax.ShapeDtypeStruct((rows, width), BF16),
        ]
        + [jax.ShapeDtypeStruct(arrived[0].shape, BF16)] * CHUNKS,
        compiler_params=pltpu.CompilerParams(vmem_limit_bytes=56 * 1024 * 1024),
        cost_estimate=pl.CostEstimate(
            flops=12 * pairs * HEAD_DIM, bytes_accessed=16 * rows * width, transcendentals=pairs
        ),
        name="attention",
    )(slots, queries, normed_grad, *entry_args)


def column_kernel(chunk, place_ref, parts_ref, out_ref, total):
    step = pl.program_id(0)

    @pl.when(step == 0)
    def _():
        total[...] = jnp.zeros_like(total)

    for s in range(chunk):
        block = place_ref[step * chunk + s]

        @pl.when(block >= 0)
        def _():
            total[block] += parts_ref[s].astype(F32)

    @pl.when(step == pl.num_programs(0) - 1)
    def _():
        out_ref[...] = total[...].astype(BF16)


def column_sum(place, returned, blocks):
    slots, _, width = returned.shape
    chunk = 8
    return pl.pallas_call(
        functools.partial(column_kernel, chunk),
        grid_spec=pltpu.PrefetchScalarGridSpec(
            num_scalar_prefetch=1,
            grid=(slots // chunk,),
            in_specs=[pl.BlockSpec((chunk, BLK, width), lambda s, w: (s, 0, 0))],
            out_specs=pl.BlockSpec((blocks, BLK, width), lambda s, w: (0, 0, 0)),
            scratch_shapes=[pltpu.VMEM((blocks, BLK, width), F32)],
        ),
        out_shape=jax.ShapeDtypeStruct((blocks, BLK, width), BF16),
        compiler_params=pltpu.CompilerParams(vmem_limit_bytes=24 * 1024 * 1024),
        name="column_sum",
    )(place, returned)


def from_partner(value):
    return lax.ppermute(value, "vintage", [(0, 1), (1, 0)])


def exchange(value, groups):
    return lax.all_to_all(
        value, "tile", split_axis=0, concat_axis=0, tiled=True, axis_index_groups=groups
    )


def shards(patches, out_grad, w_query, w_key, w_value, w_out, key_tiles, key_blocks):
    tokens = patches[0]
    rows = tokens.shape[0]
    tile_count = lax.axis_size("tile")
    plane = tile_count // MAJOR
    my_tile = lax.axis_index("tile")
    my_row, my_place = my_tile // plane, my_tile % plane
    columns = [[z * plane + c for z in range(MAJOR)] for c in range(plane)]
    planes = [[z * plane + c for c in range(plane)] for z in range(MAJOR)]
    block_count = rows // BLK
    list_len = key_tiles.shape[2]
    entry_count = block_count * list_len

    def plane_rows(table):
        table = table[0].reshape(MAJOR, plane, entry_count)
        return lax.dynamic_index_in_dim(table, my_row, 0, keepdims=False)

    tiles, picks = plane_rows(key_tiles), plane_rows(key_blocks)
    earlier = jnp.arange(entry_count)[:, None] > jnp.arange(entry_count)[None, :]
    same = (tiles[:, :, None] == tiles[:, None, :]) & earlier[None]
    ranks = jnp.sum(same.astype(jnp.int32), axis=2)
    slots = ((tiles % plane) * MAJOR + tiles // plane) * CAP + ranks
    my_slots = lax.dynamic_index_in_dim(slots, my_place, 0, keepdims=False)
    ids = jnp.arange(MAJOR * CAP, dtype=jnp.int32)
    hits = slots[:, None, :] == my_place * (MAJOR * CAP) + ids[None, :, None]
    place = jnp.sum(jnp.where(hits, picks[:, None, :] + 1, 0), axis=2) - 1
    place = jnp.where(place >= 0, (ids // CAP)[None, :] * block_count + place, -1).reshape(-1)
    picked = jnp.maximum(place, 0)

    arrived = []
    for c in range(CHUNKS):
        cols = slice(c * HALF, (c + 1) * HALF)
        weight = jnp.concatenate([w_key[:, cols], w_value[:, cols]], axis=1)
        mine = jnp.dot(tokens, weight, preferred_element_type=F32).astype(BF16)
        whole = lax.all_gather(
            from_partner(mine), "tile", axis_index_groups=columns, tiled=True
        ).reshape(MAJOR * block_count, BLK, 2 * HALF)
        arrived.append(exchange(whole[picked], planes))
    queries = jnp.dot(tokens, w_query, preferred_element_type=F32).astype(BF16)
    normed_grad = dot_nt(out_grad[0], w_out)
    normed_low, query_grad, *back = attention(my_slots, queries, normed_grad, arrived, list_len)
    layer_out = jnp.dot(normed_low, w_out, preferred_element_type=F32).astype(BF16)
    total = dot_nt(query_grad, w_query)
    for c in range(CHUNKS):
        cols = slice(c * HALF, (c + 1) * HALF)
        sums = column_sum(place, exchange(back[c], planes), MAJOR * block_count)
        own = exchange(sums, columns).reshape(MAJOR, rows, 2 * HALF)
        kv_grad = from_partner(jnp.sum(own.astype(F32), axis=0).astype(BF16))
        total += dot_nt(kv_grad[:, :HALF], w_key[:, cols]) + dot_nt(kv_grad[:, HALF:], w_value[:, cols])
    return (layer_out[None], total.astype(BF16)[None])


def solution(mesh):
    in_specs = (
        P("vintage", "tile", None),
        P("vintage", "tile", None),
        P(),
        P(),
        P(),
        P(),
        P("vintage", None, None),
        P("vintage", None, None),
    )
    out_specs = (P("vintage", "tile", None), P("vintage", "tile", None))
    return jax.shard_map(shards, mesh=mesh, in_specs=in_specs, out_specs=out_specs, check_vma=False)
```

```python
import functools

import jax
import jax.numpy as jnp
from jax import lax
from jax.experimental import pallas as pl
from jax.experimental.pallas import tpu as pltpu
from jax.sharding import PartitionSpec as P

HEADS = 12
KV_HEADS = 4
HEAD_DIM = 64
BLK = 128
CAP = 2
MAJOR = 4
GROUP = HEADS // KV_HEADS
GROUP_WIDTH = GROUP * HEAD_DIM
WIDE = 2 * HEAD_DIM
TEMPER = HEAD_DIM ** (-0.5)
EPSILON = 1e-06
F32 = jnp.float32
BF16 = jnp.bfloat16
AXES = ("vintage", "tile")
WHOLE = pl.BlockSpec(memory_space=pltpu.VMEM)


def dot_nt(a, b):
    return lax.dot_general(a, b, (((1,), (1,)), ((), ())), preferred_element_type=F32)


def dot_tn(a, b):
    return lax.dot_general(a, b, (((0,), (0,)), ((), ())), preferred_element_type=F32)


def stack_heads(rows):
    return jnp.concatenate(
        [rows[:, r * HEAD_DIM : (r + 1) * HEAD_DIM] for r in range(GROUP)], axis=0
    )


def spread_heads(stacked):
    return jnp.concatenate([stacked[r * BLK : (r + 1) * BLK] for r in range(GROUP)], axis=1)


def params(mebibytes):
    return pltpu.CompilerParams(vmem_limit_bytes=mebibytes * 1024 * 1024)


def pack_kernel(peers, row_ref, place_ref, own, up1, down1, far2, far3, *refs):
    outs, column = refs[:peers], refs[peers]
    row = row_ref[0]
    column[row] = own[...]

    @pl.when(row > 0)
    def _():
        column[jnp.maximum(row - 1, 0)] = up1[...]

    @pl.when(row < MAJOR - 1)
    def _():
        column[jnp.minimum(row + 1, MAJOR - 1)] = down1[...]

    column[(row + 2) % MAJOR] = far2[...]

    @pl.when((row == 0) | (row == MAJOR - 1))
    def _():
        column[MAJOR - 1 - row] = far3[...]

    for p in range(peers):
        for i in range(MAJOR * CAP):
            block = jnp.maximum(place_ref[p * MAJOR * CAP + i], 0)
            outs[p][i] = column[i // CAP, block]


def pack(row, place, tiles, peers):
    blocks = tiles[0].shape[0]
    smem = pl.BlockSpec(memory_space=pltpu.SMEM)
    return pl.pallas_call(
        functools.partial(pack_kernel, peers),
        in_specs=[smem, smem] + [WHOLE] * 5,
        out_specs=[WHOLE] * peers,
        out_shape=[jax.ShapeDtypeStruct((MAJOR * CAP, BLK, WIDE), BF16)] * peers,
        scratch_shapes=[pltpu.VMEM((MAJOR, blocks, BLK, WIDE), BF16)],
        compiler_params=params(16),
        name="pack",
    )(row, place, *tiles)


def forward_kernel(g, list_len, peers, slot_ref, q_ref, *refs):
    sources = refs[:peers]
    attended_ref, probs_ref, kv_ref = refs[peers:]
    step = pl.program_id(0)
    per_peer = MAJOR * CAP
    for l in range(list_len):
        slot = slot_ref[step * list_len + l]
        for p in range(peers):

            @pl.when(slot // per_peer == p)
            def _():
                kv_ref[0, l * BLK : (l + 1) * BLK, :] = sources[p][slot % per_peer]

    rows = kv_ref[0]
    queries = q_ref[:, g * GROUP_WIDTH : (g + 1) * GROUP_WIDTH] * jnp.asarray(TEMPER, BF16)
    scores = dot_nt(stack_heads(queries), rows[:, :HEAD_DIM])
    expo = jnp.exp(scores - jnp.max(scores, axis=-1, keepdims=True))
    probs = expo * (1.0 / jnp.sum(expo, axis=-1, keepdims=True))
    probs_ref[0] = probs
    out = jnp.dot(probs.astype(BF16), rows[:, HEAD_DIM:], preferred_element_type=F32)
    attended_ref[...] = spread_heads(out.astype(BF16))


def forward(g, slots, queries, sources, list_len):
    rows, width = queries.shape
    blocks = rows // BLK
    keys = list_len * BLK
    pairs = GROUP * rows * keys
    return pl.pallas_call(
        functools.partial(forward_kernel, g, list_len, len(sources)),
        grid_spec=pltpu.PrefetchScalarGridSpec(
            num_scalar_prefetch=1,
            grid=(blocks,),
            in_specs=[pl.BlockSpec((BLK, width), lambda r, s: (r, 0))]
            + [pl.BlockSpec(x.shape, lambda r, s: (0, 0, 0)) for x in sources],
            out_specs=[
                pl.BlockSpec((BLK, GROUP_WIDTH), lambda r, s: (r, 0)),
                pl.BlockSpec((1, GROUP * BLK, keys), lambda r, s: (r, 0, 0)),
                pl.BlockSpec((1, keys, WIDE), lambda r, s: (r, 0, 0)),
            ],
        ),
        out_shape=[
            jax.ShapeDtypeStruct((rows, GROUP_WIDTH), BF16),
            jax.ShapeDtypeStruct((blocks, GROUP * BLK, keys), F32),
            jax.ShapeDtypeStruct((blocks, keys, WIDE), BF16),
        ],
        compiler_params=params(48),
        cost_estimate=pl.CostEstimate(
            flops=4 * pairs * HEAD_DIM, bytes_accessed=4 * pairs, transcendentals=pairs
        ),
        name="forward",
    )(slots, queries, *sources)


def norm_kernel(ng_ref, *refs):
    attended_refs, (normed_ref, ag_ref) = refs[:KV_HEADS], refs[KV_HEADS:]
    attended = jnp.concatenate([ref[...] for ref in attended_refs], axis=1).astype(F32)
    width = attended.shape[1]
    inverse = lax.rsqrt(jnp.sum(attended * attended, axis=-1, keepdims=True) / width + EPSILON)
    normed = attended * inverse
    normed_ref[...] = normed.astype(BF16)
    normed_grad = ng_ref[...]
    shared = jnp.sum(normed_grad * normed, axis=-1, keepdims=True) / width
    ag_ref[...] = ((normed_grad - normed * shared) * inverse).astype(BF16)


def normalise(normed_grad, attended):
    rows, width = normed_grad.shape
    spec = pl.BlockSpec((BLK, width), lambda r: (r, 0))
    return pl.pallas_call(
        norm_kernel,
        grid=(rows // BLK,),
        in_specs=[spec] + [pl.BlockSpec((BLK, GROUP_WIDTH), lambda r: (r, 0))] * KV_HEADS,
        out_specs=[spec, spec],
        out_shape=[jax.ShapeDtypeStruct((rows, width), BF16)] * 2,
        compiler_params=params(16),
        name="norm",
    )(normed_grad, *attended)


def backward_kernel(g, list_len, peers, slot_ref, q_ref, ag_ref, probs_ref, kv_ref, qg_ref, *outs):
    step = pl.program_id(0)
    per_peer = MAJOR * CAP
    cols = slice(g * GROUP_WIDTH, (g + 1) * GROUP_WIDTH)
    queries = stack_heads(q_ref[:, cols] * jnp.asarray(TEMPER, BF16))
    out_grad = stack_heads(ag_ref[:, cols])
    rows = kv_ref[0]
    probs = probs_ref[0]
    prob_grad = dot_nt(out_grad, rows[:, HEAD_DIM:])
    row_dot = jnp.sum(probs * prob_grad, axis=-1, keepdims=True)
    score_grad = (probs * (prob_grad - row_dot)).astype(BF16)
    query_grad = jnp.dot(score_grad, rows[:, :HEAD_DIM], preferred_element_type=F32) * TEMPER
    qg_ref[...] = spread_heads(query_grad.astype(BF16))
    key_part = dot_tn(score_grad, queries)
    value_part = dot_tn(probs.astype(BF16), out_grad)
    parts = jnp.concatenate([key_part, value_part], axis=1).astype(BF16)
    for l in range(list_len):
        slot = slot_ref[step * list_len + l]
        for p in range(peers):

            @pl.when(slot // per_peer == p)
            def _():
                outs[p][slot % per_peer] = parts[l * BLK : (l + 1) * BLK]


def backward(g, slots, queries, attended_grad, probs, kv, peers):
    rows, width = queries.shape
    blocks, _, keys = probs.shape
    list_len = keys // BLK
    pairs = GROUP * rows * keys
    row_spec = pl.BlockSpec((BLK, width), lambda r, s: (r, 0))
    per_peer = (MAJOR * CAP, BLK, WIDE)
    return pl.pallas_call(
        functools.partial(backward_kernel, g, list_len, peers),
        grid_spec=pltpu.PrefetchScalarGridSpec(
            num_scalar_prefetch=1,
            grid=(blocks,),
            in_specs=[
                row_spec,
                row_spec,
                pl.BlockSpec((1, GROUP * BLK, keys), lambda r, s: (r, 0, 0)),
                pl.BlockSpec((1, keys, WIDE), lambda r, s: (r, 0, 0)),
            ],
            out_specs=[pl.BlockSpec((BLK, GROUP_WIDTH), lambda r, s: (r, 0))]
            + [pl.BlockSpec(per_peer, lambda r, s: (0, 0, 0))] * peers,
        ),
        out_shape=[jax.ShapeDtypeStruct((rows, GROUP_WIDTH), BF16)]
        + [jax.ShapeDtypeStruct(per_peer, BF16)] * peers,
        compiler_params=params(48),
        cost_estimate=pl.CostEstimate(
            flops=8 * pairs * HEAD_DIM, bytes_accessed=4 * pairs, transcendentals=0
        ),
        name="backward",
    )(slots, queries, attended_grad, probs, kv)


def column_kernel(peers, blocks, row_ref, place_ref, *refs):
    parts, (own, next_up, next_down, far2, far3, total) = refs[:peers], refs[peers:]
    total[...] = jnp.zeros_like(total)
    for p in range(peers):
        for i in range(MAJOR * CAP):
            place = place_ref[p * MAJOR * CAP + i]

            @pl.when(place >= 0)
            def _():
                total[i // CAP, place] += parts[p][i].astype(F32)

    row = row_ref[0]
    own[...] = total[row].astype(BF16)
    next_up[...] = total[jnp.minimum(row + 1, MAJOR - 1)]
    next_down[...] = total[jnp.maximum(row - 1, 0)]
    far2[...] = total[(row + 2) % MAJOR]
    far3[...] = total[MAJOR - 1 - row].astype(BF16)


def column_sum(row, place, parts, blocks):
    peers = len(parts)
    smem = pl.BlockSpec(memory_space=pltpu.SMEM)
    shape = (blocks, BLK, WIDE)
    return pl.pallas_call(
        functools.partial(column_kernel, peers, blocks),
        in_specs=[smem, smem] + [WHOLE] * peers,
        out_specs=[WHOLE] * 5,
        out_shape=[jax.ShapeDtypeStruct(shape, kind) for kind in (BF16, F32, F32, F32, BF16)],
        scratch_shapes=[pltpu.VMEM((MAJOR,) + shape, F32)],
        compiler_params=params(24),
        name="column_sum",
    )(row, place, *parts)


def shards(patches, out_grad, w_query, w_key, w_value, w_out, key_tiles, key_blocks):
    tokens = patches[0]
    rows = tokens.shape[0]
    tile_count = lax.axis_size("tile")
    plane = tile_count // MAJOR
    my_tile = lax.axis_index("tile")
    my_row, my_place = my_tile // plane, my_tile % plane
    block_count = rows // BLK
    list_len = key_tiles.shape[2]
    entry_count = block_count * list_len

    def hop(value, moves, swap):
        pairs = [
            (
                v * tile_count + a * plane + c,
                (v ^ int(swap)) * tile_count + b * plane + c,
            )
            for v in range(2)
            for a, b in moves
            for c in range(plane)
        ]
        return lax.ppermute(value, AXES, pairs)

    def to_peer(value, p):
        pairs = [(t, t // plane * plane + (t % plane ^ p)) for t in range(tile_count)]
        return lax.ppermute(value, "tile", pairs)

    def plane_rows(table):
        table = table[0].reshape(MAJOR, plane, entry_count)
        return lax.dynamic_index_in_dim(table, my_row, 0, keepdims=False)

    stay = [(z, z) for z in range(MAJOR)]
    up = [(z, z + 1) for z in range(MAJOR - 1)]
    down = [(z + 1, z) for z in range(MAJOR - 1)]

    tiles, picks = plane_rows(key_tiles), plane_rows(key_blocks)
    earlier = jnp.arange(entry_count)[:, None] > jnp.arange(entry_count)[None, :]
    same = (tiles[:, :, None] == tiles[:, None, :]) & earlier[None]
    ranks = jnp.sum(same.astype(jnp.int32), axis=2)
    slots = tiles // plane * CAP + ranks
    columns = tiles % plane
    ids = jnp.arange(MAJOR * CAP, dtype=jnp.int32)
    hits = (slots[:, None, :] == ids[None, :, None]) & (columns == my_place)[:, None, :]
    place = jnp.sum(jnp.where(hits, picks[:, None, :] + 1, 0), axis=2) - 1
    place = place[jnp.arange(plane) ^ my_place].reshape(-1)
    my_slots = lax.dynamic_index_in_dim(
        (columns ^ my_place) * (MAJOR * CAP) + slots, my_place, 0, keepdims=False
    )
    row_index = my_row.reshape(1)

    def chunk_weight(g):
        cols = slice(g * HEAD_DIM, (g + 1) * HEAD_DIM)
        return jnp.concatenate([w_key[:, cols], w_value[:, cols]], axis=1)

    weights = [chunk_weight(g) for g in range(KV_HEADS)]
    arrived = []
    for g in range(KV_HEADS):
        mine = jnp.dot(tokens, weights[g], preferred_element_type=F32).astype(BF16)
        mine = mine.reshape(block_count, BLK, WIDE)
        up1 = hop(mine, up, True)
        down1 = hop(mine, down, True)
        own = hop(mine, stay, True)
        far2 = jnp.where(my_row >= 2, hop(up1, up[1:], False), hop(down1, down[:-1], False))
        far3 = hop(far2, [up[-1], down[0]], False)
        send = pack(row_index, place, (own, up1, down1, far2, far3), plane)
        arrived.append([send[0]] + [to_peer(send[p], p) for p in range(1, plane)])
    queries = jnp.dot(tokens, w_query, preferred_element_type=F32).astype(BF16)
    normed_grad = dot_nt(out_grad[0], w_out)
    kept = [forward(g, my_slots, queries, arrived[g], list_len) for g in range(KV_HEADS)]
    normed_low, attended_grad = normalise(normed_grad, [k[0] for k in kept])
    query_grads, terms = [], []
    for g in range(KV_HEADS):
        query_grad, *back = backward(
            g, my_slots, queries, attended_grad, kept[g][1], kept[g][2], plane
        )
        query_grads.append(query_grad)
        parts = [back[0]] + [to_peer(back[p], p) for p in range(1, plane)]
        own, next_up, next_down, far2, far3 = column_sum(row_index, place, parts, block_count)
        own = hop(own, stay, True)
        far2 = (far2 + hop(far3, [up[0], down[-1]], False).astype(F32)).astype(BF16)
        next_up = (next_up + hop(far2, up[:-1], False).astype(F32)).astype(BF16)
        next_down = (next_down + hop(far2, down[1:], False).astype(F32)).astype(BF16)
        kv_grad = own.astype(F32) + hop(next_up, up, True) + hop(next_down, down, True)
        terms.append(dot_nt(kv_grad.astype(BF16).reshape(rows, WIDE), weights[g]))
    layer_out = jnp.dot(normed_low, w_out, preferred_element_type=F32).astype(BF16)
    total = dot_nt(jnp.concatenate(query_grads, axis=1), w_query)
    for term in terms:
        total += term
    return (layer_out[None], total.astype(BF16)[None])


def solution(mesh):
    in_specs = (
        P("vintage", "tile", None),
        P("vintage", "tile", None),
        P(),
        P(),
        P(),
        P(),
        P("vintage", None, None),
        P("vintage", None, None),
    )
    out_specs = (P("vintage", "tile", None), P("vintage", "tile", None))
    return jax.shard_map(shards, mesh=mesh, in_specs=in_specs, out_specs=out_specs, check_vma=False)
```

```python
import functools

import jax
import jax.numpy as jnp
from jax import lax
from jax.experimental import pallas as pl
from jax.experimental.pallas import tpu as pltpu
from jax.sharding import PartitionSpec as P

HEADS = 12
KV_HEADS = 4
HEAD_DIM = 64
BLK = 128
CAP = 2
GROUP = HEADS // KV_HEADS
KV = KV_HEADS * HEAD_DIM
TEMPER = HEAD_DIM ** (-0.5)
EPSILON = 1e-06
F32 = jnp.float32
BF16 = jnp.bfloat16


def dot_nt(a, b):
    return lax.dot_general(a, b, (((1,), (1,)), ((), ())), preferred_element_type=F32)


def dot_tn(a, b):
    return lax.dot_general(a, b, (((0,), (0,)), ((), ())), preferred_element_type=F32)


def stack_heads(rows, g):
    first = g * GROUP * HEAD_DIM
    return jnp.concatenate(
        [rows[:, first + r * HEAD_DIM : first + (r + 1) * HEAD_DIM] for r in range(GROUP)], axis=0
    )


def spread_heads(stacked):
    return jnp.concatenate([stacked[r * BLK : (r + 1) * BLK] for r in range(GROUP)], axis=1)


def attention_kernel(list_len, slot_ref, q_ref, ng_ref, *refs):
    arrived, (normed_ref, qg_ref) = refs[:2], refs[2:4]
    back, (probs_scr, kv_scr, parts_scr, in_sems, out_sems) = refs[4:6], refs[6:]
    step = pl.program_id(0)
    entries = kv_scr.shape[0]
    per_part = arrived[0].shape[0]

    def fetch(e, part, slot):
        return pltpu.make_async_copy(arrived[part].at[slot], kv_scr.at[e], in_sems.at[e])

    def give(e, part, slot):
        return pltpu.make_async_copy(parts_scr.at[e], back[part].at[slot], out_sems.at[e])

    def start(copy, e):
        slot = slot_ref[e]
        for part in range(2):

            @pl.when(slot // per_part == part)
            def _():
                copy(e, part, slot % per_part).start()

    @pl.when(step == 0)
    def _():
        for e in range(entries):
            start(fetch, e)

    first = step * list_len
    for l in range(list_len):
        fetch(first + l, 0, 0).wait()
    keys = jnp.concatenate([kv_scr[first + l, :, :KV] for l in range(list_len)], axis=0)
    values = jnp.concatenate([kv_scr[first + l, :, KV:] for l in range(list_len)], axis=0)
    queries = q_ref[...] * jnp.asarray(TEMPER, BF16)
    attended = []
    for g in range(KV_HEADS):
        cols = slice(g * HEAD_DIM, (g + 1) * HEAD_DIM)
        scores = dot_nt(stack_heads(queries, g), keys[:, cols])
        expo = jnp.exp(scores - jnp.max(scores, axis=-1, keepdims=True))
        probs = expo * (1.0 / jnp.sum(expo, axis=-1, keepdims=True))
        probs_scr[g] = probs
        out = jnp.dot(probs.astype(BF16), values[:, cols], preferred_element_type=F32)
        attended.append(spread_heads(out.astype(BF16)))
    attended = jnp.concatenate(attended, axis=1).astype(F32)
    width = attended.shape[1]
    inverse = lax.rsqrt(jnp.sum(attended * attended, axis=-1, keepdims=True) / width + EPSILON)
    normed = attended * inverse
    normed_ref[...] = normed.astype(BF16)
    normed_grad = ng_ref[...]
    shared = jnp.sum(normed_grad * normed, axis=-1, keepdims=True) / width
    attended_grad = ((normed_grad - normed * shared) * inverse).astype(BF16)
    for g in range(KV_HEADS):
        cols = slice(g * HEAD_DIM, (g + 1) * HEAD_DIM)
        out_grad = stack_heads(attended_grad, g)
        prob_grad = dot_nt(out_grad, values[:, cols])
        probs = probs_scr[g]
        row_dot = jnp.sum(probs * prob_grad, axis=-1, keepdims=True)
        score_grad = (probs * (prob_grad - row_dot)).astype(BF16)
        query_grad = jnp.dot(score_grad, keys[:, cols], preferred_element_type=F32) * TEMPER
        left = g * GROUP * HEAD_DIM
        qg_ref[:, left : left + GROUP * HEAD_DIM] = spread_heads(query_grad.astype(BF16))
        key_part = dot_tn(score_grad, stack_heads(queries, g)).astype(BF16)
        value_part = dot_tn(probs.astype(BF16), out_grad).astype(BF16)
        for l in range(list_len):
            rows = slice(l * BLK, (l + 1) * BLK)
            parts_scr[first + l, :, g * HEAD_DIM : (g + 1) * HEAD_DIM] = key_part[rows]
            parts_scr[first + l, :, KV + g * HEAD_DIM : KV + (g + 1) * HEAD_DIM] = value_part[rows]
    for l in range(list_len):
        start(give, first + l)

    @pl.when(step == pl.num_programs(0) - 1)
    def _():
        for e in range(entries):
            give(e, 0, 0).wait()


def attention(slots, queries, normed_grad, arrived, list_len):
    rows, width = queries.shape
    blocks = rows // BLK
    entries = blocks * list_len
    row_spec = pl.BlockSpec((BLK, width), lambda r, s: (r, 0))
    anywhere = pl.BlockSpec(memory_space=pl.ANY)
    keys = list_len * BLK
    pairs = HEADS * rows * keys
    return pl.pallas_call(
        functools.partial(attention_kernel, list_len),
        grid_spec=pltpu.PrefetchScalarGridSpec(
            num_scalar_prefetch=1,
            grid=(blocks,),
            in_specs=[row_spec, row_spec, anywhere, anywhere],
            out_specs=[row_spec, row_spec, anywhere, anywhere],
            scratch_shapes=[
                pltpu.VMEM((KV_HEADS, GROUP * BLK, keys), F32),
                pltpu.VMEM((entries, BLK, 2 * KV), BF16),
                pltpu.VMEM((entries, BLK, 2 * KV), BF16),
                pltpu.SemaphoreType.DMA((entries,)),
                pltpu.SemaphoreType.DMA((entries,)),
            ],
        ),
        out_shape=[jax.ShapeDtypeStruct((rows, width), BF16)] * 2
        + [jax.ShapeDtypeStruct(arrived[0].shape, BF16)] * 2,
        compiler_params=pltpu.CompilerParams(vmem_limit_bytes=56 * 1024 * 1024),
        cost_estimate=pl.CostEstimate(
            flops=12 * pairs * HEAD_DIM, bytes_accessed=16 * rows * width, transcendentals=pairs
        ),
        name="attention",
    )(slots, queries, normed_grad, *arrived)


def owner_kernel(chunk, wanted_ref, parts_ref, out_ref, total):
    step = pl.program_id(0)

    @pl.when(step == 0)
    def _():
        total[...] = jnp.zeros_like(total)

    for s in range(chunk):
        block = wanted_ref[step * chunk + s]

        @pl.when(block >= 0)
        def _():
            total[block] += parts_ref[s].astype(F32)

    @pl.when(step == pl.num_programs(0) - 1)
    def _():
        out_ref[...] = total[...].astype(BF16)


def owner_sum(wanted, returned, blocks):
    slots = returned.shape[0]
    chunk = 4
    return pl.pallas_call(
        functools.partial(owner_kernel, chunk),
        grid_spec=pltpu.PrefetchScalarGridSpec(
            num_scalar_prefetch=1,
            grid=(slots // chunk,),
            in_specs=[pl.BlockSpec((chunk, BLK, 2 * KV), lambda s, w: (s, 0, 0))],
            out_specs=pl.BlockSpec((blocks, BLK, 2 * KV), lambda s, w: (0, 0, 0)),
            scratch_shapes=[pltpu.VMEM((blocks, BLK, 2 * KV), F32)],
        ),
        out_shape=jax.ShapeDtypeStruct((blocks, BLK, 2 * KV), BF16),
        compiler_params=pltpu.CompilerParams(vmem_limit_bytes=24 * 1024 * 1024),
        name="owner_sum",
    )(wanted, returned)


def shards(patches, out_grad, w_query, w_key, w_value, w_out, key_tiles, key_blocks):
    tokens = patches[0]
    rows = tokens.shape[0]
    tile_count = lax.axis_size("tile")
    half = tile_count // 2
    my_tile = lax.axis_index("tile")
    my_half, my_place = my_tile // half, my_tile % half
    groups = [list(range(half)), list(range(half, tile_count))]
    block_count = rows // BLK
    list_len = key_tiles.shape[2]
    entry_count = block_count * list_len

    def cross(value, shift):
        pairs = [
            (v * tile_count + t, (1 - v) * tile_count + (t + shift) % tile_count)
            for v in range(2)
            for t in range(tile_count)
        ]
        return lax.ppermute(value, ("vintage", "tile"), pairs)

    def exchange(value):
        return lax.all_to_all(
            value, "tile", split_axis=0, concat_axis=0, tiled=True, axis_index_groups=groups
        )

    def half_rows(table):
        table = table[0].reshape(2, half, entry_count)
        return lax.dynamic_index_in_dim(table, my_half, 0, keepdims=False)

    tiles, picks = half_rows(key_tiles), half_rows(key_blocks)
    earlier = jnp.arange(entry_count)[:, None] > jnp.arange(entry_count)[None, :]
    same = (tiles[:, :, None] == tiles[:, None, :]) & earlier[None]
    ranks = jnp.sum(same.astype(jnp.int32), axis=2)
    is_far = (tiles // half != my_half).astype(jnp.int32)
    slots = (is_far * half + tiles % half) * CAP + ranks
    my_slots = lax.dynamic_index_in_dim(slots, my_place, 0, keepdims=False)
    part_ids = jnp.arange(2, dtype=jnp.int32)[:, None, None] * half + my_place
    ids = part_ids * CAP + jnp.arange(CAP, dtype=jnp.int32)[None, None, :]
    hits = slots[None, :, :, None] == ids[:, :, None, :]
    wanted = jnp.sum(jnp.where(hits, picks[None, :, :, None] + 1, 0), axis=2) - 1
    wanted = wanted.reshape(2, half * CAP)

    keys = jnp.dot(tokens, w_key, preferred_element_type=F32).astype(BF16)
    values = jnp.dot(tokens, w_value, preferred_element_type=F32).astype(BF16)
    mine = jnp.concatenate([keys, values], axis=-1).reshape(block_count, BLK, 2 * KV)
    tiles_here = [cross(mine, 0), cross(mine, half)]
    arrived = [exchange(tiles_here[p][jnp.maximum(wanted[p], 0)]) for p in range(2)]
    queries = jnp.dot(tokens, w_query, preferred_element_type=F32).astype(BF16)
    normed_grad = dot_nt(out_grad[0], w_out)
    normed_low, query_grad, *back = attention(my_slots, queries, normed_grad, arrived, list_len)
    far = cross(owner_sum(wanted[1], exchange(back[1]), block_count), half)
    near = cross(owner_sum(wanted[0], exchange(back[0]), block_count), 0)
    layer_out = jnp.dot(normed_low, w_out, preferred_element_type=F32).astype(BF16)
    query_term = dot_nt(query_grad, w_query)
    kv_grad = (near.astype(F32) + far.astype(F32)).astype(BF16).reshape(rows, 2 * KV)
    kv_term = dot_nt(kv_grad[:, :KV], w_key) + dot_nt(kv_grad[:, KV:], w_value)
    input_grad = (query_term + kv_term).astype(BF16)
    return (layer_out[None], input_grad[None])


def solution(mesh):
    in_specs = (
        P("vintage", "tile", None),
        P("vintage", "tile", None),
        P(),
        P(),
        P(),
        P(),
        P("vintage", None, None),
        P("vintage", None, None),
    )
    out_specs = (P("vintage", "tile", None), P("vintage", "tile", None))
    return jax.shard_map(shards, mesh=mesh, in_specs=in_specs, out_specs=out_specs, check_vma=False)
```

```python
import functools

import jax
import jax.numpy as jnp
from jax import lax
from jax.experimental import pallas as pl
from jax.experimental.pallas import tpu as pltpu
from jax.sharding import PartitionSpec as P

HEADS = 12
KV_HEADS = 4
HEAD_DIM = 64
BLK = 128
CAP = 2
GROUP = HEADS // KV_HEADS
KV = KV_HEADS * HEAD_DIM
PAIR = 2 * HEAD_DIM
TEMPER = HEAD_DIM ** (-0.5)
EPSILON = 1e-06
F32 = jnp.float32
BF16 = jnp.bfloat16


def dot_nt(a, b):
    return lax.dot_general(a, b, (((1,), (1,)), ((), ())), preferred_element_type=F32)


def dot_tn(a, b):
    return lax.dot_general(a, b, (((0,), (0,)), ((), ())), preferred_element_type=F32)


def feature_heads(features, g):
    first = g * GROUP
    return jnp.concatenate(
        [features[(first + r) * HEAD_DIM : (first + r + 1) * HEAD_DIM] for r in range(GROUP)],
        axis=1,
    )


def pad_half(features, odd):
    zeros = jnp.zeros_like(features)
    return jnp.concatenate([zeros, features] if odd else [features, zeros], axis=0)


def take_half(features, odd):
    return features[odd * HEAD_DIM : (odd + 1) * HEAD_DIM]


def attention_kernel(list_len, slot_ref, q_ref, ng_ref, *refs):
    arrived, (normed_ref, qg_ref) = refs[:2], refs[2:4]
    back, (probs_scr, kv_scr, parts_scr, in_sems, out_sems) = refs[4:6], refs[6:]
    step = pl.program_id(0)
    entries = in_sems.shape[0]
    per_part = arrived[0].shape[0]

    def rows_of(e):
        return pl.ds(pl.multiple_of(e * BLK, BLK), BLK)

    def fetch(e, part, slot):
        return pltpu.make_async_copy(arrived[part].at[slot], kv_scr.at[rows_of(e)], in_sems.at[e])

    def give(e, part, slot):
        return pltpu.make_async_copy(parts_scr.at[rows_of(e)], back[part].at[slot], out_sems.at[e])

    def start(copy, e):
        slot = slot_ref[e]
        for part in range(2):

            @pl.when(slot // per_part == part)
            def _():
                copy(e, part, slot % per_part).start()

    @pl.when(step == 0)
    def _():
        for e in range(entries):
            start(fetch, e)

    first = step * list_len
    for l in range(list_len):
        fetch(first + l, 0, 0).wait()
    here = pl.ds(pl.multiple_of(step * list_len * BLK, list_len * BLK), list_len * BLK)
    keys = [kv_scr[here, j * PAIR : (j + 1) * PAIR] for j in range(KV // PAIR)]
    values = [kv_scr[here, KV + j * PAIR : KV + (j + 1) * PAIR] for j in range(KV // PAIR)]
    queries = q_ref[...] * jnp.asarray(TEMPER, BF16)
    padded = [pad_half(feature_heads(queries, g), g % 2) for g in range(KV_HEADS)]
    attended = []
    for g in range(KV_HEADS):
        scores = jnp.dot(keys[g // 2], padded[g], preferred_element_type=F32)
        expo = jnp.exp(scores - jnp.max(scores, axis=0, keepdims=True))
        probs = expo * (1.0 / jnp.sum(expo, axis=0, keepdims=True))
        probs_scr[g] = probs
        out = take_half(dot_tn(values[g // 2], probs.astype(BF16)), g % 2)
        attended += [out[:, r * BLK : (r + 1) * BLK] for r in range(GROUP)]
    attended = jnp.concatenate(attended, axis=0).astype(BF16).astype(F32)
    width = attended.shape[0]
    inverse = lax.rsqrt(jnp.sum(attended * attended, axis=0, keepdims=True) / width + EPSILON)
    normed = attended * inverse
    normed_ref[...] = normed.astype(BF16)
    normed_grad = ng_ref[...]
    shared = jnp.sum(normed_grad * normed, axis=0, keepdims=True) / width
    attended_grad = ((normed_grad - normed * shared) * inverse).astype(BF16)
    for j in range(KV // PAIR):
        key_part = value_part = 0.0
        for odd in range(2):
            g = 2 * j + odd
            out_grad = pad_half(feature_heads(attended_grad, g), odd)
            prob_grad = jnp.dot(values[j], out_grad, preferred_element_type=F32)
            probs = probs_scr[g]
            row_dot = jnp.sum(probs * prob_grad, axis=0, keepdims=True)
            score_grad = (probs * (prob_grad - row_dot)).astype(BF16)
            query_grad = (take_half(dot_tn(keys[j], score_grad), odd) * TEMPER).astype(BF16)
            for r in range(GROUP):
                top = (g * GROUP + r) * HEAD_DIM
                qg_ref[top : top + HEAD_DIM, :] = query_grad[:, r * BLK : (r + 1) * BLK]
            key_part += dot_nt(score_grad, padded[g])
            value_part += dot_nt(probs.astype(BF16), out_grad)
        parts_scr[here, j * PAIR : (j + 1) * PAIR] = key_part.astype(BF16)
        parts_scr[here, KV + j * PAIR : KV + (j + 1) * PAIR] = value_part.astype(BF16)
    for l in range(list_len):
        start(give, first + l)

    @pl.when(step == pl.num_programs(0) - 1)
    def _():
        for e in range(entries):
            give(e, 0, 0).wait()


def attention(slots, queries, normed_grad, arrived, list_len):
    width, rows = queries.shape
    blocks = rows // BLK
    entries = blocks * list_len
    row_spec = pl.BlockSpec((width, BLK), lambda r, s: (0, r))
    anywhere = pl.BlockSpec(memory_space=pl.ANY)
    keys = list_len * BLK
    pairs = HEADS * rows * keys
    return pl.pallas_call(
        functools.partial(attention_kernel, list_len),
        grid_spec=pltpu.PrefetchScalarGridSpec(
            num_scalar_prefetch=1,
            grid=(blocks,),
            in_specs=[row_spec, row_spec, anywhere, anywhere],
            out_specs=[row_spec, row_spec, anywhere, anywhere],
            scratch_shapes=[
                pltpu.VMEM((KV_HEADS, keys, GROUP * BLK), F32),
                pltpu.VMEM((entries * BLK, 2 * KV), BF16),
                pltpu.VMEM((entries * BLK, 2 * KV), BF16),
                pltpu.SemaphoreType.DMA((entries,)),
                pltpu.SemaphoreType.DMA((entries,)),
            ],
        ),
        out_shape=[jax.ShapeDtypeStruct((width, rows), BF16)] * 2
        + [jax.ShapeDtypeStruct(arrived[0].shape, BF16)] * 2,
        compiler_params=pltpu.CompilerParams(vmem_limit_bytes=56 * 1024 * 1024),
        cost_estimate=pl.CostEstimate(
            flops=12 * pairs * HEAD_DIM, bytes_accessed=16 * rows * width, transcendentals=pairs
        ),
        name="attention",
    )(slots, queries, normed_grad, *arrived)


def owner_kernel(chunk, wanted_ref, parts_ref, out_ref, total):
    step = pl.program_id(0)

    @pl.when(step == 0)
    def _():
        total[...] = jnp.zeros_like(total)

    for s in range(chunk):
        block = wanted_ref[step * chunk + s]

        @pl.when(block >= 0)
        def _():
            total[block] += parts_ref[s].astype(F32)

    @pl.when(step == pl.num_programs(0) - 1)
    def _():
        out_ref[...] = total[...].astype(BF16)


def owner_sum(wanted, returned, blocks):
    slots = returned.shape[0]
    chunk = 4
    return pl.pallas_call(
        functools.partial(owner_kernel, chunk),
        grid_spec=pltpu.PrefetchScalarGridSpec(
            num_scalar_prefetch=1,
            grid=(slots // chunk,),
            in_specs=[pl.BlockSpec((chunk, BLK, 2 * KV), lambda s, w: (s, 0, 0))],
            out_specs=pl.BlockSpec((blocks, BLK, 2 * KV), lambda s, w: (0, 0, 0)),
            scratch_shapes=[pltpu.VMEM((blocks, BLK, 2 * KV), F32)],
        ),
        out_shape=jax.ShapeDtypeStruct((blocks, BLK, 2 * KV), BF16),
        compiler_params=pltpu.CompilerParams(vmem_limit_bytes=24 * 1024 * 1024),
        name="owner_sum",
    )(wanted, returned)


def shards(patches, out_grad, w_query, w_key, w_value, w_out, key_tiles, key_blocks):
    tokens = patches[0]
    rows = tokens.shape[0]
    tile_count = lax.axis_size("tile")
    half = tile_count // 2
    my_tile = lax.axis_index("tile")
    my_half, my_place = my_tile // half, my_tile % half
    groups = [list(range(half)), list(range(half, tile_count))]
    block_count = rows // BLK
    list_len = key_tiles.shape[2]
    entry_count = block_count * list_len

    def cross(value, shift):
        pairs = [
            (v * tile_count + t, (1 - v) * tile_count + (t + shift) % tile_count)
            for v in range(2)
            for t in range(tile_count)
        ]
        return lax.ppermute(value, ("vintage", "tile"), pairs)

    def exchange(value):
        return lax.all_to_all(
            value, "tile", split_axis=0, concat_axis=0, tiled=True, axis_index_groups=groups
        )

    def half_rows(table):
        table = table[0].reshape(2, half, entry_count)
        return lax.dynamic_index_in_dim(table, my_half, 0, keepdims=False)

    tiles, picks = half_rows(key_tiles), half_rows(key_blocks)
    earlier = jnp.arange(entry_count)[:, None] > jnp.arange(entry_count)[None, :]
    same = (tiles[:, :, None] == tiles[:, None, :]) & earlier[None]
    ranks = jnp.sum(same.astype(jnp.int32), axis=2)
    is_far = (tiles // half != my_half).astype(jnp.int32)
    slots = (is_far * half + tiles % half) * CAP + ranks
    my_slots = lax.dynamic_index_in_dim(slots, my_place, 0, keepdims=False)
    part_ids = jnp.arange(2, dtype=jnp.int32)[:, None, None] * half + my_place
    ids = part_ids * CAP + jnp.arange(CAP, dtype=jnp.int32)[None, None, :]
    hits = slots[None, :, :, None] == ids[:, :, None, :]
    wanted = jnp.sum(jnp.where(hits, picks[None, :, :, None] + 1, 0), axis=2) - 1
    wanted = wanted.reshape(2, half * CAP)

    keys = jnp.dot(tokens, w_key, preferred_element_type=F32).astype(BF16)
    values = jnp.dot(tokens, w_value, preferred_element_type=F32).astype(BF16)
    mine = jnp.concatenate([keys, values], axis=-1).reshape(block_count, BLK, 2 * KV)
    tiles_here = [cross(mine, 0), cross(mine, half)]
    arrived = [exchange(tiles_here[p][jnp.maximum(wanted[p], 0)]) for p in range(2)]
    queries = lax.dot_general(
        w_query, tokens, (((0,), (1,)), ((), ())), preferred_element_type=F32
    ).astype(BF16)
    normed_grad = dot_nt(w_out, out_grad[0])
    normed_low, query_grad, *back = attention(my_slots, queries, normed_grad, arrived, list_len)
    far = cross(owner_sum(wanted[1], exchange(back[1]), block_count), half)
    near = cross(owner_sum(wanted[0], exchange(back[0]), block_count), 0)
    layer_out = dot_tn(normed_low, w_out).astype(BF16)
    query_term = lax.dot_general(
        query_grad, w_query, (((0,), (1,)), ((), ())), preferred_element_type=F32
    )
    kv_grad = (near.astype(F32) + far.astype(F32)).astype(BF16).reshape(rows, 2 * KV)
    kv_term = dot_nt(kv_grad[:, :KV], w_key) + dot_nt(kv_grad[:, KV:], w_value)
    input_grad = (query_term + kv_term).astype(BF16)
    return (layer_out[None], input_grad[None])


def solution(mesh):
    in_specs = (
        P("vintage", "tile", None),
        P("vintage", "tile", None),
        P(),
        P(),
        P(),
        P(),
        P("vintage", None, None),
        P("vintage", None, None),
    )
    out_specs = (P("vintage", "tile", None), P("vintage", "tile", None))
    return jax.shard_map(shards, mesh=mesh, in_specs=in_specs, out_specs=out_specs, check_vma=False)
```

```python
import functools

import jax
import jax.numpy as jnp
from jax import lax
from jax.experimental import pallas as pl
from jax.experimental.pallas import tpu as pltpu
from jax.sharding import PartitionSpec as P

HEADS = 12
KV_HEADS = 4
HEAD_DIM = 64
BLK = 128
CAP = 2
GROUP = HEADS // KV_HEADS
KV = KV_HEADS * HEAD_DIM
PAIR = 2 * HEAD_DIM
TEMPER = HEAD_DIM ** (-0.5)
EPSILON = 1e-06
F32 = jnp.float32
BF16 = jnp.bfloat16


def dot_nt(a, b):
    return lax.dot_general(a, b, (((1,), (1,)), ((), ())), preferred_element_type=F32)


def dot_tn(a, b):
    return lax.dot_general(a, b, (((0,), (0,)), ((), ())), preferred_element_type=F32)


def feature_heads(features, g):
    first = g * GROUP
    return jnp.concatenate(
        [features[(first + r) * HEAD_DIM : (first + r + 1) * HEAD_DIM] for r in range(GROUP)],
        axis=1,
    )


def two_groups(features, j):
    low, high = feature_heads(features, 2 * j), feature_heads(features, 2 * j + 1)
    zeros = jnp.zeros_like(low)
    return jnp.concatenate(
        [jnp.concatenate([low, zeros], axis=1), jnp.concatenate([zeros, high], axis=1)], axis=0
    )


def head_rows(pair_out):
    heads = []
    for i in range(2 * GROUP):
        top = i // GROUP * HEAD_DIM
        heads.append(pair_out[top : top + HEAD_DIM, i * BLK : (i + 1) * BLK])
    return jnp.concatenate(heads, axis=0)


def attention_kernel(list_len, slot_ref, q_ref, ng_ref, *refs):
    arrived, (normed_ref, qg_ref) = refs[:2], refs[2:4]
    back, (expo_scr, kv_scr, parts_scr, in_sems, out_sems) = refs[4:6], refs[6:]
    step = pl.program_id(0)
    entries = in_sems.shape[0]
    per_part = arrived[0].shape[0]

    def rows_of(e):
        return pl.ds(pl.multiple_of(e * BLK, BLK), BLK)

    def fetch(e, part, slot):
        return pltpu.make_async_copy(arrived[part].at[slot], kv_scr.at[rows_of(e)], in_sems.at[e])

    def give(e, part, slot):
        return pltpu.make_async_copy(parts_scr.at[rows_of(e)], back[part].at[slot], out_sems.at[e])

    def start(copy, e):
        slot = slot_ref[e]
        for part in range(2):

            @pl.when(slot // per_part == part)
            def _():
                copy(e, part, slot % per_part).start()

    @pl.when(step == 0)
    def _():
        for e in range(entries):
            start(fetch, e)

    first = step * list_len
    for l in range(list_len):
        fetch(first + l, 0, 0).wait()
    here = pl.ds(pl.multiple_of(step * list_len * BLK, list_len * BLK), list_len * BLK)
    keys = [kv_scr[here, j * PAIR : (j + 1) * PAIR] for j in range(KV // PAIR)]
    values = [kv_scr[here, KV + j * PAIR : KV + (j + 1) * PAIR] for j in range(KV // PAIR)]
    queries = q_ref[...] * jnp.asarray(TEMPER, BF16)
    pairs = range(KV // PAIR)
    wide = [two_groups(queries, j) for j in pairs]
    scores = [jnp.dot(keys[j], wide[j], preferred_element_type=F32) for j in pairs]
    attended, scales = [], []
    for j in pairs:
        expo = jnp.exp(scores[j] - jnp.max(scores[j], axis=0, keepdims=True))
        scale = 1.0 / jnp.sum(expo, axis=0, keepdims=True)
        expo_scr[j] = expo.astype(BF16)
        attended.append(head_rows(dot_tn(values[j], expo_scr[j]) * scale))
        scales += [
            jnp.broadcast_to(scale[:, i * BLK : (i + 1) * BLK], (HEAD_DIM, BLK))
            for i in range(2 * GROUP)
        ]
    exact = jnp.concatenate(attended, axis=0)
    attended = exact.astype(BF16).astype(F32)
    width = attended.shape[0]
    inverse = lax.rsqrt(jnp.sum(attended * attended, axis=0, keepdims=True) / width + EPSILON)
    normed = attended * inverse
    normed_ref[...] = normed.astype(BF16)
    normed_grad = ng_ref[...]
    shared = jnp.sum(normed_grad * normed, axis=0, keepdims=True) / width
    attended_grad = (normed_grad - normed * shared) * inverse
    scaled_grad = (attended_grad * jnp.concatenate(scales, axis=0)).astype(BF16)
    overlap = scaled_grad.astype(F32) * exact
    grads = [two_groups(scaled_grad, j) for j in pairs]
    prob_grads = [jnp.dot(values[j], grads[j], preferred_element_type=F32) for j in pairs]
    for j in pairs:
        heads = range(2 * GROUP * j, 2 * GROUP * (j + 1))
        row_dot = jnp.concatenate(
            [
                jnp.sum(overlap[h * HEAD_DIM : (h + 1) * HEAD_DIM], axis=0, keepdims=True)
                for h in heads
            ],
            axis=1,
        )
        expo = expo_scr[j]
        value_part = dot_nt(expo, grads[j])
        score_grad = (expo.astype(F32) * (prob_grads[j] - row_dot)).astype(BF16)
        query_grad = head_rows(dot_tn(keys[j], score_grad) * TEMPER).astype(BF16)
        qg_ref[heads.start * HEAD_DIM : heads.stop * HEAD_DIM, :] = query_grad
        key_part = dot_nt(score_grad, wide[j])
        parts_scr[here, j * PAIR : (j + 1) * PAIR] = key_part.astype(BF16)
        parts_scr[here, KV + j * PAIR : KV + (j + 1) * PAIR] = value_part.astype(BF16)
    for l in range(list_len):
        start(give, first + l)

    @pl.when(step == pl.num_programs(0) - 1)
    def _():
        for e in range(entries):
            give(e, 0, 0).wait()


def attention(slots, queries, normed_grad, arrived, list_len):
    width, rows = queries.shape
    blocks = rows // BLK
    entries = blocks * list_len
    row_spec = pl.BlockSpec((width, BLK), lambda r, s: (0, r))
    anywhere = pl.BlockSpec(memory_space=pl.ANY)
    keys = list_len * BLK
    pairs = HEADS * rows * keys
    return pl.pallas_call(
        functools.partial(attention_kernel, list_len),
        grid_spec=pltpu.PrefetchScalarGridSpec(
            num_scalar_prefetch=1,
            grid=(blocks,),
            in_specs=[row_spec, row_spec, anywhere, anywhere],
            out_specs=[row_spec, row_spec, anywhere, anywhere],
            scratch_shapes=[
                pltpu.VMEM((KV // PAIR, keys, 2 * GROUP * BLK), BF16),
                pltpu.VMEM((entries * BLK, 2 * KV), BF16),
                pltpu.VMEM((entries * BLK, 2 * KV), BF16),
                pltpu.SemaphoreType.DMA((entries,)),
                pltpu.SemaphoreType.DMA((entries,)),
            ],
        ),
        out_shape=[jax.ShapeDtypeStruct((width, rows), BF16)] * 2
        + [jax.ShapeDtypeStruct(arrived[0].shape, BF16)] * 2,
        compiler_params=pltpu.CompilerParams(vmem_limit_bytes=56 * 1024 * 1024),
        cost_estimate=pl.CostEstimate(
            flops=12 * pairs * HEAD_DIM, bytes_accessed=16 * rows * width, transcendentals=pairs
        ),
        name="attention",
    )(slots, queries, normed_grad, *arrived)


def owner_kernel(chunk, wanted_ref, parts_ref, out_ref, total):
    step = pl.program_id(0)

    @pl.when(step == 0)
    def _():
        total[...] = jnp.zeros_like(total)

    for s in range(chunk):
        block = wanted_ref[step * chunk + s]

        @pl.when(block >= 0)
        def _():
            total[block] += parts_ref[s].astype(F32)

    @pl.when(step == pl.num_programs(0) - 1)
    def _():
        out_ref[...] = total[...].astype(BF16)


def owner_sum(wanted, returned, blocks):
    slots = returned.shape[0]
    chunk = 4
    return pl.pallas_call(
        functools.partial(owner_kernel, chunk),
        grid_spec=pltpu.PrefetchScalarGridSpec(
            num_scalar_prefetch=1,
            grid=(slots // chunk,),
            in_specs=[pl.BlockSpec((chunk, BLK, 2 * KV), lambda s, w: (s, 0, 0))],
            out_specs=pl.BlockSpec((blocks, BLK, 2 * KV), lambda s, w: (0, 0, 0)),
            scratch_shapes=[pltpu.VMEM((blocks, BLK, 2 * KV), F32)],
        ),
        out_shape=jax.ShapeDtypeStruct((blocks, BLK, 2 * KV), BF16),
        compiler_params=pltpu.CompilerParams(vmem_limit_bytes=24 * 1024 * 1024),
        name="owner_sum",
    )(wanted, returned)


def shards(patches, out_grad, w_query, w_key, w_value, w_out, key_tiles, key_blocks):
    tokens = patches[0]
    rows = tokens.shape[0]
    tile_count = lax.axis_size("tile")
    half = tile_count // 2
    my_tile = lax.axis_index("tile")
    my_half, my_place = my_tile // half, my_tile % half
    groups = [list(range(half)), list(range(half, tile_count))]
    swaps = [
        [v * tile_count + t, (1 - v) * tile_count + t + half] for v in range(2) for t in range(half)
    ]
    block_count = rows // BLK
    list_len = key_tiles.shape[2]
    entry_count = block_count * list_len

    def cross(value, shift):
        pairs = [
            (v * tile_count + t, (1 - v) * tile_count + (t + shift) % tile_count)
            for v in range(2)
            for t in range(tile_count)
        ]
        return lax.ppermute(value, ("vintage", "tile"), pairs)

    def exchange(value):
        return lax.all_to_all(
            value, "tile", split_axis=0, concat_axis=0, tiled=True, axis_index_groups=groups
        )

    def half_rows(table):
        table = table[0].reshape(2, half, entry_count)
        return lax.dynamic_index_in_dim(table, my_half, 0, keepdims=False)

    tiles, picks = half_rows(key_tiles), half_rows(key_blocks)
    earlier = jnp.arange(entry_count)[:, None] > jnp.arange(entry_count)[None, :]
    same = (tiles[:, :, None] == tiles[:, None, :]) & earlier[None]
    ranks = jnp.sum(same.astype(jnp.int32), axis=2)
    is_far = (tiles // half != my_half).astype(jnp.int32)
    slots = (is_far * half + tiles % half) * CAP + ranks
    my_slots = lax.dynamic_index_in_dim(slots, my_place, 0, keepdims=False)
    part_ids = jnp.arange(2, dtype=jnp.int32)[:, None, None] * half + my_place
    ids = part_ids * CAP + jnp.arange(CAP, dtype=jnp.int32)[None, None, :]
    hits = slots[None, :, :, None] == ids[:, :, None, :]
    wanted = jnp.sum(jnp.where(hits, picks[None, :, :, None] + 1, 0), axis=2) - 1
    wanted = wanted.reshape(2, half * CAP)

    keys = jnp.dot(tokens, w_key, preferred_element_type=F32).astype(BF16)
    values = jnp.dot(tokens, w_value, preferred_element_type=F32).astype(BF16)
    mine = jnp.concatenate([keys, values], axis=-1).reshape(block_count, BLK, 2 * KV)
    both = lax.all_gather(mine, ("vintage", "tile"), axis_index_groups=swaps)
    both = both.reshape(2 * block_count, BLK, 2 * KV)
    picked = jnp.maximum(wanted, 0)
    near_send = cross(mine, 0)[picked[0]]
    far_send = both[picked[1] + (my_half ^ 1) * block_count]
    arrived = [exchange(near_send), exchange(far_send)]
    queries = lax.dot_general(
        w_query, tokens, (((0,), (1,)), ((), ())), preferred_element_type=F32
    ).astype(BF16)
    normed_grad = dot_nt(w_out, out_grad[0])
    normed_low, query_grad, *back = attention(my_slots, queries, normed_grad, arrived, list_len)
    far = cross(owner_sum(wanted[1], exchange(back[1]), block_count), half)
    near = cross(owner_sum(wanted[0], exchange(back[0]), block_count), 0)
    layer_out = dot_tn(normed_low, w_out).astype(BF16)
    query_term = lax.dot_general(
        query_grad, w_query, (((0,), (1,)), ((), ())), preferred_element_type=F32
    )
    kv_grad = (near.astype(F32) + far.astype(F32)).astype(BF16).reshape(rows, 2 * KV)
    kv_term = dot_nt(kv_grad[:, :KV], w_key) + dot_nt(kv_grad[:, KV:], w_value)
    input_grad = (query_term + kv_term).astype(BF16)
    return (layer_out[None], input_grad[None])


def solution(mesh):
    in_specs = (
        P("vintage", "tile", None),
        P("vintage", "tile", None),
        P(),
        P(),
        P(),
        P(),
        P("vintage", None, None),
        P("vintage", None, None),
    )
    out_specs = (P("vintage", "tile", None), P("vintage", "tile", None))
    return jax.shard_map(shards, mesh=mesh, in_specs=in_specs, out_specs=out_specs, check_vma=False)
```

```python
import functools

import jax
import jax.numpy as jnp
from jax import lax
from jax.experimental import pallas as pl
from jax.experimental.pallas import tpu as pltpu
from jax.sharding import PartitionSpec as P

HEADS = 12
KV_HEADS = 4
HEAD_DIM = 64
BLK = 128
CAP = 2
GROUP = HEADS // KV_HEADS
KV = KV_HEADS * HEAD_DIM
PAIR = 2 * HEAD_DIM
SWAP_FLOPS = 40_000_000_000
TEMPER = HEAD_DIM ** (-0.5)
EPSILON = 1e-06
F32 = jnp.float32
BF16 = jnp.bfloat16


def params(mebibytes):
    return pltpu.CompilerParams(vmem_limit_bytes=mebibytes * 1024 * 1024)


def dot_nt(a, b):
    return lax.dot_general(a, b, (((1,), (1,)), ((), ())), preferred_element_type=F32)


def dot_tn(a, b):
    return lax.dot_general(a, b, (((0,), (0,)), ((), ())), preferred_element_type=F32)


def feature_heads(features, g):
    first = g * GROUP
    return jnp.concatenate(
        [features[(first + r) * HEAD_DIM : (first + r + 1) * HEAD_DIM] for r in range(GROUP)],
        axis=1,
    )


def two_groups(features, j):
    low, high = feature_heads(features, 2 * j), feature_heads(features, 2 * j + 1)
    zeros = jnp.zeros_like(low)
    return jnp.concatenate(
        [jnp.concatenate([low, zeros], axis=1), jnp.concatenate([zeros, high], axis=1)], axis=0
    )


def head_rows(pair_out):
    heads = []
    for i in range(2 * GROUP):
        top = i // GROUP * HEAD_DIM
        heads.append(pair_out[top : top + HEAD_DIM, i * BLK : (i + 1) * BLK])
    return jnp.concatenate(heads, axis=0)


def attention_kernel(list_len, slot_ref, q_ref, ng_ref, *refs):
    arrived, (normed_ref, qg_ref) = refs[:2], refs[2:4]
    back, (expo_scr, kv_scr, parts_scr, in_sems, out_sems) = refs[4:6], refs[6:]
    step = pl.program_id(0)
    entries = in_sems.shape[0]
    per_part = arrived[0].shape[0]

    def rows_of(e):
        return pl.ds(pl.multiple_of(e * BLK, BLK), BLK)

    def fetch(e, part, slot):
        return pltpu.make_async_copy(arrived[part].at[slot], kv_scr.at[rows_of(e)], in_sems.at[e])

    def give(e, part, slot):
        return pltpu.make_async_copy(parts_scr.at[rows_of(e)], back[part].at[slot], out_sems.at[e])

    def start(copy, e):
        slot = slot_ref[e]
        for part in range(2):

            @pl.when(slot // per_part == part)
            def _():
                copy(e, part, slot % per_part).start()

    @pl.when(step == 0)
    def _():
        for e in range(entries):
            start(fetch, e)

    first = step * list_len
    for l in range(list_len):
        fetch(first + l, 0, 0).wait()
    here = pl.ds(pl.multiple_of(step * list_len * BLK, list_len * BLK), list_len * BLK)
    keys = [kv_scr[here, j * PAIR : (j + 1) * PAIR] for j in range(KV // PAIR)]
    values = [kv_scr[here, KV + j * PAIR : KV + (j + 1) * PAIR] for j in range(KV // PAIR)]
    queries = q_ref[...] * jnp.asarray(TEMPER, BF16)
    pairs = range(KV // PAIR)
    wide = [two_groups(queries, j) for j in pairs]
    scores = [jnp.dot(keys[j], wide[j], preferred_element_type=F32) for j in pairs]
    attended, scales = [], []
    for j in pairs:
        expo = jnp.exp(scores[j] - jnp.max(scores[j], axis=0, keepdims=True))
        scale = 1.0 / jnp.sum(expo, axis=0, keepdims=True)
        expo_scr[j] = expo.astype(BF16)
        attended.append(head_rows(dot_tn(values[j], expo_scr[j]) * scale))
        scales += [
            jnp.broadcast_to(scale[:, i * BLK : (i + 1) * BLK], (HEAD_DIM, BLK))
            for i in range(2 * GROUP)
        ]
    exact = jnp.concatenate(attended, axis=0)
    attended = exact.astype(BF16).astype(F32)
    width = attended.shape[0]
    inverse = lax.rsqrt(jnp.sum(attended * attended, axis=0, keepdims=True) / width + EPSILON)
    normed = attended * inverse
    normed_ref[...] = normed.astype(BF16)
    normed_grad = ng_ref[...]
    shared = jnp.sum(normed_grad * normed, axis=0, keepdims=True) / width
    attended_grad = (normed_grad - normed * shared) * inverse
    scaled_grad = (attended_grad * jnp.concatenate(scales, axis=0)).astype(BF16)
    overlap = scaled_grad.astype(F32) * exact
    grads = [two_groups(scaled_grad, j) for j in pairs]
    prob_grads = [jnp.dot(values[j], grads[j], preferred_element_type=F32) for j in pairs]
    for j in pairs:
        heads = range(2 * GROUP * j, 2 * GROUP * (j + 1))
        row_dot = jnp.concatenate(
            [
                jnp.sum(overlap[h * HEAD_DIM : (h + 1) * HEAD_DIM], axis=0, keepdims=True)
                for h in heads
            ],
            axis=1,
        )
        expo = expo_scr[j]
        value_part = dot_nt(expo, grads[j])
        score_grad = (expo.astype(F32) * (prob_grads[j] - row_dot)).astype(BF16)
        query_grad = head_rows(dot_tn(keys[j], score_grad) * TEMPER).astype(BF16)
        qg_ref[heads.start * HEAD_DIM : heads.stop * HEAD_DIM, :] = query_grad
        key_part = dot_nt(score_grad, wide[j])
        parts_scr[here, j * PAIR : (j + 1) * PAIR] = key_part.astype(BF16)
        parts_scr[here, KV + j * PAIR : KV + (j + 1) * PAIR] = value_part.astype(BF16)
    for l in range(list_len):
        start(give, first + l)

    @pl.when(step == pl.num_programs(0) - 1)
    def _():
        for e in range(entries):
            give(e, 0, 0).wait()


def attention(slots, queries, normed_grad, arrived, list_len):
    width, rows = queries.shape
    blocks = rows // BLK
    entries = blocks * list_len
    row_spec = pl.BlockSpec((width, BLK), lambda r, s: (0, r))
    anywhere = pl.BlockSpec(memory_space=pl.ANY)
    keys = list_len * BLK
    pairs = HEADS * rows * keys
    return pl.pallas_call(
        functools.partial(attention_kernel, list_len),
        grid_spec=pltpu.PrefetchScalarGridSpec(
            num_scalar_prefetch=1,
            grid=(blocks,),
            in_specs=[row_spec, row_spec, anywhere, anywhere],
            out_specs=[row_spec, row_spec, anywhere, anywhere],
            scratch_shapes=[
                pltpu.VMEM((KV // PAIR, keys, 2 * GROUP * BLK), BF16),
                pltpu.VMEM((entries * BLK, 2 * KV), BF16),
                pltpu.VMEM((entries * BLK, 2 * KV), BF16),
                pltpu.SemaphoreType.DMA((entries,)),
                pltpu.SemaphoreType.DMA((entries,)),
            ],
        ),
        out_shape=[jax.ShapeDtypeStruct((width, rows), BF16)] * 2
        + [jax.ShapeDtypeStruct(arrived[0].shape, BF16)] * 2,
        compiler_params=params(56),
        cost_estimate=pl.CostEstimate(
            flops=12 * pairs * HEAD_DIM, bytes_accessed=16 * rows * width, transcendentals=pairs
        ),
        name="attention",
    )(slots, queries, normed_grad, *arrived)


def project_kernel(tokens_ref, wk_ref, wv_ref, out_ref):
    tokens = tokens_ref[...]
    for first, weight in ((0, wk_ref), (KV, wv_ref)):
        out = jnp.dot(tokens, weight[...], preferred_element_type=F32)
        out_ref[0, :, first : first + KV] = out.astype(BF16)


def project(tokens, w_key, w_value):
    rows, width = tokens.shape
    weight = pl.BlockSpec((width, KV), lambda r: (0, 0))
    return pl.pallas_call(
        project_kernel,
        grid=(rows // BLK,),
        in_specs=[pl.BlockSpec((BLK, width), lambda r: (r, 0)), weight, weight],
        out_specs=pl.BlockSpec((1, BLK, 2 * KV), lambda r: (r, 0, 0)),
        out_shape=jax.ShapeDtypeStruct((rows // BLK, BLK, 2 * KV), BF16),
        compiler_params=params(56),
        name="project",
    )(tokens, w_key, w_value)


def pack_kernel(slots, picked_ref, tile_ref, out_ref, sems):
    copies = [
        pltpu.make_async_copy(tile_ref.at[picked_ref[i]], out_ref.at[i], sems.at[i])
        for i in range(slots)
    ]
    for copy in copies:
        copy.start()
    for copy in copies:
        copy.wait()


def pack(picked, tile, flops):
    slots = picked.shape[0]
    return pl.pallas_call(
        functools.partial(pack_kernel, slots),
        in_specs=[
            pl.BlockSpec(memory_space=pltpu.SMEM),
            pl.BlockSpec(memory_space=pltpu.VMEM),
        ],
        out_specs=pl.BlockSpec(memory_space=pl.ANY),
        out_shape=jax.ShapeDtypeStruct((slots,) + tile.shape[1:], BF16),
        scratch_shapes=[pltpu.SemaphoreType.DMA((slots,))],
        compiler_params=params(56),
        cost_estimate=pl.CostEstimate(
            flops=flops, bytes_accessed=2 * slots * tile[0].size, transcendentals=0
        ),
        name="pack",
    )(picked, tile)


def finish_kernel(near_ref, far_ref, term_ref, wk_ref, wv_ref, out_ref):
    grad = (near_ref[0].astype(F32) + far_ref[0].astype(F32)).astype(BF16)
    total = dot_nt(grad[:, :KV], wk_ref[...]) + dot_nt(grad[:, KV:], wv_ref[...])
    out_ref[...] = (term_ref[...] + total).astype(BF16)


def finish(near, far, term, w_key, w_value):
    rows, width = term.shape
    weight = pl.BlockSpec((width, KV), lambda r: (0, 0))
    part = pl.BlockSpec((1, BLK, 2 * KV), lambda r: (r, 0, 0))
    row = pl.BlockSpec((BLK, width), lambda r: (r, 0))
    return pl.pallas_call(
        finish_kernel,
        grid=(rows // BLK,),
        in_specs=[part, part, row, weight, weight],
        out_specs=row,
        out_shape=jax.ShapeDtypeStruct((rows, width), BF16),
        compiler_params=params(32),
        name="finish",
    )(near, far, term, w_key, w_value)


def owner_kernel(chunk, wanted_ref, parts_ref, out_ref, total):
    step = pl.program_id(0)

    @pl.when(step == 0)
    def _():
        total[...] = jnp.zeros_like(total)

    for s in range(chunk):
        block = wanted_ref[step * chunk + s]

        @pl.when(block >= 0)
        def _():
            total[block] += parts_ref[s].astype(F32)

    @pl.when(step == pl.num_programs(0) - 1)
    def _():
        out_ref[...] = total[...].astype(BF16)


def owner_sum(wanted, returned, blocks):
    slots = returned.shape[0]
    chunk = 4
    return pl.pallas_call(
        functools.partial(owner_kernel, chunk),
        grid_spec=pltpu.PrefetchScalarGridSpec(
            num_scalar_prefetch=1,
            grid=(slots // chunk,),
            in_specs=[pl.BlockSpec((chunk, BLK, 2 * KV), lambda s, w: (s, 0, 0))],
            out_specs=pl.BlockSpec((blocks, BLK, 2 * KV), lambda s, w: (0, 0, 0)),
            scratch_shapes=[pltpu.VMEM((blocks, BLK, 2 * KV), F32)],
        ),
        out_shape=jax.ShapeDtypeStruct((blocks, BLK, 2 * KV), BF16),
        compiler_params=params(56),
        name="owner_sum",
    )(wanted, returned)


def shards(patches, out_grad, w_query, w_key, w_value, w_out, key_tiles, key_blocks):
    tokens = patches[0]
    rows = tokens.shape[0]
    tile_count = lax.axis_size("tile")
    half = tile_count // 2
    my_tile = lax.axis_index("tile")
    my_half, my_place = my_tile // half, my_tile % half
    groups = [list(range(half)), list(range(half, tile_count))]
    block_count = rows // BLK
    list_len = key_tiles.shape[2]
    entry_count = block_count * list_len

    def cross(value, shift):
        pairs = [
            (v * tile_count + t, (1 - v) * tile_count + (t + shift) % tile_count)
            for v in range(2)
            for t in range(tile_count)
        ]
        return lax.ppermute(value, ("vintage", "tile"), pairs)

    def exchange(value):
        return lax.all_to_all(
            value, "tile", split_axis=0, concat_axis=0, tiled=True, axis_index_groups=groups
        )

    def half_rows(table):
        table = table[0].reshape(2, half, entry_count)
        return lax.dynamic_index_in_dim(table, my_half, 0, keepdims=False)

    tiles, picks = half_rows(key_tiles), half_rows(key_blocks)
    earlier = jnp.arange(entry_count)[:, None] > jnp.arange(entry_count)[None, :]
    same = (tiles[:, :, None] == tiles[:, None, :]) & earlier[None]
    ranks = jnp.sum(same.astype(jnp.int32), axis=2)
    is_far = (tiles // half != my_half).astype(jnp.int32)
    slots = (is_far * half + tiles % half) * CAP + ranks
    my_slots = lax.dynamic_index_in_dim(slots, my_place, 0, keepdims=False)
    part_ids = jnp.arange(2, dtype=jnp.int32)[:, None, None] * half + my_place
    ids = part_ids * CAP + jnp.arange(CAP, dtype=jnp.int32)[None, None, :]
    hits = slots[None, :, :, None] == ids[:, :, None, :]
    wanted = jnp.sum(jnp.where(hits, picks[None, :, :, None] + 1, 0), axis=2) - 1
    wanted = wanted.reshape(2, half * CAP)

    picked = jnp.maximum(wanted, 0)
    mine = project(tokens, w_key, w_value)
    far_tile = cross(mine, half)
    near_tile = cross(mine, 0)
    arrived = [
        exchange(pack(picked[0], near_tile, 0)),
        exchange(pack(picked[1], far_tile, SWAP_FLOPS)),
    ]
    queries = lax.dot_general(
        w_query, tokens, (((0,), (1,)), ((), ())), preferred_element_type=F32
    ).astype(BF16)
    normed_grad = dot_nt(w_out, out_grad[0])
    normed_low, query_grad, *back = attention(my_slots, queries, normed_grad, arrived, list_len)
    layer_out = dot_tn(normed_low, w_out).astype(BF16)
    query_term = lax.dot_general(
        query_grad, w_query, (((0,), (1,)), ((), ())), preferred_element_type=F32
    )
    far = cross(owner_sum(wanted[1], exchange(back[1]), block_count), half)
    near_parts, query_term, layer_out = lax.optimization_barrier(
        (exchange(back[0]), query_term, layer_out)
    )
    near = cross(owner_sum(wanted[0], near_parts, block_count), 0)
    input_grad = finish(near, far, query_term, w_key, w_value)
    return (layer_out[None], input_grad[None])


def solution(mesh):
    in_specs = (
        P("vintage", "tile", None),
        P("vintage", "tile", None),
        P(),
        P(),
        P(),
        P(),
        P("vintage", None, None),
        P("vintage", None, None),
    )
    out_specs = (P("vintage", "tile", None), P("vintage", "tile", None))
    return jax.shard_map(shards, mesh=mesh, in_specs=in_specs, out_specs=out_specs, check_vma=False)
```

```python
import functools

import jax
import jax.numpy as jnp
from jax import lax
from jax.experimental import pallas as pl
from jax.experimental.pallas import tpu as pltpu
from jax.sharding import PartitionSpec as P

HEADS = 12
KV_HEADS = 4
HEAD_DIM = 64
BLK = 128
CAP = 2
GROUP = HEADS // KV_HEADS
KV = KV_HEADS * HEAD_DIM
PAIR = 2 * HEAD_DIM
SWAP_FLOPS = 40_000_000_000
TEMPER = HEAD_DIM ** (-0.5)
EPSILON = 1e-06
WHOLE = pl.BlockSpec(memory_space=pltpu.VMEM)
F32 = jnp.float32
BF16 = jnp.bfloat16


def params(mebibytes):
    return pltpu.CompilerParams(vmem_limit_bytes=mebibytes * 1024 * 1024)


def dot_nt(a, b):
    return lax.dot_general(a, b, (((1,), (1,)), ((), ())), preferred_element_type=F32)


def dot_tn(a, b):
    return lax.dot_general(a, b, (((0,), (0,)), ((), ())), preferred_element_type=F32)


def feature_heads(features, g):
    first = g * GROUP
    return jnp.concatenate(
        [features[(first + r) * HEAD_DIM : (first + r + 1) * HEAD_DIM] for r in range(GROUP)],
        axis=1,
    )


def two_groups(features, j):
    low, high = feature_heads(features, 2 * j), feature_heads(features, 2 * j + 1)
    zeros = jnp.zeros_like(low)
    return jnp.concatenate(
        [jnp.concatenate([low, zeros], axis=1), jnp.concatenate([zeros, high], axis=1)], axis=0
    )


def head_rows(pair_out):
    heads = []
    for i in range(2 * GROUP):
        top = i // GROUP * HEAD_DIM
        heads.append(pair_out[top : top + HEAD_DIM, i * BLK : (i + 1) * BLK])
    return jnp.concatenate(heads, axis=0)


def attention_kernel(list_len, slot_ref, q_ref, ng_ref, *refs):
    expo_scr, kv_scr, parts_scr, in_sems, out_sems = refs[-5:]
    sources = (len(refs) - 7) // 2
    arrived, (normed_ref, qg_ref) = refs[:sources], refs[sources : sources + 2]
    back = refs[sources + 2 : 2 * sources + 2]
    step = pl.program_id(0)
    entries = in_sems.shape[0]

    def rows_of(e):
        return pl.ds(pl.multiple_of(e * BLK, BLK), BLK)

    def fetch(e, source, slot):
        return pltpu.make_async_copy(
            arrived[source].at[slot], kv_scr.at[rows_of(e)], in_sems.at[e]
        )

    def give(e, source, slot):
        return pltpu.make_async_copy(
            parts_scr.at[rows_of(e)], back[source].at[slot], out_sems.at[e]
        )

    def start(copy, begin, count):
        def one(i, carry):
            e = begin + i
            slot = slot_ref[e]
            for source in range(sources):

                @pl.when(slot // CAP == source)
                def _():
                    copy(e, source, slot % CAP).start()

            return carry

        lax.fori_loop(0, count, one, 0)

    @pl.when(step == 0)
    def _():
        start(fetch, 0, entries)

    first = step * list_len
    for l in range(list_len):
        fetch(first + l, 0, 0).wait()
    here = pl.ds(pl.multiple_of(step * list_len * BLK, list_len * BLK), list_len * BLK)
    keys = [kv_scr[here, j * PAIR : (j + 1) * PAIR] for j in range(KV // PAIR)]
    values = [kv_scr[here, KV + j * PAIR : KV + (j + 1) * PAIR] for j in range(KV // PAIR)]
    queries = q_ref[...] * jnp.asarray(TEMPER, BF16)
    pairs = range(KV // PAIR)
    wide = [two_groups(queries, j) for j in pairs]
    scores = [jnp.dot(keys[j], wide[j], preferred_element_type=F32) for j in pairs]
    attended, scales = [], []
    for j in pairs:
        expo = jnp.exp(scores[j] - jnp.max(scores[j], axis=0, keepdims=True))
        scale = 1.0 / jnp.sum(expo, axis=0, keepdims=True)
        expo_scr[j] = expo.astype(BF16)
        attended.append(head_rows(dot_tn(values[j], expo_scr[j]) * scale))
        scales += [
            jnp.broadcast_to(scale[:, i * BLK : (i + 1) * BLK], (HEAD_DIM, BLK))
            for i in range(2 * GROUP)
        ]
    exact = jnp.concatenate(attended, axis=0)
    attended = exact.astype(BF16).astype(F32)
    width = attended.shape[0]
    inverse = lax.rsqrt(jnp.sum(attended * attended, axis=0, keepdims=True) / width + EPSILON)
    normed = attended * inverse
    normed_ref[...] = normed.astype(BF16)
    normed_grad = ng_ref[...]
    shared = jnp.sum(normed_grad * normed, axis=0, keepdims=True) / width
    attended_grad = (normed_grad - normed * shared) * inverse
    scaled_grad = (attended_grad * jnp.concatenate(scales, axis=0)).astype(BF16)
    overlap = scaled_grad.astype(F32) * exact
    grads = [two_groups(scaled_grad, j) for j in pairs]
    prob_grads = [jnp.dot(values[j], grads[j], preferred_element_type=F32) for j in pairs]
    for j in pairs:
        heads = range(2 * GROUP * j, 2 * GROUP * (j + 1))
        row_dot = jnp.concatenate(
            [
                jnp.sum(overlap[h * HEAD_DIM : (h + 1) * HEAD_DIM], axis=0, keepdims=True)
                for h in heads
            ],
            axis=1,
        )
        expo = expo_scr[j]
        value_part = dot_nt(expo, grads[j])
        score_grad = (expo.astype(F32) * (prob_grads[j] - row_dot)).astype(BF16)
        query_grad = head_rows(dot_tn(keys[j], score_grad) * TEMPER).astype(BF16)
        qg_ref[heads.start * HEAD_DIM : heads.stop * HEAD_DIM, :] = query_grad
        key_part = dot_nt(score_grad, wide[j])
        parts_scr[here, j * PAIR : (j + 1) * PAIR] = key_part.astype(BF16)
        parts_scr[here, KV + j * PAIR : KV + (j + 1) * PAIR] = value_part.astype(BF16)
    start(give, first, list_len)

    @pl.when(step == pl.num_programs(0) - 1)
    def _():
        for e in range(entries):
            give(e, 0, 0).wait()


def attention(slots, queries, normed_grad, arrived, list_len):
    width, rows = queries.shape
    blocks = rows // BLK
    entries = blocks * list_len
    row_spec = pl.BlockSpec((width, BLK), lambda r, s: (0, r))
    anywhere = pl.BlockSpec(memory_space=pl.ANY)
    keys = list_len * BLK
    pairs = HEADS * rows * keys
    return pl.pallas_call(
        functools.partial(attention_kernel, list_len),
        grid_spec=pltpu.PrefetchScalarGridSpec(
            num_scalar_prefetch=1,
            grid=(blocks,),
            in_specs=[row_spec, row_spec] + [anywhere] * len(arrived),
            out_specs=[row_spec, row_spec] + [anywhere] * len(arrived),
            scratch_shapes=[
                pltpu.VMEM((KV // PAIR, keys, 2 * GROUP * BLK), BF16),
                pltpu.VMEM((entries * BLK, 2 * KV), BF16),
                pltpu.VMEM((entries * BLK, 2 * KV), BF16),
                pltpu.SemaphoreType.DMA((entries,)),
                pltpu.SemaphoreType.DMA((entries,)),
            ],
        ),
        out_shape=[jax.ShapeDtypeStruct((width, rows), BF16)] * 2
        + [jax.ShapeDtypeStruct(arrived[0].shape, BF16)] * len(arrived),
        compiler_params=params(56),
        cost_estimate=pl.CostEstimate(
            flops=12 * pairs * HEAD_DIM, bytes_accessed=16 * rows * width, transcendentals=pairs
        ),
        name="attention",
    )(slots, queries, normed_grad, *arrived)


def project_kernel(tokens_ref, wk_ref, wv_ref, out_ref):
    tokens = tokens_ref[...]
    for first, weight in ((0, wk_ref), (KV, wv_ref)):
        out = jnp.dot(tokens, weight[...], preferred_element_type=F32)
        out_ref[:, first : first + KV] = out.astype(BF16)


def project(tokens, w_key, w_value):
    return pl.pallas_call(
        project_kernel,
        in_specs=[WHOLE] * 3,
        out_specs=WHOLE,
        out_shape=jax.ShapeDtypeStruct((tokens.shape[0], 2 * KV), BF16),
        compiler_params=params(16),
        name="project",
    )(tokens, w_key, w_value)


def pack_kernel(peers, picked_ref, tile_ref, *refs):
    outs, sems = refs[:peers], refs[peers]
    copies = [
        pltpu.make_async_copy(
            tile_ref.at[picked_ref[p * CAP + s]], outs[p].at[s], sems.at[p * CAP + s]
        )
        for p in range(peers)
        for s in range(CAP)
    ]
    for copy in copies:
        copy.start()
    for copy in copies:
        copy.wait()


def pack(picked, tile, flops):
    peers = picked.shape[0] // CAP
    shape = (CAP,) + tile.shape[1:]
    return pl.pallas_call(
        functools.partial(pack_kernel, peers),
        in_specs=[pl.BlockSpec(memory_space=pltpu.SMEM), WHOLE],
        out_specs=[pl.BlockSpec(memory_space=pl.ANY)] * peers,
        out_shape=[jax.ShapeDtypeStruct(shape, BF16)] * peers,
        scratch_shapes=[pltpu.SemaphoreType.DMA((peers * CAP,))],
        compiler_params=params(16),
        cost_estimate=pl.CostEstimate(
            flops=flops, bytes_accessed=2 * peers * CAP * tile[0].size, transcendentals=0
        ),
        name="pack",
    )(picked, tile)


def finish_kernel(near_ref, far_ref, term_ref, wk_ref, wv_ref, out_ref):
    grad = (near_ref[...].astype(F32) + far_ref[...].astype(F32)).astype(BF16)
    total = dot_nt(grad[:, :KV], wk_ref[...]) + dot_nt(grad[:, KV:], wv_ref[...])
    out_ref[...] = (term_ref[...] + total).astype(BF16)


def finish(near, far, term, w_key, w_value):
    return pl.pallas_call(
        finish_kernel,
        in_specs=[WHOLE] * 5,
        out_specs=WHOLE,
        out_shape=jax.ShapeDtypeStruct(term.shape, BF16),
        compiler_params=params(24),
        name="finish",
    )(near, far, term, w_key, w_value)


def owner_kernel(wanted_ref, *refs):
    parts, (out_ref, total) = refs[:-2], refs[-2:]
    total[...] = jnp.zeros_like(total)
    for p, part in enumerate(parts):
        for s in range(CAP):
            block = wanted_ref[p * CAP + s]

            @pl.when(block >= 0)
            def _():
                total[block] += part[s].astype(F32)

    out_ref[...] = total[...].astype(BF16)


def owner_sum(wanted, parts, blocks):
    shape = (blocks,) + parts[0].shape[1:]
    return pl.pallas_call(
        owner_kernel,
        in_specs=[pl.BlockSpec(memory_space=pltpu.SMEM)] + [WHOLE] * len(parts),
        out_specs=WHOLE,
        out_shape=jax.ShapeDtypeStruct(shape, BF16),
        scratch_shapes=[pltpu.VMEM(shape, F32)],
        compiler_params=params(16),
        name="owner_sum",
    )(wanted, *parts)


def shards(patches, out_grad, w_query, w_key, w_value, w_out, key_tiles, key_blocks):
    tokens = patches[0]
    rows = tokens.shape[0]
    tile_count = lax.axis_size("tile")
    half = tile_count // 2
    my_tile = lax.axis_index("tile")
    my_half, my_place = my_tile // half, my_tile % half
    block_count = rows // BLK
    list_len = key_tiles.shape[2]
    entry_count = block_count * list_len

    def cross(value, shift):
        pairs = [
            (v * tile_count + t, (1 - v) * tile_count + (t + shift) % tile_count)
            for v in range(2)
            for t in range(tile_count)
        ]
        return lax.ppermute(value, ("vintage", "tile"), pairs)

    def exchange(values):
        moved = [values[0]]
        for p in range(1, half):
            pairs = [(t, t // half * half + (t % half ^ p)) for t in range(tile_count)]
            moved.append(lax.ppermute(values[p], "tile", pairs))
        return moved

    def half_rows(table):
        table = table[0].reshape(2, half, entry_count)
        return lax.dynamic_index_in_dim(table, my_half, 0, keepdims=False)

    tiles, picks = half_rows(key_tiles), half_rows(key_blocks)
    earlier = jnp.arange(entry_count)[:, None] > jnp.arange(entry_count)[None, :]
    same = (tiles[:, :, None] == tiles[:, None, :]) & earlier[None]
    ranks = jnp.sum(same.astype(jnp.int32), axis=2)
    is_far = (tiles // half != my_half).astype(jnp.int32)
    holders = (tiles % half) ^ my_place
    my_slots = lax.dynamic_index_in_dim(
        (is_far * half + holders) * CAP + ranks, my_place, 0, keepdims=False
    )
    slots = (is_far * half + tiles % half) * CAP + ranks
    slots = slots[jnp.arange(half) ^ my_place]
    picks = picks[jnp.arange(half) ^ my_place]
    part_ids = jnp.arange(2, dtype=jnp.int32)[:, None, None] * half + my_place
    ids = part_ids * CAP + jnp.arange(CAP, dtype=jnp.int32)[None, None, :]
    hits = slots[None, :, :, None] == ids[:, :, None, :]
    wanted = jnp.sum(jnp.where(hits, picks[None, :, :, None] + 1, 0), axis=2) - 1
    wanted = wanted.reshape(2, half * CAP)

    picked = jnp.maximum(wanted, 0)
    mine = project(tokens, w_key, w_value).reshape(block_count, BLK, 2 * KV)
    far_tile = cross(mine, half)
    near_tile = cross(mine, 0)
    arrived = exchange(pack(picked[0], near_tile, 0)) + exchange(
        pack(picked[1], far_tile, SWAP_FLOPS)
    )
    queries = lax.dot_general(
        w_query, tokens, (((0,), (1,)), ((), ())), preferred_element_type=F32
    ).astype(BF16)
    normed_grad = dot_nt(w_out, out_grad[0])
    normed_low, query_grad, *back = attention(my_slots, queries, normed_grad, arrived, list_len)
    layer_out = dot_tn(normed_low, w_out).astype(BF16)
    query_term = lax.dot_general(
        query_grad, w_query, (((0,), (1,)), ((), ())), preferred_element_type=F32
    )
    far = cross(owner_sum(wanted[1], exchange(back[half:]), block_count), half)
    near_parts, query_term, layer_out = lax.optimization_barrier(
        (exchange(back[:half]), query_term, layer_out)
    )
    near = cross(owner_sum(wanted[0], near_parts, block_count), 0)
    input_grad = finish(
        near.reshape(rows, 2 * KV), far.reshape(rows, 2 * KV), query_term, w_key, w_value
    )
    return (layer_out[None], input_grad[None])


def solution(mesh):
    in_specs = (
        P("vintage", "tile", None),
        P("vintage", "tile", None),
        P(),
        P(),
        P(),
        P(),
        P("vintage", None, None),
        P("vintage", None, None),
    )
    out_specs = (P("vintage", "tile", None), P("vintage", "tile", None))
    return jax.shard_map(shards, mesh=mesh, in_specs=in_specs, out_specs=out_specs, check_vma=False)
```

```python
import functools

import jax
import jax.numpy as jnp
from jax import lax
from jax.experimental import pallas as pl
from jax.experimental.pallas import tpu as pltpu
from jax.sharding import PartitionSpec as P

HEADS = 12
KV_HEADS = 4
HEAD_DIM = 64
BLK = 128
CAP = 2
GROUP = HEADS // KV_HEADS
KV = KV_HEADS * HEAD_DIM
PAIR = 2 * HEAD_DIM
CODE = 16
MAJOR = 4
TEMPER = HEAD_DIM ** (-0.5)
EPSILON = 1e-06
WHOLE = pl.BlockSpec(memory_space=pltpu.VMEM)
F32 = jnp.float32
BF16 = jnp.bfloat16


def params(mebibytes):
    return pltpu.CompilerParams(vmem_limit_bytes=mebibytes * 1024 * 1024)


def dot_nt(a, b):
    return lax.dot_general(a, b, (((1,), (1,)), ((), ())), preferred_element_type=F32)


def dot_tn(a, b):
    return lax.dot_general(a, b, (((0,), (0,)), ((), ())), preferred_element_type=F32)


def feature_heads(features, g):
    first = g * GROUP
    return jnp.concatenate(
        [features[(first + r) * HEAD_DIM : (first + r + 1) * HEAD_DIM] for r in range(GROUP)],
        axis=1,
    )


def two_groups(features, j):
    low, high = feature_heads(features, 2 * j), feature_heads(features, 2 * j + 1)
    zeros = jnp.zeros_like(low)
    return jnp.concatenate(
        [jnp.concatenate([low, zeros], axis=1), jnp.concatenate([zeros, high], axis=1)], axis=0
    )


def head_rows(pair_out):
    heads = []
    for i in range(2 * GROUP):
        top = i // GROUP * HEAD_DIM
        heads.append(pair_out[top : top + HEAD_DIM, i * BLK : (i + 1) * BLK])
    return jnp.concatenate(heads, axis=0)


def attention_kernel(list_len, get_ref, put_ref, q_ref, ng_ref, *refs):
    expo_scr, kv_scr, parts_scr, in_sems, out_sems = refs[-5:]
    sources = (len(refs) - 7) // 2
    arrived, (normed_ref, qg_ref) = refs[:sources], refs[sources : sources + 2]
    back = refs[sources + 2 : 2 * sources + 2]
    step = pl.program_id(0)
    entries = in_sems.shape[0]

    def rows_of(e):
        return pl.ds(pl.multiple_of(e * BLK, BLK), BLK)

    def fetch(e, source, slot):
        return pltpu.make_async_copy(
            arrived[source].at[slot], kv_scr.at[rows_of(e)], in_sems.at[e]
        )

    def give(e, source, slot):
        return pltpu.make_async_copy(
            parts_scr.at[rows_of(e)], back[source].at[slot], out_sems.at[e]
        )

    def start(copy, code_ref, begin, count):
        def one(i, carry):
            e = begin + i
            code = code_ref[e]
            for source in range(sources):

                @pl.when(code // CODE == source)
                def _():
                    copy(e, source, code % CODE).start()

            return carry

        lax.fori_loop(0, count, one, 0)

    @pl.when(step == 0)
    def _():
        start(fetch, get_ref, 0, entries)

    first = step * list_len
    for l in range(list_len):
        fetch(first + l, 0, 0).wait()
    here = pl.ds(pl.multiple_of(step * list_len * BLK, list_len * BLK), list_len * BLK)
    keys = [kv_scr[here, j * PAIR : (j + 1) * PAIR] for j in range(KV // PAIR)]
    values = [kv_scr[here, KV + j * PAIR : KV + (j + 1) * PAIR] for j in range(KV // PAIR)]
    queries = q_ref[...] * jnp.asarray(TEMPER, BF16)
    pairs = range(KV // PAIR)
    wide = [two_groups(queries, j) for j in pairs]
    scores = [jnp.dot(keys[j], wide[j], preferred_element_type=F32) for j in pairs]
    attended, scales = [], []
    for j in pairs:
        expo = jnp.exp(scores[j] - jnp.max(scores[j], axis=0, keepdims=True))
        scale = 1.0 / jnp.sum(expo, axis=0, keepdims=True)
        expo_scr[j] = expo.astype(BF16)
        attended.append(head_rows(dot_tn(values[j], expo_scr[j]) * scale))
        scales += [
            jnp.broadcast_to(scale[:, i * BLK : (i + 1) * BLK], (HEAD_DIM, BLK))
            for i in range(2 * GROUP)
        ]
    exact = jnp.concatenate(attended, axis=0)
    attended = exact.astype(BF16).astype(F32)
    width = attended.shape[0]
    inverse = lax.rsqrt(jnp.sum(attended * attended, axis=0, keepdims=True) / width + EPSILON)
    normed = attended * inverse
    normed_ref[...] = normed.astype(BF16)
    normed_grad = ng_ref[...]
    shared = jnp.sum(normed_grad * normed, axis=0, keepdims=True) / width
    attended_grad = (normed_grad - normed * shared) * inverse
    scaled_grad = (attended_grad * jnp.concatenate(scales, axis=0)).astype(BF16)
    overlap = scaled_grad.astype(F32) * exact
    grads = [two_groups(scaled_grad, j) for j in pairs]
    prob_grads = [jnp.dot(values[j], grads[j], preferred_element_type=F32) for j in pairs]
    for j in pairs:
        heads = range(2 * GROUP * j, 2 * GROUP * (j + 1))
        row_dot = jnp.concatenate(
            [
                jnp.sum(overlap[h * HEAD_DIM : (h + 1) * HEAD_DIM], axis=0, keepdims=True)
                for h in heads
            ],
            axis=1,
        )
        expo = expo_scr[j]
        value_part = dot_nt(expo, grads[j])
        score_grad = (expo.astype(F32) * (prob_grads[j] - row_dot)).astype(BF16)
        query_grad = head_rows(dot_tn(keys[j], score_grad) * TEMPER).astype(BF16)
        qg_ref[heads.start * HEAD_DIM : heads.stop * HEAD_DIM, :] = query_grad
        key_part = dot_nt(score_grad, wide[j])
        parts_scr[here, j * PAIR : (j + 1) * PAIR] = key_part.astype(BF16)
        parts_scr[here, KV + j * PAIR : KV + (j + 1) * PAIR] = value_part.astype(BF16)
    start(give, put_ref, first, list_len)

    @pl.when(step == pl.num_programs(0) - 1)
    def _():
        for e in range(entries):
            give(e, 0, 0).wait()


def attention(gets, puts, queries, normed_grad, arrived, list_len):
    width, rows = queries.shape
    slot_shape = (CAP,) + arrived[0].shape[1:]
    blocks = rows // BLK
    entries = blocks * list_len
    row_spec = pl.BlockSpec((width, BLK), lambda r, g, p: (0, r))
    anywhere = pl.BlockSpec(memory_space=pl.ANY)
    keys = list_len * BLK
    pairs = HEADS * rows * keys
    return pl.pallas_call(
        functools.partial(attention_kernel, list_len),
        grid_spec=pltpu.PrefetchScalarGridSpec(
            num_scalar_prefetch=2,
            grid=(blocks,),
            in_specs=[row_spec, row_spec] + [anywhere] * len(arrived),
            out_specs=[row_spec, row_spec] + [anywhere] * len(arrived),
            scratch_shapes=[
                pltpu.VMEM((KV // PAIR, keys, 2 * GROUP * BLK), BF16),
                pltpu.VMEM((entries * BLK, 2 * KV), BF16),
                pltpu.VMEM((entries * BLK, 2 * KV), BF16),
                pltpu.SemaphoreType.DMA((entries,)),
                pltpu.SemaphoreType.DMA((entries,)),
            ],
        ),
        out_shape=[jax.ShapeDtypeStruct((width, rows), BF16)] * 2
        + [jax.ShapeDtypeStruct(slot_shape, BF16)] * len(arrived),
        compiler_params=params(56),
        cost_estimate=pl.CostEstimate(
            flops=12 * pairs * HEAD_DIM, bytes_accessed=16 * rows * width, transcendentals=pairs
        ),
        name="attention",
    )(gets, puts, queries, normed_grad, *arrived)


def project_kernel(tokens_hbm, wk_hbm, wv_hbm, out_ref, tokens, wk, wv, sems):
    moves = ((wk_hbm, wk), (tokens_hbm, tokens), (wv_hbm, wv))
    copies = [pltpu.make_async_copy(src, dst, sems.at[i]) for i, (src, dst) in enumerate(moves)]
    for copy in copies:
        copy.start()
    copies[0].wait()
    copies[1].wait()
    keys = jnp.dot(tokens[...], wk[...], preferred_element_type=F32)
    out_ref[:, :KV] = keys.astype(BF16)
    copies[2].wait()
    values = jnp.dot(tokens[...], wv[...], preferred_element_type=F32)
    out_ref[:, KV:] = values.astype(BF16)


def project(tokens, w_key, w_value):
    args = (tokens, w_key, w_value)
    return pl.pallas_call(
        project_kernel,
        in_specs=[pl.BlockSpec(memory_space=pl.ANY)] * 3,
        out_specs=WHOLE,
        out_shape=jax.ShapeDtypeStruct((tokens.shape[0], 2 * KV), BF16),
        scratch_shapes=[pltpu.VMEM(x.shape, BF16) for x in args]
        + [pltpu.SemaphoreType.DMA((3,))],
        compiler_params=params(56),
        name="project",
    )(*args)


def pack_kernel(picked_ref, tile_ref, *outs):
    for i, out in enumerate(outs):
        for s in range(CAP):
            out[s] = tile_ref[picked_ref[i * CAP + s]]


def pack(picked, tile):
    peers = picked.shape[0] // CAP
    shape = (CAP,) + tile.shape[1:]
    return pl.pallas_call(
        pack_kernel,
        in_specs=[pl.BlockSpec(memory_space=pltpu.SMEM), WHOLE],
        out_specs=[WHOLE] * peers,
        out_shape=[jax.ShapeDtypeStruct(shape, BF16)] * peers,
        compiler_params=params(16),
        name="pack",
    )(picked, tile)


def finish_kernel(parts, *refs):
    term_ref, wk_ref, wv_ref, out_ref = refs[parts:]
    grad = refs[0][...].astype(F32)
    for ref in refs[1:parts]:
        grad += ref[...].astype(F32)
    grad = grad.astype(BF16)
    total = dot_nt(grad[:, :KV], wk_ref[...]) + dot_nt(grad[:, KV:], wv_ref[...])
    out_ref[...] = (term_ref[...] + total).astype(BF16)


def finish(parts, term, w_key, w_value):
    return pl.pallas_call(
        functools.partial(finish_kernel, len(parts)),
        in_specs=[WHOLE] * (len(parts) + 3),
        out_specs=WHOLE,
        out_shape=jax.ShapeDtypeStruct(term.shape, BF16),
        compiler_params=params(24),
        name="finish",
    )(*parts, term, w_key, w_value)


def owner_kernel(peers, wanted_ref, *refs):
    parts, extra, (out_ref, total) = refs[:peers], refs[peers:-2], refs[-2:]
    total[...] = extra[0][...].astype(F32) if extra else jnp.zeros_like(total)
    for p, part in enumerate(parts):
        for s in range(CAP):
            block = wanted_ref[p * CAP + s]

            @pl.when(block >= 0)
            def _():
                total[block] += part[s].astype(F32)

    out_ref[...] = total[...].astype(BF16)


def owner_sum(wanted, parts, blocks, *extra):
    shape = (blocks,) + parts[0].shape[1:]
    args = (*parts, *extra)
    return pl.pallas_call(
        functools.partial(owner_kernel, len(parts)),
        in_specs=[pl.BlockSpec(memory_space=pltpu.SMEM)] + [WHOLE] * len(args),
        out_specs=WHOLE,
        out_shape=jax.ShapeDtypeStruct(shape, BF16),
        scratch_shapes=[pltpu.VMEM(shape, F32)],
        compiler_params=params(16),
        name="owner_sum",
    )(wanted, *args)


def shards(patches, out_grad, w_query, w_key, w_value, w_out, key_tiles, key_blocks):
    tokens = patches[0]
    rows = tokens.shape[0]
    tile_count = lax.axis_size("tile")
    plane = tile_count // MAJOR
    my_tile = lax.axis_index("tile")
    my_row, my_place = my_tile // plane, my_tile % plane
    block_count = rows // BLK
    list_len = key_tiles.shape[2]
    entry_count = block_count * list_len

    def swap(value, d, cross):
        pairs = [
            (v * tile_count + t, (v ^ cross) * tile_count + (t // plane ^ d) * plane + t % plane)
            for v in range(2)
            for t in range(tile_count)
        ]
        return lax.ppermute(value, ("vintage", "tile"), pairs)

    def after(value, earlier):
        return lax.optimization_barrier((value, earlier))[0]

    def spread(values, earlier=None):
        moved = []
        for i, value in enumerate(values):
            pairs = [(t, t // plane * plane + (t % plane ^ (i + 1))) for t in range(tile_count)]
            if earlier is not None:
                value = after(value, earlier[i])
            moved.append(lax.ppermute(value, "tile", pairs))
        return moved

    def plane_rows(table):
        table = table[0].reshape(MAJOR, plane, entry_count)
        return lax.dynamic_index_in_dim(table, my_row, 0, keepdims=False)

    def mine_of(table):
        return lax.dynamic_index_in_dim(table, my_place, 0, keepdims=False)

    tiles, picks = plane_rows(key_tiles), plane_rows(key_blocks)
    earlier = jnp.arange(entry_count)[:, None] > jnp.arange(entry_count)[None, :]
    same = (tiles[:, :, None] == tiles[:, None, :]) & earlier[None]
    ranks = jnp.sum(same.astype(jnp.int32), axis=2)
    groups, columns = (tiles // plane) ^ my_row, tiles % plane
    my_source = mine_of(groups) * plane + (mine_of(columns) ^ my_place)
    puts = my_source * CODE + mine_of(ranks)
    gets = jnp.where(my_source % plane == 0, my_source * CODE + mine_of(picks), puts)
    ids = jnp.arange(MAJOR * CAP, dtype=jnp.int32)
    slots = groups * CAP + ranks
    hits = (slots[:, None, :] == ids[None, :, None]) & (columns == my_place)[:, None, :]
    wanted = jnp.sum(jnp.where(hits, picks[:, None, :] + 1, 0), axis=2) - 1
    wanted = wanted[jnp.arange(plane) ^ my_place].reshape(plane, MAJOR, CAP)
    wanted = wanted.transpose(1, 0, 2).reshape(MAJOR, plane * CAP)
    picked = jnp.maximum(wanted[:, CAP:], 0)

    mine = project(tokens, w_key, w_value).reshape(block_count, BLK, 2 * KV)
    far_tile = swap(mine, 2, 1)
    next_tile = swap(mine, 1, 1)
    own_tile = swap(mine, 0, 1)
    own = spread(pack(picked[0], own_tile))
    beside = spread(pack(picked[1], next_tile), own)
    last_tile = swap(after(far_tile, own[-1]), 1, 0)
    far = spread(pack(picked[2], after(far_tile, own[-1])), beside)
    last = spread(pack(picked[3], last_tile), far)
    arrived = [own_tile, *own, next_tile, *beside, far_tile, *far, last_tile, *last]
    queries = lax.dot_general(
        w_query, tokens, (((0,), (1,)), ((), ())), preferred_element_type=F32
    ).astype(BF16)
    normed_grad = dot_nt(w_out, out_grad[0])
    normed_low, query_grad, *back = attention(
        gets, puts, queries, normed_grad, arrived, list_len
    )
    back = [back[d * plane : (d + 1) * plane] for d in range(MAJOR)]
    layer_out = dot_tn(normed_low, w_out).astype(BF16)
    query_term = lax.dot_general(
        query_grad, w_query, (((0,), (1,)), ((), ())), preferred_element_type=F32
    )
    last = spread(back[3][1:])
    far = spread(back[2][1:], last)
    beside = spread(back[1][1:], far)
    last_sum = swap(owner_sum(wanted[3], [back[3][0], *last], block_count), 1, 0)
    far_sum = owner_sum(wanted[2], [back[2][0], *far], block_count, last_sum)
    own = spread([after(x, far_sum) for x in back[0][1:]], beside)
    next_sum = owner_sum(wanted[1], [back[1][0], *beside], block_count)
    *own, query_term, layer_out = lax.optimization_barrier((*own, query_term, layer_out))
    own_sum = owner_sum(wanted[0], [back[0][0], *own], block_count)
    sums = [swap(far_sum, 2, 1), swap(next_sum, 1, 1), swap(own_sum, 0, 1)]
    input_grad = finish([x.reshape(rows, 2 * KV) for x in sums], query_term, w_key, w_value)
    return (layer_out[None], input_grad[None])


def solution(mesh):
    in_specs = (
        P("vintage", "tile", None),
        P("vintage", "tile", None),
        P(),
        P(),
        P(),
        P(),
        P("vintage", None, None),
        P("vintage", None, None),
    )
    out_specs = (P("vintage", "tile", None), P("vintage", "tile", None))
    return jax.shard_map(shards, mesh=mesh, in_specs=in_specs, out_specs=out_specs, check_vma=False)
```

```python
import functools

import jax
import jax.numpy as jnp
from jax import lax
from jax.experimental import pallas as pl
from jax.experimental.pallas import tpu as pltpu
from jax.sharding import PartitionSpec as P

HEADS = 12
KV_HEADS = 4
HEAD_DIM = 64
BLK = 128
CAP = 2
GROUP = HEADS // KV_HEADS
KV = KV_HEADS * HEAD_DIM
PAIR = 2 * HEAD_DIM
CODE = 16
FAR_FLOPS = 30_000_000_000
MAJOR = 4
TEMPER = HEAD_DIM ** (-0.5)
EPSILON = 1e-06
WHOLE = pl.BlockSpec(memory_space=pltpu.VMEM)
F32 = jnp.float32
BF16 = jnp.bfloat16


def params(mebibytes):
    return pltpu.CompilerParams(vmem_limit_bytes=mebibytes * 1024 * 1024)


def dot_nt(a, b):
    return lax.dot_general(a, b, (((1,), (1,)), ((), ())), preferred_element_type=F32)


def dot_tn(a, b):
    return lax.dot_general(a, b, (((0,), (0,)), ((), ())), preferred_element_type=F32)


def feature_heads(features, g):
    first = g * GROUP
    return jnp.concatenate(
        [features[(first + r) * HEAD_DIM : (first + r + 1) * HEAD_DIM] for r in range(GROUP)],
        axis=1,
    )


def two_groups(features, j):
    low, high = feature_heads(features, 2 * j), feature_heads(features, 2 * j + 1)
    zeros = jnp.zeros_like(low)
    return jnp.concatenate(
        [jnp.concatenate([low, zeros], axis=1), jnp.concatenate([zeros, high], axis=1)], axis=0
    )


def head_rows(pair_out):
    heads = []
    for i in range(2 * GROUP):
        top = i // GROUP * HEAD_DIM
        heads.append(pair_out[top : top + HEAD_DIM, i * BLK : (i + 1) * BLK])
    return jnp.concatenate(heads, axis=0)


def attention_kernel(list_len, per_step, get_ref, put_ref, q_ref, ng_ref, *refs):
    expo_scr, kv_scr, parts_scr, in_sems, out_sems = refs[-5:]
    sources = (len(refs) - 7) // 2
    arrived, (normed_ref, qg_ref) = refs[:sources], refs[sources : sources + 2]
    back = refs[sources + 2 : 2 * sources + 2]
    step = pl.program_id(0)
    entries = in_sems.shape[0]

    def rows_of(e):
        return pl.ds(pl.multiple_of(e * BLK, BLK), BLK)

    def fetch(e, source, slot):
        return pltpu.make_async_copy(
            arrived[source].at[slot], kv_scr.at[rows_of(e)], in_sems.at[e]
        )

    def give(e, source, slot):
        return pltpu.make_async_copy(
            parts_scr.at[rows_of(e)], back[source].at[slot], out_sems.at[e]
        )

    def start(copy, code_ref, begin, count):
        def one(i, carry):
            e = begin + i
            code = code_ref[e]
            for source in range(sources):

                @pl.when(code // CODE == source)
                def _():
                    copy(e, source, code % CODE).start()

            return carry

        lax.fori_loop(0, count, one, 0)

    @pl.when(step == 0)
    def _():
        start(fetch, get_ref, 0, entries)

    first = step * per_step * list_len
    for i in range(per_step * list_len):
        fetch(first + i, 0, 0).wait()
    pairs = range(KV // PAIR)
    keys, values, wide, scores, exact, scales, grads, overlap, prob_grads = (
        {} for _ in range(9)
    )

    def rows_at(b):
        size = list_len * BLK
        return pl.ds(pl.multiple_of((step * per_step + b) * size, size), size)

    def cols_at(b):
        return slice(b * BLK, (b + 1) * BLK)

    def score(b):
        here = rows_at(b)
        queries = q_ref[:, cols_at(b)] * jnp.asarray(TEMPER, BF16)
        for j in pairs:
            keys[b, j] = kv_scr[here, j * PAIR : (j + 1) * PAIR]
            values[b, j] = kv_scr[here, KV + j * PAIR : KV + (j + 1) * PAIR]
            wide[b, j] = two_groups(queries, j)
            scores[b, j] = jnp.dot(keys[b, j], wide[b, j], preferred_element_type=F32)

    def soften(b, j):
        expo = jnp.exp(scores[b, j] - jnp.max(scores[b, j], axis=0, keepdims=True))
        scale = 1.0 / jnp.sum(expo, axis=0, keepdims=True)
        expo_scr[b, j] = expo.astype(BF16)
        exact[b, j] = head_rows(dot_tn(values[b, j], expo_scr[b, j]) * scale)
        scales[b, j] = jnp.concatenate(
            [
                jnp.broadcast_to(scale[:, i * BLK : (i + 1) * BLK], (HEAD_DIM, BLK))
                for i in range(2 * GROUP)
            ],
            axis=0,
        )

    def normalise(b):
        whole = jnp.concatenate([exact[b, j] for j in pairs], axis=0)
        attended = whole.astype(BF16).astype(F32)
        width = attended.shape[0]
        square = jnp.sum(attended * attended, axis=0, keepdims=True) / width
        inverse = lax.rsqrt(square + EPSILON)
        normed = attended * inverse
        normed_ref[:, cols_at(b)] = normed.astype(BF16)
        normed_grad = ng_ref[:, cols_at(b)]
        shared = jnp.sum(normed_grad * normed, axis=0, keepdims=True) / width
        attended_grad = (normed_grad - normed * shared) * inverse
        scale = jnp.concatenate([scales[b, j] for j in pairs], axis=0)
        scaled_grad = (attended_grad * scale).astype(BF16)
        overlap[b] = scaled_grad.astype(F32) * whole
        for j in pairs:
            grads[b, j] = two_groups(scaled_grad, j)

    def regrade(b, j):
        prob_grads[b, j] = jnp.dot(values[b, j], grads[b, j], preferred_element_type=F32)

    def finish_pair(b, j):
        here = rows_at(b)
        heads = range(2 * GROUP * j, 2 * GROUP * (j + 1))
        row_dot = jnp.concatenate(
            [
                jnp.sum(overlap[b][h * HEAD_DIM : (h + 1) * HEAD_DIM], axis=0, keepdims=True)
                for h in heads
            ],
            axis=1,
        )
        expo = expo_scr[b, j]
        value_part = dot_nt(expo, grads[b, j])
        score_grad = (expo.astype(F32) * (prob_grads[b, j] - row_dot)).astype(BF16)
        query_grad = head_rows(dot_tn(keys[b, j], score_grad) * TEMPER).astype(BF16)
        qg_ref[heads.start * HEAD_DIM : heads.stop * HEAD_DIM, cols_at(b)] = query_grad
        key_part = dot_nt(score_grad, wide[b, j])
        parts_scr[here, j * PAIR : (j + 1) * PAIR] = key_part.astype(BF16)
        parts_scr[here, KV + j * PAIR : KV + (j + 1) * PAIR] = value_part.astype(BF16)

    for b in range(per_step):
        score(b)
    for j in pairs:
        soften(0, j)
    normalise(0)
    for b in range(per_step):
        for j in pairs:
            regrade(b, j)
            if b + 1 < per_step:
                soften(b + 1, j)
        for j in pairs:
            finish_pair(b, j)
            if b + 1 < per_step and j == 0:
                normalise(b + 1)
    start(give, put_ref, first, per_step * list_len)

    @pl.when(step == pl.num_programs(0) - 1)
    def _():
        for e in range(entries):
            give(e, 0, 0).wait()


def attention(gets, puts, queries, normed_grad, arrived, list_len):
    width, rows = queries.shape
    slot_shape = (CAP,) + arrived[0].shape[1:]
    blocks = rows // BLK
    entries = blocks * list_len
    per_step = 2 if list_len <= 4 and blocks % 2 == 0 else 1
    row_spec = pl.BlockSpec((width, per_step * BLK), lambda r, g, p: (0, r))
    anywhere = pl.BlockSpec(memory_space=pl.ANY)
    keys = list_len * BLK
    pairs = HEADS * rows * keys
    return pl.pallas_call(
        functools.partial(attention_kernel, list_len, per_step),
        grid_spec=pltpu.PrefetchScalarGridSpec(
            num_scalar_prefetch=2,
            grid=(blocks // per_step,),
            in_specs=[row_spec, row_spec] + [anywhere] * len(arrived),
            out_specs=[row_spec, row_spec] + [anywhere] * len(arrived),
            scratch_shapes=[
                pltpu.VMEM((per_step, KV // PAIR, keys, 2 * GROUP * BLK), BF16),
                pltpu.VMEM((entries * BLK, 2 * KV), BF16),
                pltpu.VMEM((entries * BLK, 2 * KV), BF16),
                pltpu.SemaphoreType.DMA((entries,)),
                pltpu.SemaphoreType.DMA((entries,)),
            ],
        ),
        out_shape=[jax.ShapeDtypeStruct((width, rows), BF16)] * 2
        + [jax.ShapeDtypeStruct(slot_shape, BF16)] * len(arrived),
        compiler_params=params(56),
        cost_estimate=pl.CostEstimate(
            flops=12 * pairs * HEAD_DIM, bytes_accessed=16 * rows * width, transcendentals=pairs
        ),
        name="attention",
    )(gets, puts, queries, normed_grad, *arrived)


def project_kernel(tokens_hbm, wk_hbm, wv_hbm, out_ref, tokens, wk, wv, sems):
    moves = ((wk_hbm, wk), (tokens_hbm, tokens), (wv_hbm, wv))
    copies = [pltpu.make_async_copy(src, dst, sems.at[i]) for i, (src, dst) in enumerate(moves)]
    for copy in copies:
        copy.start()
    copies[0].wait()
    copies[1].wait()
    keys = jnp.dot(tokens[...], wk[...], preferred_element_type=F32)
    out_ref[:, :KV] = keys.astype(BF16)
    copies[2].wait()
    values = jnp.dot(tokens[...], wv[...], preferred_element_type=F32)
    out_ref[:, KV:] = values.astype(BF16)


def project(tokens, w_key, w_value):
    args = (tokens, w_key, w_value)
    return pl.pallas_call(
        project_kernel,
        in_specs=[pl.BlockSpec(memory_space=pl.ANY)] * 3,
        out_specs=WHOLE,
        out_shape=jax.ShapeDtypeStruct((tokens.shape[0], 2 * KV), BF16),
        scratch_shapes=[pltpu.VMEM(x.shape, BF16) for x in args]
        + [pltpu.SemaphoreType.DMA((3,))],
        compiler_params=params(56),
        name="project",
    )(*args)


def pack_kernel(picked_ref, tile_ref, *outs):
    for i, out in enumerate(outs):
        for s in range(CAP):
            out[s] = tile_ref[picked_ref[i * CAP + s]]


def pack(picked, tile):
    peers = picked.shape[0] // CAP
    shape = (CAP,) + tile.shape[1:]
    return pl.pallas_call(
        pack_kernel,
        in_specs=[pl.BlockSpec(memory_space=pltpu.SMEM), WHOLE],
        out_specs=[WHOLE] * peers,
        out_shape=[jax.ShapeDtypeStruct(shape, BF16)] * peers,
        compiler_params=params(16),
        name="pack",
    )(picked, tile)


def finish_kernel(parts, *refs):
    term_ref, wk_ref, wv_ref, out_ref = refs[parts:]
    grad = refs[0][...].astype(F32)
    for ref in refs[1:parts]:
        grad += ref[...].astype(F32)
    grad = grad.astype(BF16)
    total = dot_nt(grad[:, :KV], wk_ref[...]) + dot_nt(grad[:, KV:], wv_ref[...])
    out_ref[...] = (term_ref[...] + total).astype(out_ref.dtype)


def finish(parts, term, w_key, w_value, kind, flops):
    return pl.pallas_call(
        functools.partial(finish_kernel, len(parts)),
        in_specs=[WHOLE] * (len(parts) + 3),
        out_specs=WHOLE,
        out_shape=jax.ShapeDtypeStruct(term.shape, kind),
        compiler_params=params(24),
        cost_estimate=pl.CostEstimate(
            flops=flops, bytes_accessed=4 * term.size, transcendentals=0
        ),
        name="finish",
    )(*parts, term, w_key, w_value)


def owner_kernel(peers, wanted_ref, *refs):
    parts, extra, (out_ref, total) = refs[:peers], refs[peers:-2], refs[-2:]
    total[...] = extra[0][...].astype(F32) if extra else jnp.zeros_like(total)
    for p, part in enumerate(parts):
        for s in range(CAP):
            block = wanted_ref[p * CAP + s]

            @pl.when(block >= 0)
            def _():
                total[block] += part[s].astype(F32)

    out_ref[...] = total[...].astype(BF16)


def owner_sum(wanted, parts, blocks, *extra):
    shape = (blocks,) + parts[0].shape[1:]
    args = (*parts, *extra)
    return pl.pallas_call(
        functools.partial(owner_kernel, len(parts)),
        in_specs=[pl.BlockSpec(memory_space=pltpu.SMEM)] + [WHOLE] * len(args),
        out_specs=WHOLE,
        out_shape=jax.ShapeDtypeStruct(shape, BF16),
        scratch_shapes=[pltpu.VMEM(shape, F32)],
        compiler_params=params(16),
        name="owner_sum",
    )(wanted, *args)


def shards(patches, out_grad, w_query, w_key, w_value, w_out, key_tiles, key_blocks):
    tokens = patches[0]
    rows = tokens.shape[0]
    tile_count = lax.axis_size("tile")
    plane = tile_count // MAJOR
    my_tile = lax.axis_index("tile")
    my_row, my_place = my_tile // plane, my_tile % plane
    block_count = rows // BLK
    list_len = key_tiles.shape[2]
    entry_count = block_count * list_len

    def swap(value, d, cross):
        pairs = [
            (v * tile_count + t, (v ^ cross) * tile_count + (t // plane ^ d) * plane + t % plane)
            for v in range(2)
            for t in range(tile_count)
        ]
        return lax.ppermute(value, ("vintage", "tile"), pairs)

    def after(value, earlier):
        return lax.optimization_barrier((value, earlier))[0]

    def spread(values, earlier=None):
        moved = []
        for i, value in enumerate(values):
            pairs = [(t, t // plane * plane + (t % plane ^ (i + 1))) for t in range(tile_count)]
            if earlier is not None:
                value = after(value, earlier[i])
            moved.append(lax.ppermute(value, "tile", pairs))
        return moved

    def plane_rows(table):
        table = table[0].reshape(MAJOR, plane, entry_count)
        return lax.dynamic_index_in_dim(table, my_row, 0, keepdims=False)

    def mine_of(table):
        return lax.dynamic_index_in_dim(table, my_place, 0, keepdims=False)

    tiles, picks = plane_rows(key_tiles), plane_rows(key_blocks)
    earlier = jnp.arange(entry_count)[:, None] > jnp.arange(entry_count)[None, :]
    same = (tiles[:, :, None] == tiles[:, None, :]) & earlier[None]
    ranks = jnp.sum(same.astype(jnp.int32), axis=2)
    groups, columns = (tiles // plane) ^ my_row, tiles % plane
    my_source = mine_of(groups) * plane + (mine_of(columns) ^ my_place)
    puts = my_source * CODE + mine_of(ranks)
    gets = jnp.where(my_source % plane == 0, my_source * CODE + mine_of(picks), puts)
    ids = jnp.arange(MAJOR * CAP, dtype=jnp.int32)
    slots = groups * CAP + ranks
    hits = (slots[:, None, :] == ids[None, :, None]) & (columns == my_place)[:, None, :]
    wanted = jnp.sum(jnp.where(hits, picks[:, None, :] + 1, 0), axis=2) - 1
    wanted = wanted[jnp.arange(plane) ^ my_place].reshape(plane, MAJOR, CAP)
    wanted = wanted.transpose(1, 0, 2).reshape(MAJOR, plane * CAP)
    picked = jnp.maximum(wanted[:, CAP:], 0)

    mine = project(tokens, w_key, w_value).reshape(block_count, BLK, 2 * KV)
    next_tile = swap(mine, 1, 1)
    own_tile = swap(mine, 0, 1)
    far_tile = swap(after(mine, own_tile), 2, 1)
    own = spread(pack(picked[0], own_tile))
    beside = spread(pack(picked[1], next_tile), own)
    last_tile = swap(after(far_tile, own[-1]), 1, 0)
    far = spread(pack(picked[2], after(far_tile, own[-1])), beside)
    last = spread(pack(picked[3], last_tile), far)
    arrived = [own_tile, *own, next_tile, *beside, far_tile, *far, last_tile, *last]
    queries = lax.dot_general(
        w_query, tokens, (((0,), (1,)), ((), ())), preferred_element_type=F32
    ).astype(BF16)
    normed_grad = dot_nt(w_out, out_grad[0])
    normed_low, query_grad, *back = attention(
        gets, puts, queries, normed_grad, arrived, list_len
    )
    back = [back[d * plane : (d + 1) * plane] for d in range(MAJOR)]
    layer_out = dot_tn(normed_low, w_out).astype(BF16)
    query_term = lax.dot_general(
        query_grad, w_query, (((0,), (1,)), ((), ())), preferred_element_type=F32
    )
    last = spread(back[3][1:])
    far = spread(back[2][1:])
    beside = spread(back[1][1:], far)
    last_sum = swap(owner_sum(wanted[3], [back[3][0], *last], block_count), 1, 0)
    far_sum = owner_sum(wanted[2], [back[2][0], *far], block_count, last_sum)
    own = spread([after(x, far_sum) for x in back[0][1:]], beside)
    next_sum = owner_sum(wanted[1], [back[1][0], *beside], block_count)
    *own, query_term, layer_out = lax.optimization_barrier((*own, query_term, layer_out))
    own_sum = owner_sum(wanted[0], [back[0][0], *own], block_count)
    far_grad = swap(far_sum, 2, 1).reshape(rows, 2 * KV)
    near_grads = [x.reshape(rows, 2 * KV) for x in (swap(next_sum, 1, 1), swap(own_sum, 0, 1))]
    query_term = finish([far_grad], query_term, w_key, w_value, F32, FAR_FLOPS)
    input_grad = finish(near_grads, query_term, w_key, w_value, BF16, 800_000_000)
    return (layer_out[None], input_grad[None])


def solution(mesh):
    in_specs = (
        P("vintage", "tile", None),
        P("vintage", "tile", None),
        P(),
        P(),
        P(),
        P(),
        P("vintage", None, None),
        P("vintage", None, None),
    )
    out_specs = (P("vintage", "tile", None), P("vintage", "tile", None))
    return jax.shard_map(shards, mesh=mesh, in_specs=in_specs, out_specs=out_specs, check_vma=False)
```

```python
import functools

import jax
import jax.numpy as jnp
from jax import lax
from jax.experimental import pallas as pl
from jax.experimental.pallas import tpu as pltpu
from jax.sharding import PartitionSpec as P

HEADS = 12
KV_HEADS = 4
HEAD_DIM = 64
BLK = 128
CAP = 2
GROUP = HEADS // KV_HEADS
KV = KV_HEADS * HEAD_DIM
PAIR = 2 * HEAD_DIM
CODE = 16
FAR_SUM_FLOPS = 8_000_000_000
FAR_FLOPS = 30_000_000_000
MAJOR = 4
TEMPER = HEAD_DIM ** (-0.5)
EPSILON = 1e-06
WHOLE = pl.BlockSpec(memory_space=pltpu.VMEM)
F32 = jnp.float32
BF16 = jnp.bfloat16


def params(mebibytes):
    return pltpu.CompilerParams(vmem_limit_bytes=mebibytes * 1024 * 1024)


def dot_nt(a, b):
    return lax.dot_general(a, b, (((1,), (1,)), ((), ())), preferred_element_type=F32)


def dot_tn(a, b):
    return lax.dot_general(a, b, (((0,), (0,)), ((), ())), preferred_element_type=F32)


def feature_heads(features, g):
    first = g * GROUP
    return jnp.concatenate(
        [features[(first + r) * HEAD_DIM : (first + r + 1) * HEAD_DIM] for r in range(GROUP)],
        axis=1,
    )


def two_groups(features, j):
    low, high = feature_heads(features, 2 * j), feature_heads(features, 2 * j + 1)
    zeros = jnp.zeros_like(low)
    return jnp.concatenate(
        [jnp.concatenate([low, zeros], axis=1), jnp.concatenate([zeros, high], axis=1)], axis=0
    )


def head_rows(pair_out):
    heads = []
    for i in range(2 * GROUP):
        top = i // GROUP * HEAD_DIM
        heads.append(pair_out[top : top + HEAD_DIM, i * BLK : (i + 1) * BLK])
    return jnp.concatenate(heads, axis=0)


def attention_kernel(list_len, per_step, get_ref, put_ref, q_ref, ng_ref, *refs):
    expo_scr, kv_scr, parts_scr, in_sems, out_sems = refs[-5:]
    sources = (len(refs) - 7) // 2
    arrived, (normed_ref, qg_ref) = refs[:sources], refs[sources : sources + 2]
    back = refs[sources + 2 : 2 * sources + 2]
    step = pl.program_id(0)
    entries = in_sems.shape[0]

    def rows_of(e):
        return pl.ds(pl.multiple_of(e * BLK, BLK), BLK)

    def fetch(e, source, slot):
        return pltpu.make_async_copy(
            arrived[source].at[slot], kv_scr.at[rows_of(e)], in_sems.at[e]
        )

    def give(e, source, slot):
        return pltpu.make_async_copy(
            parts_scr.at[rows_of(e)], back[source].at[slot], out_sems.at[e]
        )

    def start(copy, code_ref, begin, count):
        def one(i, carry):
            e = begin + i
            code = code_ref[e]
            for source in range(sources):

                @pl.when(code // CODE == source)
                def _():
                    copy(e, source, code % CODE).start()

            return carry

        lax.fori_loop(0, count, one, 0)

    @pl.when(step == 0)
    def _():
        start(fetch, get_ref, 0, entries)

    first = step * per_step * list_len
    for i in range(per_step * list_len):
        fetch(first + i, 0, 0).wait()
    pairs = range(KV // PAIR)
    keys, values, wide, scores, exact, scales, grads, overlap, prob_grads = (
        {} for _ in range(9)
    )

    def rows_at(b):
        size = list_len * BLK
        return pl.ds(pl.multiple_of((step * per_step + b) * size, size), size)

    def cols_at(b):
        return slice(b * BLK, (b + 1) * BLK)

    def score(b):
        here = rows_at(b)
        queries = q_ref[:, cols_at(b)] * jnp.asarray(TEMPER, BF16)
        for j in pairs:
            keys[b, j] = kv_scr[here, j * PAIR : (j + 1) * PAIR]
            values[b, j] = kv_scr[here, KV + j * PAIR : KV + (j + 1) * PAIR]
            wide[b, j] = two_groups(queries, j)
            scores[b, j] = jnp.dot(keys[b, j], wide[b, j], preferred_element_type=F32)

    def soften(b, j):
        expo = jnp.exp(scores[b, j] - jnp.max(scores[b, j], axis=0, keepdims=True))
        scale = 1.0 / jnp.sum(expo, axis=0, keepdims=True)
        expo_scr[b, j] = expo.astype(BF16)
        exact[b, j] = head_rows(dot_tn(values[b, j], expo_scr[b, j]) * scale)
        scales[b, j] = jnp.concatenate(
            [
                jnp.broadcast_to(scale[:, i * BLK : (i + 1) * BLK], (HEAD_DIM, BLK))
                for i in range(2 * GROUP)
            ],
            axis=0,
        )

    def normalise(b):
        whole = jnp.concatenate([exact[b, j] for j in pairs], axis=0)
        attended = whole.astype(BF16).astype(F32)
        width = attended.shape[0]
        square = jnp.sum(attended * attended, axis=0, keepdims=True) / width
        inverse = lax.rsqrt(square + EPSILON)
        normed = attended * inverse
        normed_ref[:, cols_at(b)] = normed.astype(BF16)
        normed_grad = ng_ref[:, cols_at(b)]
        shared = jnp.sum(normed_grad * normed, axis=0, keepdims=True) / width
        attended_grad = (normed_grad - normed * shared) * inverse
        scale = jnp.concatenate([scales[b, j] for j in pairs], axis=0)
        scaled_grad = (attended_grad * scale).astype(BF16)
        overlap[b] = scaled_grad.astype(F32) * whole
        for j in pairs:
            grads[b, j] = two_groups(scaled_grad, j)

    def regrade(b, j):
        prob_grads[b, j] = jnp.dot(values[b, j], grads[b, j], preferred_element_type=F32)

    def finish_pair(b, j):
        here = rows_at(b)
        heads = range(2 * GROUP * j, 2 * GROUP * (j + 1))
        row_dot = jnp.concatenate(
            [
                jnp.sum(overlap[b][h * HEAD_DIM : (h + 1) * HEAD_DIM], axis=0, keepdims=True)
                for h in heads
            ],
            axis=1,
        )
        expo = expo_scr[b, j]
        value_part = dot_nt(expo, grads[b, j])
        score_grad = (expo.astype(F32) * (prob_grads[b, j] - row_dot)).astype(BF16)
        query_grad = head_rows(dot_tn(keys[b, j], score_grad) * TEMPER).astype(BF16)
        qg_ref[heads.start * HEAD_DIM : heads.stop * HEAD_DIM, cols_at(b)] = query_grad
        key_part = dot_nt(score_grad, wide[b, j])
        parts_scr[here, j * PAIR : (j + 1) * PAIR] = key_part.astype(BF16)
        parts_scr[here, KV + j * PAIR : KV + (j + 1) * PAIR] = value_part.astype(BF16)

    for b in range(per_step):
        score(b)
    for j in pairs:
        soften(0, j)
    normalise(0)
    for b in range(per_step):
        for j in pairs:
            regrade(b, j)
            if b + 1 < per_step:
                soften(b + 1, j)
        for j in pairs:
            finish_pair(b, j)
            if b + 1 < per_step and j == 0:
                normalise(b + 1)
    start(give, put_ref, first, per_step * list_len)

    @pl.when(step == pl.num_programs(0) - 1)
    def _():
        for e in range(entries):
            give(e, 0, 0).wait()


def attention(gets, puts, queries, normed_grad, arrived, list_len):
    width, rows = queries.shape
    slot_shape = (CAP,) + arrived[0].shape[1:]
    blocks = rows // BLK
    entries = blocks * list_len
    per_step = 2 if list_len <= 4 and blocks % 2 == 0 else 1
    row_spec = pl.BlockSpec((width, per_step * BLK), lambda r, g, p: (0, r))
    anywhere = pl.BlockSpec(memory_space=pl.ANY)
    keys = list_len * BLK
    pairs = HEADS * rows * keys
    return pl.pallas_call(
        functools.partial(attention_kernel, list_len, per_step),
        grid_spec=pltpu.PrefetchScalarGridSpec(
            num_scalar_prefetch=2,
            grid=(blocks // per_step,),
            in_specs=[row_spec, row_spec] + [anywhere] * len(arrived),
            out_specs=[row_spec, row_spec] + [anywhere] * len(arrived),
            scratch_shapes=[
                pltpu.VMEM((per_step, KV // PAIR, keys, 2 * GROUP * BLK), BF16),
                pltpu.VMEM((entries * BLK, 2 * KV), BF16),
                pltpu.VMEM((entries * BLK, 2 * KV), BF16),
                pltpu.SemaphoreType.DMA((entries,)),
                pltpu.SemaphoreType.DMA((entries,)),
            ],
        ),
        out_shape=[jax.ShapeDtypeStruct((width, rows), BF16)] * 2
        + [jax.ShapeDtypeStruct(slot_shape, BF16)] * len(arrived),
        compiler_params=params(56),
        cost_estimate=pl.CostEstimate(
            flops=12 * pairs * HEAD_DIM, bytes_accessed=16 * rows * width, transcendentals=pairs
        ),
        name="attention",
    )(gets, puts, queries, normed_grad, *arrived)


def plan(plane, list_len, my_tile, tiles, picks, gets, puts, wanted, counts):
    entries = gets.shape[0]
    block_count = entries // list_len
    my_row, my_place = lax.div(my_tile, plane), lax.rem(my_tile, plane)
    spare = MAJOR * plane * CAP

    def clear(i, carry):
        wanted[i] = -1
        return carry

    lax.fori_loop(0, spare + 1, clear, 0)

    def one_asker(p, carry):
        asker = my_row * plane + (my_place ^ p)

        def zero(t, carry):
            counts[t] = 0
            return carry

        lax.fori_loop(0, counts.shape[0], zero, 0)
        for e in range(entries):
            row = asker * block_count + e // list_len
            tile, pick = tiles[0, row, e % list_len], picks[0, row, e % list_len]
            rank = counts[tile]
            counts[tile] = rank + 1
            group, column = lax.div(tile, plane) ^ my_row, lax.rem(tile, plane)
            mine = column == my_place
            wanted[jnp.where(mine, (group * plane + p) * CAP + rank, spare)] = pick

            @pl.when(p == 0)
            def _():
                code = (group * plane + (column ^ my_place)) * CODE
                puts[e] = code + rank
                gets[e] = code + jnp.where(mine, pick, rank)

        return carry

    lax.fori_loop(0, plane, one_asker, 0)


def project_kernel(
    plane, list_len, my_tile, tiles, picks, tokens_hbm, wk_hbm, wv_hbm,
    out_ref, gets, puts, wanted, tokens, wk, wv, counts, sems,
):
    copies = []
    for src, dst, pieces in ((wk_hbm, wk, 2), (tokens_hbm, tokens, 4), (wv_hbm, wv, 2)):
        size = src.shape[0] // pieces
        for i in range(pieces):
            part = pl.ds(i * size, size)
            copies.append(
                pltpu.make_async_copy(src.at[part], dst.at[part], sems.at[len(copies)])
            )
    for copy in copies:
        copy.start()
    plan(plane, list_len, my_tile[0], tiles, picks, gets, puts, wanted, counts)
    for copy in copies[:6]:
        copy.wait()
    keys = jnp.dot(tokens[...], wk[...], preferred_element_type=F32)
    out_ref[:, :KV] = keys.astype(BF16)
    for copy in copies[6:]:
        copy.wait()
    values = jnp.dot(tokens[...], wv[...], preferred_element_type=F32)
    out_ref[:, KV:] = values.astype(BF16)


def project(plane, my_tile, key_tiles, key_blocks, tokens, w_key, w_value):
    list_len = key_tiles.shape[2]
    rows = tokens.shape[0]
    entries = rows // BLK * list_len
    smem = pl.BlockSpec(memory_space=pltpu.SMEM)
    args = (tokens, w_key, w_value)
    slots = MAJOR * plane * CAP + 1
    return pl.pallas_call(
        functools.partial(project_kernel, plane, list_len),
        in_specs=[smem] * 3 + [pl.BlockSpec(memory_space=pl.ANY)] * 3,
        out_specs=[WHOLE] + [smem] * 3,
        out_shape=[jax.ShapeDtypeStruct((rows, 2 * KV), BF16)]
        + [jax.ShapeDtypeStruct((n,), jnp.int32) for n in (entries, entries, slots)],
        scratch_shapes=[pltpu.VMEM(x.shape, BF16) for x in args]
        + [pltpu.SMEM((MAJOR * plane,), jnp.int32), pltpu.SemaphoreType.DMA((8,))],
        compiler_params=params(56),
        name="project",
    )(my_tile.reshape(1), key_tiles, key_blocks, *args)


def pack_kernel(first, wanted_ref, tile_ref, *outs):
    for i, out in enumerate(outs):
        for s in range(CAP):
            out[s] = tile_ref[jnp.maximum(wanted_ref[first + (i + 1) * CAP + s], 0)]


def pack(group, plane, wanted, tile):
    shape = (CAP,) + tile.shape[1:]
    return pl.pallas_call(
        functools.partial(pack_kernel, group * plane * CAP),
        in_specs=[pl.BlockSpec(memory_space=pltpu.SMEM), WHOLE],
        out_specs=[WHOLE] * (plane - 1),
        out_shape=[jax.ShapeDtypeStruct(shape, BF16)] * (plane - 1),
        compiler_params=params(16),
        name="pack",
    )(wanted, tile)


def finish_kernel(parts, *refs):
    term_ref, wk_ref, wv_ref, out_ref = refs[parts:]
    grad = refs[0][...].astype(F32)
    for ref in refs[1:parts]:
        grad += ref[...].astype(F32)
    grad = grad.astype(BF16)
    total = dot_nt(grad[:, :KV], wk_ref[...]) + dot_nt(grad[:, KV:], wv_ref[...])
    out_ref[...] = (term_ref[...] + total).astype(out_ref.dtype)


def finish(parts, term, w_key, w_value, kind, flops):
    return pl.pallas_call(
        functools.partial(finish_kernel, len(parts)),
        in_specs=[WHOLE] * (len(parts) + 3),
        out_specs=WHOLE,
        out_shape=jax.ShapeDtypeStruct(term.shape, kind),
        compiler_params=params(24),
        cost_estimate=pl.CostEstimate(
            flops=flops, bytes_accessed=4 * term.size, transcendentals=0
        ),
        name="finish",
    )(*parts, term, w_key, w_value)


def owner_kernel(first, wanted_ref, *refs):
    parts, (out_ref, total) = refs[:-2], refs[-2:]
    total[...] = jnp.zeros_like(total)
    for p, part in enumerate(parts):
        for s in range(CAP):
            block = wanted_ref[first + p * CAP + s]

            @pl.when(block >= 0)
            def _():
                total[block] += part[s].astype(F32)

    out_ref[...] = total[...].astype(out_ref.dtype)


def owner_sum(group, wanted, parts, blocks, kind, flops):
    shape = (blocks,) + parts[0].shape[1:]
    return pl.pallas_call(
        functools.partial(owner_kernel, group * len(parts) * CAP),
        in_specs=[pl.BlockSpec(memory_space=pltpu.SMEM)] + [WHOLE] * len(parts),
        out_specs=WHOLE,
        out_shape=jax.ShapeDtypeStruct(shape, kind),
        scratch_shapes=[pltpu.VMEM(shape, F32)],
        compiler_params=params(16),
        cost_estimate=pl.CostEstimate(
            flops=flops, bytes_accessed=4 * parts[0].size, transcendentals=0
        ),
        name="owner_sum",
    )(wanted, *parts)


def shards(patches, out_grad, w_query, w_key, w_value, w_out, key_tiles, key_blocks):
    tokens = patches[0]
    rows = tokens.shape[0]
    tile_count = lax.axis_size("tile")
    plane = tile_count // MAJOR
    my_tile = lax.axis_index("tile")
    block_count = rows // BLK
    list_len = key_tiles.shape[2]

    def swap(value, d, cross):
        pairs = [
            (v * tile_count + t, (v ^ cross) * tile_count + (t // plane ^ d) * plane + t % plane)
            for v in range(2)
            for t in range(tile_count)
        ]
        return lax.ppermute(value, ("vintage", "tile"), pairs)

    def after(value, earlier):
        return lax.optimization_barrier((value, earlier))[0]

    def spread(values, earlier=None):
        moved = []
        for i, value in enumerate(values):
            pairs = [(t, t // plane * plane + (t % plane ^ (i + 1))) for t in range(tile_count)]
            if earlier is not None:
                value = after(value, earlier[i])
            moved.append(lax.ppermute(value, "tile", pairs))
        return moved

    mine, gets, puts, wanted = project(
        plane, my_tile, key_tiles, key_blocks, tokens, w_key, w_value
    )
    mine = mine.reshape(block_count, BLK, 2 * KV)
    next_tile = swap(mine, 1, 1)
    own_tile = swap(mine, 0, 1)
    far_tile = swap(after(mine, own_tile), 2, 1)
    own = spread(pack(0, plane, wanted, own_tile))
    beside = spread(pack(1, plane, wanted, next_tile), own)
    last_tile = swap(after(far_tile, own[-1]), 1, 0)
    far = spread(pack(2, plane, wanted, after(far_tile, own[-1])), beside)
    last = spread(pack(3, plane, wanted, last_tile), far)
    arrived = [own_tile, *own, next_tile, *beside, far_tile, *far, last_tile, *last]
    queries = lax.dot_general(
        w_query, tokens, (((0,), (1,)), ((), ())), preferred_element_type=F32
    ).astype(BF16)
    normed_grad = dot_nt(w_out, out_grad[0])
    normed_low, query_grad, *back = attention(
        gets, puts, queries, normed_grad, arrived, list_len
    )
    back = [back[d * plane : (d + 1) * plane] for d in range(MAJOR)]
    layer_out = dot_tn(normed_low, w_out).astype(BF16)
    query_term = lax.dot_general(
        query_grad, w_query, (((0,), (1,)), ((), ())), preferred_element_type=F32
    )
    last = spread(back[3][1:])
    last[0], query_term, layer_out = lax.optimization_barrier((last[0], query_term, layer_out))
    far = spread(back[2][1:], last)
    beside = spread(back[1][1:], far)
    last_sum = owner_sum(3, wanted, [back[3][0], *last], block_count, BF16, 0)
    last_sum = swap(last_sum, 1, 0).astype(F32)
    far_sum = owner_sum(2, wanted, [back[2][0], *far], block_count, F32, FAR_SUM_FLOPS)
    far_sum = (far_sum + last_sum).astype(BF16)
    next_sum = owner_sum(1, wanted, [back[1][0], *beside], block_count, BF16, 0)
    own = spread([after(after(x, far_sum), next_sum) for x in back[0][1:]], beside)
    own_sum = owner_sum(0, wanted, [back[0][0], *own], block_count, BF16, 0)
    far_grad = swap(far_sum, 2, 1).reshape(rows, 2 * KV)
    near_grads = [x.reshape(rows, 2 * KV) for x in (swap(next_sum, 1, 1), swap(own_sum, 0, 1))]
    query_term = finish([far_grad], query_term, w_key, w_value, F32, FAR_FLOPS)
    input_grad = finish(near_grads, query_term, w_key, w_value, BF16, 800_000_000)
    return (layer_out[None], input_grad[None])


def solution(mesh):
    in_specs = (
        P("vintage", "tile", None),
        P("vintage", "tile", None),
        P(),
        P(),
        P(),
        P(),
        P("vintage", None, None),
        P("vintage", None, None),
    )
    out_specs = (P("vintage", "tile", None), P("vintage", "tile", None))
    return jax.shard_map(shards, mesh=mesh, in_specs=in_specs, out_specs=out_specs, check_vma=False)
```

```python
import functools

import jax
import jax.numpy as jnp
from jax import lax
from jax.experimental import pallas as pl
from jax.experimental.pallas import tpu as pltpu
from jax.sharding import PartitionSpec as P

HEADS = 12
KV_HEADS = 4
HEAD_DIM = 64
BLK = 128
CAP = 2
GROUP = HEADS // KV_HEADS
KV = KV_HEADS * HEAD_DIM
PAIR = 2 * HEAD_DIM
CODE = 16
NEXT_FLOPS = 10_000_000_000
FAR_SUM_FLOPS = 5_000_000_000
FAR_FLOPS = 20_000_000_000
MAJOR = 4
TEMPER = HEAD_DIM ** (-0.5)
EPSILON = 1e-06
WHOLE = pl.BlockSpec(memory_space=pltpu.VMEM)
F32 = jnp.float32
BF16 = jnp.bfloat16


def params(mebibytes):
    return pltpu.CompilerParams(vmem_limit_bytes=mebibytes * 1024 * 1024)


def dot_nt(a, b):
    return lax.dot_general(a, b, (((1,), (1,)), ((), ())), preferred_element_type=F32)


def dot_tn(a, b):
    return lax.dot_general(a, b, (((0,), (0,)), ((), ())), preferred_element_type=F32)


def feature_heads(features, g):
    first = g * GROUP
    return jnp.concatenate(
        [features[(first + r) * HEAD_DIM : (first + r + 1) * HEAD_DIM] for r in range(GROUP)],
        axis=1,
    )


def two_groups(features, j):
    low, high = feature_heads(features, 2 * j), feature_heads(features, 2 * j + 1)
    zeros = jnp.zeros_like(low)
    return jnp.concatenate(
        [jnp.concatenate([low, zeros], axis=1), jnp.concatenate([zeros, high], axis=1)], axis=0
    )


def head_rows(pair_out):
    heads = []
    for i in range(2 * GROUP):
        top = i // GROUP * HEAD_DIM
        heads.append(pair_out[top : top + HEAD_DIM, i * BLK : (i + 1) * BLK])
    return jnp.concatenate(heads, axis=0)


def attention_kernel(list_len, per_step, get_ref, put_ref, q_ref, ng_ref, *refs):
    expo_scr, kv_scr, parts_scr, in_sems, out_sems = refs[-5:]
    sources = (len(refs) - 7) // 2
    arrived, (normed_ref, qg_ref) = refs[:sources], refs[sources : sources + 2]
    back = refs[sources + 2 : 2 * sources + 2]
    step = pl.program_id(0)
    entries = in_sems.shape[0]

    def rows_of(e):
        return pl.ds(pl.multiple_of(e * BLK, BLK), BLK)

    def fetch(e, source, slot):
        return pltpu.make_async_copy(
            arrived[source].at[slot], kv_scr.at[rows_of(e)], in_sems.at[e]
        )

    def give(e, source, slot):
        return pltpu.make_async_copy(
            parts_scr.at[rows_of(e)], back[source].at[slot], out_sems.at[e]
        )

    def start(copy, code_ref, begin, count):
        def one(i, carry):
            e = begin + i
            code = code_ref[e]
            for source in range(sources):

                @pl.when(code // CODE == source)
                def _():
                    copy(e, source, code % CODE).start()

            return carry

        lax.fori_loop(0, count, one, 0)

    @pl.when(step == 0)
    def _():
        start(fetch, get_ref, 0, entries)

    first = step * per_step * list_len
    pairs = range(KV // PAIR)
    keys, values, wide, scores, exact, scales, grads, overlap, prob_grads = (
        {} for _ in range(9)
    )

    def rows_at(b):
        size = list_len * BLK
        return pl.ds(pl.multiple_of((step * per_step + b) * size, size), size)

    def cols_at(b):
        return pl.ds(pl.multiple_of((step * per_step + b) * BLK, BLK), BLK)

    def score(b):
        for i in range(list_len):
            fetch(first + b * list_len + i, 0, 0).wait()
        here = rows_at(b)
        queries = q_ref[:, cols_at(b)] * jnp.asarray(TEMPER, BF16)
        for j in pairs:
            keys[b, j] = kv_scr[here, j * PAIR : (j + 1) * PAIR]
            values[b, j] = kv_scr[here, KV + j * PAIR : KV + (j + 1) * PAIR]
            wide[b, j] = two_groups(queries, j)
            scores[b, j] = jnp.dot(keys[b, j], wide[b, j], preferred_element_type=F32)

    def soften(b, j):
        expo = jnp.exp(scores[b, j] - jnp.max(scores[b, j], axis=0, keepdims=True))
        scale = 1.0 / jnp.sum(expo, axis=0, keepdims=True)
        expo_scr[b, j] = expo.astype(BF16)
        exact[b, j] = head_rows(dot_tn(values[b, j], expo_scr[b, j]) * scale)
        scales[b, j] = jnp.concatenate(
            [
                jnp.broadcast_to(scale[:, i * BLK : (i + 1) * BLK], (HEAD_DIM, BLK))
                for i in range(2 * GROUP)
            ],
            axis=0,
        )

    def normalise(b):
        whole = jnp.concatenate([exact[b, j] for j in pairs], axis=0)
        attended = whole.astype(BF16).astype(F32)
        width = attended.shape[0]
        square = jnp.sum(attended * attended, axis=0, keepdims=True) / width
        inverse = lax.rsqrt(square + EPSILON)
        normed = attended * inverse
        normed_ref[:, cols_at(b)] = normed.astype(BF16)
        normed_grad = ng_ref[:, cols_at(b)]
        shared = jnp.sum(normed_grad * normed, axis=0, keepdims=True) / width
        attended_grad = (normed_grad - normed * shared) * inverse
        scale = jnp.concatenate([scales[b, j] for j in pairs], axis=0)
        scaled_grad = (attended_grad * scale).astype(BF16)
        overlap[b] = scaled_grad.astype(F32) * whole
        for j in pairs:
            grads[b, j] = two_groups(scaled_grad, j)

    def regrade(b, j):
        prob_grads[b, j] = jnp.dot(values[b, j], grads[b, j], preferred_element_type=F32)

    def finish_pair(b, j):
        here = rows_at(b)
        heads = range(2 * GROUP * j, 2 * GROUP * (j + 1))
        row_dot = jnp.concatenate(
            [
                jnp.sum(overlap[b][h * HEAD_DIM : (h + 1) * HEAD_DIM], axis=0, keepdims=True)
                for h in heads
            ],
            axis=1,
        )
        expo = expo_scr[b, j]
        value_part = dot_nt(expo, grads[b, j])
        score_grad = (expo.astype(F32) * (prob_grads[b, j] - row_dot)).astype(BF16)
        query_grad = head_rows(dot_tn(keys[b, j], score_grad) * TEMPER).astype(BF16)
        qg_ref[heads.start * HEAD_DIM : heads.stop * HEAD_DIM, cols_at(b)] = query_grad
        key_part = dot_nt(score_grad, wide[b, j])
        parts_scr[here, j * PAIR : (j + 1) * PAIR] = key_part.astype(BF16)
        parts_scr[here, KV + j * PAIR : KV + (j + 1) * PAIR] = value_part.astype(BF16)

    score(0)
    for j in pairs:
        soften(0, j)
    if per_step > 1:
        score(1)
    normalise(0)
    for b in range(per_step):
        for j in pairs:
            regrade(b, j)
            if b + 1 < per_step:
                soften(b + 1, j)
        if b + 2 < per_step:
            score(b + 2)
        for j in pairs:
            finish_pair(b, j)
            if b + 1 < per_step and j == 0:
                normalise(b + 1)
    start(give, put_ref, first, per_step * list_len)

    @pl.when(step == pl.num_programs(0) - 1)
    def _():
        for e in range(entries):
            give(e, 0, 0).wait()


def attention(gets, puts, queries, normed_grad, arrived, list_len):
    width, rows = queries.shape
    slot_shape = (CAP,) + arrived[0].shape[1:]
    blocks = rows // BLK
    entries = blocks * list_len
    resident = list_len <= 4
    per_step = blocks if resident else 1
    place = WHOLE if resident else pl.BlockSpec(memory_space=pl.ANY)
    keys = list_len * BLK
    pairs = HEADS * rows * keys
    return pl.pallas_call(
        functools.partial(attention_kernel, list_len, per_step),
        grid_spec=pltpu.PrefetchScalarGridSpec(
            num_scalar_prefetch=2,
            grid=(blocks // per_step,),
            in_specs=[WHOLE] * 2 + [place] * len(arrived),
            out_specs=[WHOLE] * 2 + [place] * len(arrived),
            scratch_shapes=[
                pltpu.VMEM((per_step, KV // PAIR, keys, 2 * GROUP * BLK), BF16),
                pltpu.VMEM((entries * BLK, 2 * KV), BF16),
                pltpu.VMEM((entries * BLK, 2 * KV), BF16),
                pltpu.SemaphoreType.DMA((entries,)),
                pltpu.SemaphoreType.DMA((entries,)),
            ],
        ),
        out_shape=[jax.ShapeDtypeStruct((width, rows), BF16)] * 2
        + [jax.ShapeDtypeStruct(slot_shape, BF16)] * len(arrived),
        compiler_params=params(40 if resident else 56),
        cost_estimate=pl.CostEstimate(
            flops=12 * pairs * HEAD_DIM, bytes_accessed=16 * rows * width, transcendentals=pairs
        ),
        name="attention",
    )(gets, puts, queries, normed_grad, *arrived)


def project_kernel(tokens_hbm, wk_hbm, wv_hbm, out_ref, tokens, wk, wv, sems):
    copies = []
    for src, dst, pieces in ((wk_hbm, wk, 2), (tokens_hbm, tokens, 4), (wv_hbm, wv, 2)):
        size = src.shape[0] // pieces
        for i in range(pieces):
            part = pl.ds(i * size, size)
            copies.append(
                pltpu.make_async_copy(src.at[part], dst.at[part], sems.at[len(copies)])
            )
    for copy in copies:
        copy.start()
    for copy in copies[:6]:
        copy.wait()
    keys = jnp.dot(tokens[...], wk[...], preferred_element_type=F32)
    out_ref[:, :KV] = keys.astype(BF16)
    for copy in copies[6:]:
        copy.wait()
    values = jnp.dot(tokens[...], wv[...], preferred_element_type=F32)
    out_ref[:, KV:] = values.astype(BF16)


def project(tokens, w_key, w_value):
    args = (tokens, w_key, w_value)
    return pl.pallas_call(
        project_kernel,
        in_specs=[pl.BlockSpec(memory_space=pl.ANY)] * 3,
        out_specs=WHOLE,
        out_shape=jax.ShapeDtypeStruct((tokens.shape[0], 2 * KV), BF16),
        scratch_shapes=[pltpu.VMEM(x.shape, BF16) for x in args]
        + [pltpu.SemaphoreType.DMA((8,))],
        compiler_params=params(56),
        name="project",
    )(*args)


def pack_kernel(first, wanted_ref, tile_ref, *outs):
    for i, out in enumerate(outs):
        for s in range(CAP):
            out[s] = tile_ref[jnp.maximum(wanted_ref[first + (i + 1) * CAP + s], 0)]


def pack(group, plane, wanted, tile):
    shape = (CAP,) + tile.shape[1:]
    return pl.pallas_call(
        functools.partial(pack_kernel, group * plane * CAP),
        in_specs=[pl.BlockSpec(memory_space=pltpu.SMEM), WHOLE],
        out_specs=[WHOLE] * (plane - 1),
        out_shape=[jax.ShapeDtypeStruct(shape, BF16)] * (plane - 1),
        compiler_params=params(16),
        name="pack",
    )(wanted, tile)


def finish_kernel(parts, *refs):
    term_ref, wk_ref, wv_ref, out_ref = refs[parts:]
    grad = refs[0][...].astype(F32)
    for ref in refs[1:parts]:
        grad += ref[...].astype(F32)
    grad = grad.astype(BF16)
    total = dot_nt(grad[:, :KV], wk_ref[...]) + dot_nt(grad[:, KV:], wv_ref[...])
    out_ref[...] = (term_ref[...] + total).astype(out_ref.dtype)


def finish(parts, term, w_key, w_value, kind, flops):
    return pl.pallas_call(
        functools.partial(finish_kernel, len(parts)),
        in_specs=[WHOLE] * (len(parts) + 3),
        out_specs=WHOLE,
        out_shape=jax.ShapeDtypeStruct(term.shape, kind),
        compiler_params=params(24),
        cost_estimate=pl.CostEstimate(
            flops=flops, bytes_accessed=4 * term.size, transcendentals=0
        ),
        name="finish",
    )(*parts, term, w_key, w_value)


def owner_kernel(first, wanted_ref, *refs):
    parts, (out_ref, total) = refs[:-2], refs[-2:]
    total[...] = jnp.zeros_like(total)
    for p, part in enumerate(parts):
        for s in range(CAP):
            block = wanted_ref[first + p * CAP + s]

            @pl.when(block >= 0)
            def _():
                total[block] += part[s].astype(F32)

    out_ref[...] = total[...].astype(out_ref.dtype)


def owner_sum(group, wanted, parts, blocks, kind, flops):
    shape = (blocks,) + parts[0].shape[1:]
    return pl.pallas_call(
        functools.partial(owner_kernel, group * len(parts) * CAP),
        in_specs=[pl.BlockSpec(memory_space=pltpu.SMEM)] + [WHOLE] * len(parts),
        out_specs=WHOLE,
        out_shape=jax.ShapeDtypeStruct(shape, kind),
        scratch_shapes=[pltpu.VMEM(shape, F32)],
        compiler_params=params(16),
        cost_estimate=pl.CostEstimate(
            flops=flops, bytes_accessed=4 * parts[0].size, transcendentals=0
        ),
        name="owner_sum",
    )(wanted, *parts)


def shards(patches, out_grad, w_query, w_key, w_value, w_out, key_tiles, key_blocks):
    tokens = patches[0]
    rows = tokens.shape[0]
    tile_count = lax.axis_size("tile")
    plane = tile_count // MAJOR
    my_tile = lax.axis_index("tile")
    my_row, my_place = my_tile // plane, my_tile % plane
    block_count = rows // BLK
    list_len = key_tiles.shape[2]
    entry_count = block_count * list_len

    def swap(value, d, cross):
        pairs = [
            (v * tile_count + t, (v ^ cross) * tile_count + (t // plane ^ d) * plane + t % plane)
            for v in range(2)
            for t in range(tile_count)
        ]
        return lax.ppermute(value, ("vintage", "tile"), pairs)

    def after(value, earlier):
        return lax.optimization_barrier((value, earlier))[0]

    def spread(values, earlier=None):
        moved = []
        for i, value in enumerate(values):
            pairs = [(t, t // plane * plane + (t % plane ^ (i + 1))) for t in range(tile_count)]
            if earlier is not None:
                value = after(value, earlier[i])
            moved.append(lax.ppermute(value, "tile", pairs))
        return moved

    def plane_rows(table):
        table = table[0].reshape(MAJOR, plane, entry_count)
        return lax.dynamic_index_in_dim(table, my_row, 0, keepdims=False)

    def mine_of(table):
        return lax.dynamic_index_in_dim(table, my_place, 0, keepdims=False)

    tiles, picks = plane_rows(key_tiles), plane_rows(key_blocks)
    earlier = jnp.arange(entry_count)[:, None] > jnp.arange(entry_count)[None, :]
    same = (tiles[:, :, None] == tiles[:, None, :]) & earlier[None]
    ranks = jnp.sum(same.astype(jnp.int32), axis=2)
    groups, columns = (tiles // plane) ^ my_row, tiles % plane
    my_source = mine_of(groups) * plane + (mine_of(columns) ^ my_place)
    puts = my_source * CODE + mine_of(ranks)
    gets = jnp.where(my_source % plane == 0, my_source * CODE + mine_of(picks), puts)
    ids = jnp.arange(MAJOR * CAP, dtype=jnp.int32)
    slots = groups * CAP + ranks
    hits = (slots[:, None, :] == ids[None, :, None]) & (columns == my_place)[:, None, :]
    wanted = jnp.sum(jnp.where(hits, picks[:, None, :] + 1, 0), axis=2) - 1
    wanted = wanted[jnp.arange(plane) ^ my_place].reshape(plane, MAJOR, CAP)
    wanted = wanted.transpose(1, 0, 2).reshape(-1)

    mine = project(tokens, w_key, w_value).reshape(block_count, BLK, 2 * KV)
    next_tile = swap(mine, 1, 1)
    own_tile = swap(mine, 0, 1)
    far_tile = swap(after(mine, own_tile), 2, 1)
    own = spread(pack(0, plane, wanted, own_tile))
    beside = spread(pack(1, plane, wanted, next_tile), own)
    last_tile = swap(after(far_tile, own[-1]), 1, 0)
    far = spread(pack(2, plane, wanted, after(far_tile, own[-1])), beside)
    last = spread(pack(3, plane, wanted, last_tile), far)
    arrived = [own_tile, *own, next_tile, *beside, far_tile, *far, last_tile, *last]
    queries = lax.dot_general(
        w_query, tokens, (((0,), (1,)), ((), ())), preferred_element_type=F32
    ).astype(BF16)
    normed_grad = dot_nt(w_out, out_grad[0])
    normed_low, query_grad, *back = attention(
        gets, puts, queries, normed_grad, arrived, list_len
    )
    back = [back[d * plane : (d + 1) * plane] for d in range(MAJOR)]
    layer_out = dot_tn(normed_low, w_out).astype(BF16)
    query_term = lax.dot_general(
        query_grad, w_query, (((0,), (1,)), ((), ())), preferred_element_type=F32
    )
    last = spread(back[3][1:])
    last[0], query_term, layer_out = lax.optimization_barrier((last[0], query_term, layer_out))
    far = spread(back[2][1:], last)
    beside = spread(back[1][1:], far)
    last_sum = owner_sum(3, wanted, [back[3][0], *last], block_count, BF16, 0)
    last_sum = swap(last_sum, 1, 0).astype(F32)
    far_sum = owner_sum(2, wanted, [back[2][0], *far], block_count, F32, FAR_SUM_FLOPS)
    far_sum = (far_sum + last_sum).astype(BF16)
    beside[0] = after(beside[0], far_sum)
    next_sum = owner_sum(1, wanted, [back[1][0], *beside], block_count, BF16, 0)
    own = spread([after(after(x, far_sum), next_sum) for x in back[0][1:]], beside)
    own_sum = owner_sum(0, wanted, [back[0][0], *own], block_count, BF16, 0)
    sums = (swap(far_sum, 2, 1), swap(next_sum, 1, 1), swap(own_sum, 0, 1))
    far_grad, next_grad, own_grad = (x.reshape(rows, 2 * KV) for x in sums)
    query_term = finish([far_grad], query_term, w_key, w_value, F32, FAR_FLOPS)
    query_term = finish([next_grad], query_term, w_key, w_value, F32, NEXT_FLOPS)
    input_grad = finish([own_grad], query_term, w_key, w_value, BF16, 800_000_000)
    return (layer_out[None], input_grad[None])


def solution(mesh):
    in_specs = (
        P("vintage", "tile", None),
        P("vintage", "tile", None),
        P(),
        P(),
        P(),
        P(),
        P("vintage", None, None),
        P("vintage", None, None),
    )
    out_specs = (P("vintage", "tile", None), P("vintage", "tile", None))
    return jax.shard_map(shards, mesh=mesh, in_specs=in_specs, out_specs=out_specs, check_vma=False)
```

```python
import functools

import jax
import jax.numpy as jnp
from jax import lax
from jax.experimental import pallas as pl
from jax.experimental.pallas import tpu as pltpu
from jax.sharding import PartitionSpec as P

HEADS = 12
KV_HEADS = 4
HEAD_DIM = 64
BLK = 128
CAP = 2
GROUP = HEADS // KV_HEADS
KV = KV_HEADS * HEAD_DIM
PAIR = 2 * HEAD_DIM
CODE = 64
FAR_SUM_FLOPS = 5_000_000_000
FAR_FLOPS = 20_000_000_000
MAJOR = 4
TEMPER = HEAD_DIM ** (-0.5)
EPSILON = 1e-06
WHOLE = pl.BlockSpec(memory_space=pltpu.VMEM)
F32 = jnp.float32
BF16 = jnp.bfloat16


def params(mebibytes):
    return pltpu.CompilerParams(vmem_limit_bytes=mebibytes * 1024 * 1024)


def dot_nt(a, b):
    return lax.dot_general(a, b, (((1,), (1,)), ((), ())), preferred_element_type=F32)


def dot_tn(a, b):
    return lax.dot_general(a, b, (((0,), (0,)), ((), ())), preferred_element_type=F32)


def feature_heads(features, g):
    first = g * GROUP
    return jnp.concatenate(
        [features[(first + r) * HEAD_DIM : (first + r + 1) * HEAD_DIM] for r in range(GROUP)],
        axis=1,
    )


def two_groups(features, j):
    low, high = feature_heads(features, 2 * j), feature_heads(features, 2 * j + 1)
    zeros = jnp.zeros_like(low)
    return jnp.concatenate(
        [jnp.concatenate([low, zeros], axis=1), jnp.concatenate([zeros, high], axis=1)], axis=0
    )


def head_rows(pair_out):
    heads = []
    for i in range(2 * GROUP):
        top = i // GROUP * HEAD_DIM
        heads.append(pair_out[top : top + HEAD_DIM, i * BLK : (i + 1) * BLK])
    return jnp.concatenate(heads, axis=0)


def attention_kernel(list_len, per_step, sources, get_ref, put_ref, q_ref, ng_ref, *refs):
    expo_scr, kv_scr, parts_scr, in_sems, out_sems = refs[-5:]
    arrived, (normed_ref, qg_ref) = refs[:sources], refs[sources : sources + 2]
    back = refs[sources + 2 : -5]
    step = pl.program_id(0)
    entries = in_sems.shape[0]

    def rows_of(e):
        return pl.ds(pl.multiple_of(e * BLK, BLK), BLK)

    def fetch(e, source, slot):
        return pltpu.make_async_copy(
            arrived[source].at[slot], kv_scr.at[rows_of(e)], in_sems.at[e]
        )

    def give(e, source, slot):
        return pltpu.make_async_copy(
            parts_scr.at[rows_of(e)], back[source].at[slot], out_sems.at[e]
        )

    def start(copy, places, code_ref, begin, count):
        def one(i, carry):
            e = begin + i
            code = code_ref[e]
            for source in range(places):

                @pl.when(code // CODE == source)
                def _():
                    copy(e, source, code % CODE).start()

            return carry

        lax.fori_loop(0, count, one, 0)

    @pl.when(step == 0)
    def _():
        start(fetch, len(arrived), get_ref, 0, entries)

    first = step * per_step * list_len
    pairs = range(KV // PAIR)
    keys, values, wide, scores, exact, scales, grads, overlap, prob_grads = (
        {} for _ in range(9)
    )

    def rows_at(b):
        size = list_len * BLK
        return pl.ds(pl.multiple_of((step * per_step + b) * size, size), size)

    def cols_at(b):
        return pl.ds(pl.multiple_of((step * per_step + b) * BLK, BLK), BLK)

    def score(b):
        for i in range(list_len):
            fetch(first + b * list_len + i, 0, 0).wait()
        here = rows_at(b)
        queries = q_ref[:, cols_at(b)] * jnp.asarray(TEMPER, BF16)
        for j in pairs:
            keys[b, j] = kv_scr[here, j * PAIR : (j + 1) * PAIR]
            values[b, j] = kv_scr[here, KV + j * PAIR : KV + (j + 1) * PAIR]
            wide[b, j] = two_groups(queries, j)
            scores[b, j] = jnp.dot(keys[b, j], wide[b, j], preferred_element_type=F32)

    def soften(b, j):
        expo = jnp.exp(scores[b, j] - jnp.max(scores[b, j], axis=0, keepdims=True))
        scale = 1.0 / jnp.sum(expo, axis=0, keepdims=True)
        expo_scr[b, j] = expo.astype(BF16)
        exact[b, j] = head_rows(dot_tn(values[b, j], expo_scr[b, j]) * scale)
        scales[b, j] = jnp.concatenate(
            [
                jnp.broadcast_to(scale[:, i * BLK : (i + 1) * BLK], (HEAD_DIM, BLK))
                for i in range(2 * GROUP)
            ],
            axis=0,
        )

    def normalise(b):
        whole = jnp.concatenate([exact[b, j] for j in pairs], axis=0)
        attended = whole.astype(BF16).astype(F32)
        width = attended.shape[0]
        square = jnp.sum(attended * attended, axis=0, keepdims=True) / width
        inverse = lax.rsqrt(square + EPSILON)
        normed = attended * inverse
        normed_ref[:, cols_at(b)] = normed.astype(BF16)
        normed_grad = ng_ref[:, cols_at(b)]
        shared = jnp.sum(normed_grad * normed, axis=0, keepdims=True) / width
        attended_grad = (normed_grad - normed * shared) * inverse
        scale = jnp.concatenate([scales[b, j] for j in pairs], axis=0)
        scaled_grad = (attended_grad * scale).astype(BF16)
        overlap[b] = scaled_grad.astype(F32) * whole
        for j in pairs:
            grads[b, j] = two_groups(scaled_grad, j)

    def regrade(b, j):
        prob_grads[b, j] = jnp.dot(values[b, j], grads[b, j], preferred_element_type=F32)

    def finish_pair(b, j):
        here = rows_at(b)
        heads = range(2 * GROUP * j, 2 * GROUP * (j + 1))
        row_dot = jnp.concatenate(
            [
                jnp.sum(overlap[b][h * HEAD_DIM : (h + 1) * HEAD_DIM], axis=0, keepdims=True)
                for h in heads
            ],
            axis=1,
        )
        expo = expo_scr[b, j]
        value_part = dot_nt(expo, grads[b, j])
        score_grad = (expo.astype(F32) * (prob_grads[b, j] - row_dot)).astype(BF16)
        query_grad = head_rows(dot_tn(keys[b, j], score_grad) * TEMPER).astype(BF16)
        qg_ref[heads.start * HEAD_DIM : heads.stop * HEAD_DIM, cols_at(b)] = query_grad
        key_part = dot_nt(score_grad, wide[b, j])
        parts_scr[here, j * PAIR : (j + 1) * PAIR] = key_part.astype(BF16)
        parts_scr[here, KV + j * PAIR : KV + (j + 1) * PAIR] = value_part.astype(BF16)

    score(0)
    for j in pairs:
        soften(0, j)
    if per_step > 1:
        score(1)
    normalise(0)
    for b in range(per_step):
        for j in pairs:
            regrade(b, j)
            if b + 1 < per_step:
                soften(b + 1, j)
        if b + 2 < per_step:
            score(b + 2)
        for j in pairs:
            finish_pair(b, j)
            if b + 1 < per_step and j == 0:
                normalise(b + 1)
    start(give, len(back), put_ref, first, per_step * list_len)

    @pl.when(step == pl.num_programs(0) - 1)
    def _():
        for e in range(entries):
            give(e, 0, 0).wait()


def attention(gets, puts, queries, normed_grad, arrived, list_len, back_shapes):
    width, rows = queries.shape
    blocks = rows // BLK
    entries = blocks * list_len
    resident = list_len <= 4
    per_step = 1
    place = WHOLE if resident else pl.BlockSpec(memory_space=pl.ANY)
    keys = list_len * BLK
    pairs = HEADS * rows * keys
    return pl.pallas_call(
        functools.partial(attention_kernel, list_len, per_step, len(arrived)),
        grid_spec=pltpu.PrefetchScalarGridSpec(
            num_scalar_prefetch=2,
            grid=(blocks // per_step,),
            in_specs=[WHOLE] * 2 + [place] * len(arrived),
            out_specs=[WHOLE] * 2 + [place] * len(back_shapes),
            scratch_shapes=[
                pltpu.VMEM((per_step, KV // PAIR, keys, 2 * GROUP * BLK), BF16),
                pltpu.VMEM((entries * BLK, 2 * KV), BF16),
                pltpu.VMEM((entries * BLK, 2 * KV), BF16),
                pltpu.SemaphoreType.DMA((entries,)),
                pltpu.SemaphoreType.DMA((entries,)),
            ],
        ),
        out_shape=[jax.ShapeDtypeStruct((width, rows), BF16)] * 2
        + [jax.ShapeDtypeStruct(shape, BF16) for shape in back_shapes],
        compiler_params=params(40 if resident else 56),
        cost_estimate=pl.CostEstimate(
            flops=12 * pairs * HEAD_DIM, bytes_accessed=16 * rows * width, transcendentals=pairs
        ),
        name="attention",
    )(gets, puts, queries, normed_grad, *arrived)


def project_kernel(tokens_hbm, wk_hbm, wv_hbm, out_ref, tokens, wk, wv, sems):
    copies = []
    for src, dst, pieces in ((wk_hbm, wk, 2), (tokens_hbm, tokens, 4), (wv_hbm, wv, 2)):
        size = src.shape[0] // pieces
        for i in range(pieces):
            part = pl.ds(i * size, size)
            copies.append(
                pltpu.make_async_copy(src.at[part], dst.at[part], sems.at[len(copies)])
            )
    for copy in copies:
        copy.start()
    for copy in copies[:6]:
        copy.wait()
    keys = jnp.dot(tokens[...], wk[...], preferred_element_type=F32)
    out_ref[:, :KV] = keys.astype(BF16)
    for copy in copies[6:]:
        copy.wait()
    values = jnp.dot(tokens[...], wv[...], preferred_element_type=F32)
    out_ref[:, KV:] = values.astype(BF16)


def project(tokens, w_key, w_value):
    args = (tokens, w_key, w_value)
    return pl.pallas_call(
        project_kernel,
        in_specs=[pl.BlockSpec(memory_space=pl.ANY)] * 3,
        out_specs=WHOLE,
        out_shape=jax.ShapeDtypeStruct((tokens.shape[0], 2 * KV), BF16),
        scratch_shapes=[pltpu.VMEM(x.shape, BF16) for x in args]
        + [pltpu.SemaphoreType.DMA((8,))],
        compiler_params=params(56),
        name="project",
    )(*args)


def pack_kernel(first, wanted_ref, tile_ref, *outs):
    for i, out in enumerate(outs):
        for s in range(CAP):
            out[s] = tile_ref[jnp.maximum(wanted_ref[first + (i + 1) * CAP + s], 0)]


def pack(group, plane, wanted, tile):
    shape = (CAP,) + tile.shape[1:]
    return pl.pallas_call(
        functools.partial(pack_kernel, group * plane * CAP),
        in_specs=[pl.BlockSpec(memory_space=pltpu.SMEM), WHOLE],
        out_specs=[WHOLE] * (plane - 1),
        out_shape=[jax.ShapeDtypeStruct(shape, BF16)] * (plane - 1),
        compiler_params=params(16),
        name="pack",
    )(wanted, tile)


def finish_kernel(parts, *refs):
    term_ref, wk_ref, wv_ref, out_ref = refs[parts:]
    grad = refs[0][...].astype(F32)
    for ref in refs[1:parts]:
        grad += ref[...].astype(F32)
    grad = grad.astype(BF16)
    total = dot_nt(grad[:, :KV], wk_ref[...]) + dot_nt(grad[:, KV:], wv_ref[...])
    out_ref[...] = (term_ref[...] + total).astype(out_ref.dtype)


def finish(parts, term, w_key, w_value, kind, flops):
    return pl.pallas_call(
        functools.partial(finish_kernel, len(parts)),
        in_specs=[WHOLE] * (len(parts) + 3),
        out_specs=WHOLE,
        out_shape=jax.ShapeDtypeStruct(term.shape, kind),
        compiler_params=params(24),
        cost_estimate=pl.CostEstimate(
            flops=flops, bytes_accessed=4 * term.size, transcendentals=0
        ),
        name="finish",
    )(*parts, term, w_key, w_value)


def owner_kernel(first, wanted_ref, *refs):
    parts, (out_ref, total) = refs[:-2], refs[-2:]
    total[...] = jnp.zeros_like(total)
    for p, part in enumerate(parts):
        for s in range(CAP):
            block = wanted_ref[first + p * CAP + s]

            @pl.when(block >= 0)
            def _():
                total[block] += part[s].astype(F32)

    out_ref[...] = total[...].astype(out_ref.dtype)


def owner_sum(group, wanted, parts, blocks, kind, flops):
    shape = (blocks,) + parts[0].shape[1:]
    return pl.pallas_call(
        functools.partial(owner_kernel, group * len(parts) * CAP),
        in_specs=[pl.BlockSpec(memory_space=pltpu.SMEM)] + [WHOLE] * len(parts),
        out_specs=WHOLE,
        out_shape=jax.ShapeDtypeStruct(shape, kind),
        scratch_shapes=[pltpu.VMEM(shape, F32)],
        compiler_params=params(16),
        cost_estimate=pl.CostEstimate(
            flops=flops, bytes_accessed=4 * parts[0].size, transcendentals=0
        ),
        name="owner_sum",
    )(wanted, *parts)


def shards(patches, out_grad, w_query, w_key, w_value, w_out, key_tiles, key_blocks):
    tokens = patches[0]
    rows = tokens.shape[0]
    tile_count = lax.axis_size("tile")
    plane = tile_count // MAJOR
    my_tile = lax.axis_index("tile")
    my_row, my_place = my_tile // plane, my_tile % plane
    block_count = rows // BLK
    list_len = key_tiles.shape[2]
    entry_count = block_count * list_len

    def swap(value, d, cross):
        pairs = [
            (v * tile_count + t, (v ^ cross) * tile_count + (t // plane ^ d) * plane + t % plane)
            for v in range(2)
            for t in range(tile_count)
        ]
        return lax.ppermute(value, ("vintage", "tile"), pairs)

    def after(value, earlier):
        return lax.optimization_barrier((value, earlier))[0]

    def spread(values, earlier=None):
        moved = []
        for i, value in enumerate(values):
            pairs = [(t, t // plane * plane + (t % plane ^ (i + 1))) for t in range(tile_count)]
            if earlier is not None:
                value = after(value, earlier[i])
            moved.append(lax.ppermute(value, "tile", pairs))
        return moved

    def plane_rows(table, row):
        table = table[0].reshape(MAJOR, plane, entry_count)
        return lax.dynamic_index_in_dim(table, row, 0, keepdims=False)

    def mine_of(table):
        return lax.dynamic_index_in_dim(table, my_place, 0, keepdims=False)

    earlier = jnp.arange(entry_count)[:, None] > jnp.arange(entry_count)[None, :]

    def ranked(tiles):
        same = (tiles[:, :, None] == tiles[:, None, :]) & earlier[None]
        return jnp.sum(same.astype(jnp.int32), axis=2)

    def asked(slots, count, picks, valid):
        ids = jnp.arange(count, dtype=jnp.int32)
        hits = (slots[:, None, :] == ids[None, :, None]) & valid[:, None, :]
        found = jnp.sum(jnp.where(hits, picks[:, None, :] + 1, 0), axis=2) - 1
        return found[jnp.arange(plane) ^ my_place]

    tiles, picks = plane_rows(key_tiles, my_row), plane_rows(key_blocks, my_row)
    ranks = ranked(tiles)
    groups, columns = (tiles // plane) ^ my_row, tiles % plane
    my_group, my_peer, my_rank = mine_of(groups), mine_of(columns) ^ my_place, mine_of(ranks)
    gets = (my_group * plane + my_peer) * CODE + jnp.where(my_peer == 0, mine_of(picks), my_rank)
    puts = jnp.where(
        my_group == 1,
        3 * plane * CODE + my_peer * CAP + my_rank,
        (jnp.maximum(my_group - 1, 0) * plane + my_peer) * CODE + my_rank,
    )
    wanted = asked(groups * CAP + ranks, MAJOR * CAP, picks, columns == my_place)
    wanted = wanted.reshape(plane, MAJOR, CAP).transpose(1, 0, 2).reshape(-1)
    tiles, picks = plane_rows(key_tiles, my_row ^ 1), plane_rows(key_blocks, my_row ^ 1)
    beside_wanted = asked(ranked(tiles), CAP, picks, tiles == my_tile).reshape(-1)
    own_wanted = jnp.concatenate([wanted[: plane * CAP], beside_wanted])

    mine = project(tokens, w_key, w_value).reshape(block_count, BLK, 2 * KV)
    next_tile = swap(mine, 1, 1)
    own_tile = swap(mine, 0, 1)
    far_tile = swap(after(mine, own_tile), 2, 1)
    own = spread(pack(0, plane, wanted, own_tile))
    beside = spread(pack(1, plane, wanted, next_tile), own)
    last_tile = swap(after(far_tile, own[-1]), 1, 0)
    far = spread(pack(2, plane, wanted, after(far_tile, own[-1])), beside)
    last = spread(pack(3, plane, wanted, last_tile), far)
    arrived = [own_tile, *own, next_tile, *beside, far_tile, *far, last_tile, *last]
    queries = lax.dot_general(
        w_query, tokens, (((0,), (1,)), ((), ())), preferred_element_type=F32
    ).astype(BF16)
    normed_grad = dot_nt(w_out, out_grad[0])
    slot_shape = (CAP, BLK, 2 * KV)
    back_shapes = [slot_shape] * (3 * plane) + [(plane * CAP, BLK, 2 * KV)]
    normed_low, query_grad, *back = attention(
        gets, puts, queries, normed_grad, arrived, list_len, back_shapes
    )
    hopped = swap(back[3 * plane], 1, 0)
    back = [back[d * plane : (d + 1) * plane] for d in range(3)]
    layer_out = dot_tn(normed_low, w_out).astype(BF16)
    query_term = lax.dot_general(
        query_grad, w_query, (((0,), (1,)), ((), ())), preferred_element_type=F32
    )
    last = spread(back[2][1:])
    last[0], query_term, layer_out = lax.optimization_barrier((last[0], query_term, layer_out))
    far = spread(back[1][1:], last)
    last_sum = owner_sum(3, wanted, [back[2][0], *last], block_count, BF16, 0)
    last_sum = swap(last_sum, 1, 0).astype(F32)
    far_sum = owner_sum(2, wanted, [back[1][0], *far], block_count, F32, FAR_SUM_FLOPS)
    far_sum = (far_sum + last_sum).astype(BF16)
    own = spread(back[0][1:], far)
    beside = [hopped[p * CAP : (p + 1) * CAP] for p in range(plane)]
    beside = [beside[0], *spread([after(x, far_sum) for x in beside[1:]], own)]
    own_sum = owner_sum(0, own_wanted, [back[0][0], *own, *beside], block_count, BF16, 0)
    far_grad, own_grad = swap(far_sum, 2, 1), swap(own_sum, 0, 1)
    query_term = finish(
        [far_grad.reshape(rows, 2 * KV)], query_term, w_key, w_value, F32, FAR_FLOPS
    )
    input_grad = finish(
        [own_grad.reshape(rows, 2 * KV)], query_term, w_key, w_value, BF16, 800_000_000
    )
    return (layer_out[None], input_grad[None])


def solution(mesh):
    in_specs = (
        P("vintage", "tile", None),
        P("vintage", "tile", None),
        P(),
        P(),
        P(),
        P(),
        P("vintage", None, None),
        P("vintage", None, None),
    )
    out_specs = (P("vintage", "tile", None), P("vintage", "tile", None))
    return jax.shard_map(shards, mesh=mesh, in_specs=in_specs, out_specs=out_specs, check_vma=False)
```

```python
import functools

import jax
import jax.numpy as jnp
from jax import lax
from jax.experimental import pallas as pl
from jax.experimental.pallas import tpu as pltpu
from jax.sharding import PartitionSpec as P

HEADS = 12
KV_HEADS = 4
HEAD_DIM = 64
BLK = 128
CAP = 2
GROUP = HEADS // KV_HEADS
KV = KV_HEADS * HEAD_DIM
PAIR = 2 * HEAD_DIM
CODE = 16
FAR_SUM_FLOPS = 8_000_000_000
FAR_FLOPS = 30_000_000_000
MAJOR = 4
TEMPER = HEAD_DIM ** (-0.5)
EPSILON = 1e-06
WHOLE = pl.BlockSpec(memory_space=pltpu.VMEM)
F32 = jnp.float32
BF16 = jnp.bfloat16


def params(mebibytes):
    return pltpu.CompilerParams(vmem_limit_bytes=mebibytes * 1024 * 1024)


def dot_nt(a, b):
    return lax.dot_general(a, b, (((1,), (1,)), ((), ())), preferred_element_type=F32)


def dot_tn(a, b):
    return lax.dot_general(a, b, (((0,), (0,)), ((), ())), preferred_element_type=F32)


def feature_heads(features, g):
    first = g * GROUP
    return jnp.concatenate(
        [features[(first + r) * HEAD_DIM : (first + r + 1) * HEAD_DIM] for r in range(GROUP)],
        axis=1,
    )


def two_groups(features, j):
    low, high = feature_heads(features, 2 * j), feature_heads(features, 2 * j + 1)
    zeros = jnp.zeros_like(low)
    return jnp.concatenate(
        [jnp.concatenate([low, zeros], axis=1), jnp.concatenate([zeros, high], axis=1)], axis=0
    )


def head_rows(pair_out):
    heads = []
    for i in range(2 * GROUP):
        top = i // GROUP * HEAD_DIM
        heads.append(pair_out[top : top + HEAD_DIM, i * BLK : (i + 1) * BLK])
    return jnp.concatenate(heads, axis=0)


def attention_kernel(list_len, per_step, get_ref, put_ref, q_ref, ng_ref, *refs):
    expo_scr, kv_scr, parts_scr, in_sems, out_sems = refs[-5:]
    sources = (len(refs) - 7) // 2
    arrived, (normed_ref, qg_ref) = refs[:sources], refs[sources : sources + 2]
    back = refs[sources + 2 : 2 * sources + 2]
    step = pl.program_id(0)
    entries = in_sems.shape[0]

    def rows_of(e):
        return pl.ds(pl.multiple_of(e * BLK, BLK), BLK)

    def fetch(e, source, slot):
        return pltpu.make_async_copy(
            arrived[source].at[slot], kv_scr.at[rows_of(e)], in_sems.at[e]
        )

    def give(e, source, slot):
        return pltpu.make_async_copy(
            parts_scr.at[rows_of(e)], back[source].at[slot], out_sems.at[e]
        )

    def start(copy, code_ref, begin, count):
        def one(i, carry):
            e = begin + i
            code = code_ref[e]
            for source in range(sources):

                @pl.when(code // CODE == source)
                def _():
                    copy(e, source, code % CODE).start()

            return carry

        lax.fori_loop(0, count, one, 0)

    @pl.when(step == 0)
    def _():
        start(fetch, get_ref, 0, entries)

    first = step * per_step * list_len
    for i in range(per_step * list_len):
        fetch(first + i, 0, 0).wait()
    pairs = range(KV // PAIR)
    keys, values, wide, scores, exact, scales, grads, overlap, prob_grads = (
        {} for _ in range(9)
    )

    def rows_at(b):
        size = list_len * BLK
        return pl.ds(pl.multiple_of((step * per_step + b) * size, size), size)

    def cols_at(b):
        return slice(b * BLK, (b + 1) * BLK)

    def score(b):
        here = rows_at(b)
        queries = q_ref[:, cols_at(b)] * jnp.asarray(TEMPER, BF16)
        for j in pairs:
            keys[b, j] = kv_scr[here, j * PAIR : (j + 1) * PAIR]
            values[b, j] = kv_scr[here, KV + j * PAIR : KV + (j + 1) * PAIR]
            wide[b, j] = two_groups(queries, j)
            scores[b, j] = jnp.dot(keys[b, j], wide[b, j], preferred_element_type=F32)

    def soften(b, j):
        expo = jnp.exp(scores[b, j] - jnp.max(scores[b, j], axis=0, keepdims=True))
        scale = 1.0 / jnp.sum(expo, axis=0, keepdims=True)
        expo_scr[b, j] = expo.astype(BF16)
        exact[b, j] = head_rows(dot_tn(values[b, j], expo_scr[b, j]) * scale)
        scales[b, j] = jnp.concatenate(
            [
                jnp.broadcast_to(scale[:, i * BLK : (i + 1) * BLK], (HEAD_DIM, BLK))
                for i in range(2 * GROUP)
            ],
            axis=0,
        )

    def normalise(b):
        whole = jnp.concatenate([exact[b, j] for j in pairs], axis=0)
        attended = whole.astype(BF16).astype(F32)
        width = attended.shape[0]
        square = jnp.sum(attended * attended, axis=0, keepdims=True) / width
        inverse = lax.rsqrt(square + EPSILON)
        normed = attended * inverse
        normed_ref[:, cols_at(b)] = normed.astype(BF16)
        normed_grad = ng_ref[:, cols_at(b)]
        shared = jnp.sum(normed_grad * normed, axis=0, keepdims=True) / width
        attended_grad = (normed_grad - normed * shared) * inverse
        scale = jnp.concatenate([scales[b, j] for j in pairs], axis=0)
        scaled_grad = (attended_grad * scale).astype(BF16)
        overlap[b] = scaled_grad.astype(F32) * whole
        for j in pairs:
            grads[b, j] = two_groups(scaled_grad, j)

    def regrade(b, j):
        prob_grads[b, j] = jnp.dot(values[b, j], grads[b, j], preferred_element_type=F32)

    def finish_pair(b, j):
        here = rows_at(b)
        heads = range(2 * GROUP * j, 2 * GROUP * (j + 1))
        row_dot = jnp.concatenate(
            [
                jnp.sum(overlap[b][h * HEAD_DIM : (h + 1) * HEAD_DIM], axis=0, keepdims=True)
                for h in heads
            ],
            axis=1,
        )
        expo = expo_scr[b, j]
        value_part = dot_nt(expo, grads[b, j])
        score_grad = (expo.astype(F32) * (prob_grads[b, j] - row_dot)).astype(BF16)
        query_grad = head_rows(dot_tn(keys[b, j], score_grad) * TEMPER).astype(BF16)
        qg_ref[heads.start * HEAD_DIM : heads.stop * HEAD_DIM, cols_at(b)] = query_grad
        key_part = dot_nt(score_grad, wide[b, j])
        parts_scr[here, j * PAIR : (j + 1) * PAIR] = key_part.astype(BF16)
        parts_scr[here, KV + j * PAIR : KV + (j + 1) * PAIR] = value_part.astype(BF16)

    for b in range(per_step):
        score(b)
    for j in pairs:
        soften(0, j)
    normalise(0)
    for b in range(per_step):
        for j in pairs:
            regrade(b, j)
            if b + 1 < per_step:
                soften(b + 1, j)
        for j in pairs:
            finish_pair(b, j)
            if b + 1 < per_step and j == 0:
                normalise(b + 1)
    start(give, put_ref, first, per_step * list_len)

    @pl.when(step == pl.num_programs(0) - 1)
    def _():
        for e in range(entries):
            give(e, 0, 0).wait()


def attention(gets, puts, queries, normed_grad, arrived, list_len):
    width, rows = queries.shape
    slot_shape = (CAP,) + arrived[0].shape[1:]
    blocks = rows // BLK
    entries = blocks * list_len
    per_step = 2 if list_len <= 4 and blocks % 2 == 0 else 1
    row_spec = pl.BlockSpec((width, per_step * BLK), lambda r, g, p: (0, r))
    anywhere = pl.BlockSpec(memory_space=pl.ANY)
    keys = list_len * BLK
    pairs = HEADS * rows * keys
    return pl.pallas_call(
        functools.partial(attention_kernel, list_len, per_step),
        grid_spec=pltpu.PrefetchScalarGridSpec(
            num_scalar_prefetch=2,
            grid=(blocks // per_step,),
            in_specs=[row_spec, row_spec] + [anywhere] * len(arrived),
            out_specs=[row_spec, row_spec] + [anywhere] * len(arrived),
            scratch_shapes=[
                pltpu.VMEM((per_step, KV // PAIR, keys, 2 * GROUP * BLK), BF16),
                pltpu.VMEM((entries * BLK, 2 * KV), BF16),
                pltpu.VMEM((entries * BLK, 2 * KV), BF16),
                pltpu.SemaphoreType.DMA((entries,)),
                pltpu.SemaphoreType.DMA((entries,)),
            ],
        ),
        out_shape=[jax.ShapeDtypeStruct((width, rows), BF16)] * 2
        + [jax.ShapeDtypeStruct(slot_shape, BF16)] * len(arrived),
        compiler_params=params(56),
        cost_estimate=pl.CostEstimate(
            flops=12 * pairs * HEAD_DIM, bytes_accessed=16 * rows * width, transcendentals=pairs
        ),
        name="attention",
    )(gets, puts, queries, normed_grad, *arrived)


def project_kernel(tokens_hbm, wk_hbm, wv_hbm, out_ref, tokens, wk, wv, sems):
    copies = []
    for src, dst, pieces in ((wk_hbm, wk, 2), (tokens_hbm, tokens, 4), (wv_hbm, wv, 2)):
        size = src.shape[0] // pieces
        for i in range(pieces):
            part = pl.ds(i * size, size)
            copies.append(
                pltpu.make_async_copy(src.at[part], dst.at[part], sems.at[len(copies)])
            )
    for copy in copies:
        copy.start()
    for copy in copies[:6]:
        copy.wait()
    keys = jnp.dot(tokens[...], wk[...], preferred_element_type=F32)
    out_ref[:, :KV] = keys.astype(BF16)
    for copy in copies[6:]:
        copy.wait()
    values = jnp.dot(tokens[...], wv[...], preferred_element_type=F32)
    out_ref[:, KV:] = values.astype(BF16)


def project(tokens, w_key, w_value):
    args = (tokens, w_key, w_value)
    return pl.pallas_call(
        project_kernel,
        in_specs=[pl.BlockSpec(memory_space=pl.ANY)] * 3,
        out_specs=WHOLE,
        out_shape=jax.ShapeDtypeStruct((tokens.shape[0], 2 * KV), BF16),
        scratch_shapes=[pltpu.VMEM(x.shape, BF16) for x in args]
        + [pltpu.SemaphoreType.DMA((8,))],
        compiler_params=params(56),
        name="project",
    )(*args)


def pack_kernel(first, wanted_ref, tile_ref, *outs):
    for i, out in enumerate(outs):
        for s in range(CAP):
            out[s] = tile_ref[jnp.maximum(wanted_ref[first + (i + 1) * CAP + s], 0)]


def pack(group, plane, wanted, tile):
    shape = (CAP,) + tile.shape[1:]
    return pl.pallas_call(
        functools.partial(pack_kernel, group * plane * CAP),
        in_specs=[pl.BlockSpec(memory_space=pltpu.SMEM), WHOLE],
        out_specs=[WHOLE] * (plane - 1),
        out_shape=[jax.ShapeDtypeStruct(shape, BF16)] * (plane - 1),
        compiler_params=params(16),
        name="pack",
    )(wanted, tile)


def finish_kernel(parts, *refs):
    term_ref, wk_ref, wv_ref, out_ref = refs[parts:]
    grad = refs[0][...].astype(F32)
    for ref in refs[1:parts]:
        grad += ref[...].astype(F32)
    grad = grad.astype(BF16)
    total = dot_nt(grad[:, :KV], wk_ref[...]) + dot_nt(grad[:, KV:], wv_ref[...])
    out_ref[...] = (term_ref[...] + total).astype(out_ref.dtype)


def finish(parts, term, w_key, w_value, kind, flops):
    return pl.pallas_call(
        functools.partial(finish_kernel, len(parts)),
        in_specs=[WHOLE] * (len(parts) + 3),
        out_specs=WHOLE,
        out_shape=jax.ShapeDtypeStruct(term.shape, kind),
        compiler_params=params(24),
        cost_estimate=pl.CostEstimate(
            flops=flops, bytes_accessed=4 * term.size, transcendentals=0
        ),
        name="finish",
    )(*parts, term, w_key, w_value)


def owner_kernel(first, wanted_ref, *refs):
    parts, (out_ref, total) = refs[:-2], refs[-2:]
    total[...] = jnp.zeros_like(total)
    for p, part in enumerate(parts):
        for s in range(CAP):
            block = wanted_ref[first + p * CAP + s]

            @pl.when(block >= 0)
            def _():
                total[block] += part[s].astype(F32)

    out_ref[...] = total[...].astype(out_ref.dtype)


def owner_sum(group, wanted, parts, blocks, kind, flops):
    shape = (blocks,) + parts[0].shape[1:]
    return pl.pallas_call(
        functools.partial(owner_kernel, group * len(parts) * CAP),
        in_specs=[pl.BlockSpec(memory_space=pltpu.SMEM)] + [WHOLE] * len(parts),
        out_specs=WHOLE,
        out_shape=jax.ShapeDtypeStruct(shape, kind),
        scratch_shapes=[pltpu.VMEM(shape, F32)],
        compiler_params=params(16),
        cost_estimate=pl.CostEstimate(
            flops=flops, bytes_accessed=4 * parts[0].size, transcendentals=0
        ),
        name="owner_sum",
    )(wanted, *parts)


def shards(patches, out_grad, w_query, w_key, w_value, w_out, key_tiles, key_blocks):
    tokens = patches[0]
    rows = tokens.shape[0]
    tile_count = lax.axis_size("tile")
    plane = tile_count // MAJOR
    my_tile = lax.axis_index("tile")
    my_row, my_place = my_tile // plane, my_tile % plane
    block_count = rows // BLK
    list_len = key_tiles.shape[2]
    entry_count = block_count * list_len

    def swap(value, d, cross):
        pairs = [
            (v * tile_count + t, (v ^ cross) * tile_count + (t // plane ^ d) * plane + t % plane)
            for v in range(2)
            for t in range(tile_count)
        ]
        return lax.ppermute(value, ("vintage", "tile"), pairs)

    def after(value, earlier):
        return lax.optimization_barrier((value, earlier))[0]

    def spread(values, earlier=None):
        moved = []
        for i, value in enumerate(values):
            pairs = [(t, t // plane * plane + (t % plane ^ (i + 1))) for t in range(tile_count)]
            if earlier is not None:
                value = after(value, earlier[i])
            moved.append(lax.ppermute(value, "tile", pairs))
        return moved

    def plane_rows(table):
        table = table[0].reshape(MAJOR, plane, entry_count)
        return lax.dynamic_index_in_dim(table, my_row, 0, keepdims=False)

    def mine_of(table):
        return lax.dynamic_index_in_dim(table, my_place, 0, keepdims=False)

    tiles, picks = plane_rows(key_tiles), plane_rows(key_blocks)
    earlier = jnp.arange(entry_count)[:, None] > jnp.arange(entry_count)[None, :]
    same = (tiles[:, :, None] == tiles[:, None, :]) & earlier[None]
    ranks = jnp.sum(same.astype(jnp.int32), axis=2)
    groups, columns = (tiles // plane) ^ my_row, tiles % plane
    my_source = mine_of(groups) * plane + (mine_of(columns) ^ my_place)
    puts = my_source * CODE + mine_of(ranks)
    gets = jnp.where(my_source % plane == 0, my_source * CODE + mine_of(picks), puts)
    ids = jnp.arange(MAJOR * CAP, dtype=jnp.int32)
    slots = groups * CAP + ranks
    hits = (slots[:, None, :] == ids[None, :, None]) & (columns == my_place)[:, None, :]
    wanted = jnp.sum(jnp.where(hits, picks[:, None, :] + 1, 0), axis=2) - 1
    wanted = wanted[jnp.arange(plane) ^ my_place].reshape(plane, MAJOR, CAP)
    wanted = wanted.transpose(1, 0, 2).reshape(-1)

    mine = project(tokens, w_key, w_value).reshape(block_count, BLK, 2 * KV)
    next_tile = swap(mine, 1, 1)
    own_tile = swap(mine, 0, 1)
    far_tile = swap(after(mine, own_tile), 2, 1)
    own = spread(pack(0, plane, wanted, own_tile))
    beside = spread(pack(1, plane, wanted, next_tile), own)
    last_tile = swap(after(far_tile, own[-1]), 1, 0)
    far = spread(pack(2, plane, wanted, after(far_tile, own[-1])), beside)
    last = spread(pack(3, plane, wanted, last_tile), far)
    arrived = [own_tile, *own, next_tile, *beside, far_tile, *far, last_tile, *last]
    queries = lax.dot_general(
        w_query, tokens, (((0,), (1,)), ((), ())), preferred_element_type=F32
    ).astype(BF16)
    normed_grad = dot_nt(w_out, out_grad[0])
    normed_low, query_grad, *back = attention(
        gets, puts, queries, normed_grad, arrived, list_len
    )
    back = [back[d * plane : (d + 1) * plane] for d in range(MAJOR)]
    layer_out = dot_tn(normed_low, w_out).astype(BF16)
    query_term = lax.dot_general(
        query_grad, w_query, (((0,), (1,)), ((), ())), preferred_element_type=F32
    )
    last = spread(back[3][1:])
    last[0], query_term, layer_out = lax.optimization_barrier((last[0], query_term, layer_out))
    far = spread(back[2][1:], last)
    beside = spread(back[1][1:], far)
    last_sum = owner_sum(3, wanted, [back[3][0], *last], block_count, BF16, 0)
    last_sum = swap(last_sum, 1, 0).astype(F32)
    far_sum = owner_sum(2, wanted, [back[2][0], *far], block_count, F32, FAR_SUM_FLOPS)
    far_sum = (far_sum + last_sum).astype(BF16)
    next_sum = owner_sum(1, wanted, [back[1][0], *beside], block_count, BF16, 0)
    own = spread([after(after(x, far_sum), next_sum) for x in back[0][1:]], beside)
    own_sum = owner_sum(0, wanted, [back[0][0], *own], block_count, BF16, 0)
    far_grad = swap(far_sum, 2, 1).reshape(rows, 2 * KV)
    near_grads = [x.reshape(rows, 2 * KV) for x in (swap(next_sum, 1, 1), swap(own_sum, 0, 1))]
    query_term = finish([far_grad], query_term, w_key, w_value, F32, FAR_FLOPS)
    input_grad = finish(near_grads, query_term, w_key, w_value, BF16, 800_000_000)
    return (layer_out[None], input_grad[None])


def solution(mesh):
    in_specs = (
        P("vintage", "tile", None),
        P("vintage", "tile", None),
        P(),
        P(),
        P(),
        P(),
        P("vintage", None, None),
        P("vintage", None, None),
    )
    out_specs = (P("vintage", "tile", None), P("vintage", "tile", None))
    return jax.shard_map(shards, mesh=mesh, in_specs=in_specs, out_specs=out_specs, check_vma=False)
```

```python
import functools

import jax
import jax.numpy as jnp
from jax import lax
from jax.experimental import pallas as pl
from jax.experimental.pallas import tpu as pltpu
from jax.sharding import PartitionSpec as P

HEADS = 12
KV_HEADS = 4
HEAD_DIM = 64
BLK = 128
CAP = 2
GROUP = HEADS // KV_HEADS
KV = KV_HEADS * HEAD_DIM
PAIR = 2 * HEAD_DIM
CODE = 64
FAR_SUM_FLOPS = 5_000_000_000
FAR_FLOPS = 20_000_000_000
MAJOR = 4
TEMPER = HEAD_DIM ** (-0.5)
EPSILON = 1e-06
WHOLE = pl.BlockSpec(memory_space=pltpu.VMEM)
F32 = jnp.float32
BF16 = jnp.bfloat16


def params(mebibytes):
    return pltpu.CompilerParams(vmem_limit_bytes=mebibytes * 1024 * 1024)


def dot_nt(a, b):
    return lax.dot_general(a, b, (((1,), (1,)), ((), ())), preferred_element_type=F32)


def dot_tn(a, b):
    return lax.dot_general(a, b, (((0,), (0,)), ((), ())), preferred_element_type=F32)


def feature_heads(features, g):
    first = g * GROUP
    return jnp.concatenate(
        [features[(first + r) * HEAD_DIM : (first + r + 1) * HEAD_DIM] for r in range(GROUP)],
        axis=1,
    )


def two_groups(features, j):
    low, high = feature_heads(features, 2 * j), feature_heads(features, 2 * j + 1)
    zeros = jnp.zeros_like(low)
    return jnp.concatenate(
        [jnp.concatenate([low, zeros], axis=1), jnp.concatenate([zeros, high], axis=1)], axis=0
    )


def head_rows(pair_out):
    heads = []
    for i in range(2 * GROUP):
        top = i // GROUP * HEAD_DIM
        heads.append(pair_out[top : top + HEAD_DIM, i * BLK : (i + 1) * BLK])
    return jnp.concatenate(heads, axis=0)


def attention_kernel(list_len, per_step, sources, get_ref, put_ref, q_ref, ng_ref, *refs):
    expo_scr, kv_scr, parts_scr, in_sems, out_sems = refs[-5:]
    arrived, (normed_ref, qg_ref) = refs[:sources], refs[sources : sources + 2]
    back = refs[sources + 2 : -5]
    step = pl.program_id(0)
    entries = in_sems.shape[0]

    def rows_of(e):
        return pl.ds(pl.multiple_of(e * BLK, BLK), BLK)

    def fetch(e, source, slot):
        return pltpu.make_async_copy(
            arrived[source].at[slot], kv_scr.at[rows_of(e)], in_sems.at[e]
        )

    def give(e, source, slot):
        return pltpu.make_async_copy(
            parts_scr.at[rows_of(e)], back[source].at[slot], out_sems.at[e]
        )

    def start(copy, places, code_ref, begin, count):
        def one(i, carry):
            e = begin + i
            code = code_ref[e]
            for source in range(places):

                @pl.when(code // CODE == source)
                def _():
                    copy(e, source, code % CODE).start()

            return carry

        lax.fori_loop(0, count, one, 0)

    @pl.when(step == 0)
    def _():
        start(fetch, len(arrived), get_ref, 0, entries)

    first = step * per_step * list_len
    for i in range(per_step * list_len):
        fetch(first + i, 0, 0).wait()
    pairs = range(KV // PAIR)
    keys, values, wide, scores, exact, scales, grads, overlap, prob_grads = (
        {} for _ in range(9)
    )

    def rows_at(b):
        size = list_len * BLK
        return pl.ds(pl.multiple_of((step * per_step + b) * size, size), size)

    def cols_at(b):
        return slice(b * BLK, (b + 1) * BLK)

    def score(b):
        here = rows_at(b)
        queries = q_ref[:, cols_at(b)] * jnp.asarray(TEMPER, BF16)
        for j in pairs:
            keys[b, j] = kv_scr[here, j * PAIR : (j + 1) * PAIR]
            values[b, j] = kv_scr[here, KV + j * PAIR : KV + (j + 1) * PAIR]
            wide[b, j] = two_groups(queries, j)
            scores[b, j] = jnp.dot(keys[b, j], wide[b, j], preferred_element_type=F32)

    def soften(b, j):
        expo = jnp.exp(scores[b, j] - jnp.max(scores[b, j], axis=0, keepdims=True))
        scale = 1.0 / jnp.sum(expo, axis=0, keepdims=True)
        expo_scr[b, j] = expo.astype(BF16)
        exact[b, j] = head_rows(dot_tn(values[b, j], expo_scr[b, j]) * scale)
        scales[b, j] = jnp.concatenate(
            [
                jnp.broadcast_to(scale[:, i * BLK : (i + 1) * BLK], (HEAD_DIM, BLK))
                for i in range(2 * GROUP)
            ],
            axis=0,
        )

    def normalise(b):
        whole = jnp.concatenate([exact[b, j] for j in pairs], axis=0)
        attended = whole.astype(BF16).astype(F32)
        width = attended.shape[0]
        square = jnp.sum(attended * attended, axis=0, keepdims=True) / width
        inverse = lax.rsqrt(square + EPSILON)
        normed = attended * inverse
        normed_ref[:, cols_at(b)] = normed.astype(BF16)
        normed_grad = ng_ref[:, cols_at(b)]
        shared = jnp.sum(normed_grad * normed, axis=0, keepdims=True) / width
        attended_grad = (normed_grad - normed * shared) * inverse
        scale = jnp.concatenate([scales[b, j] for j in pairs], axis=0)
        scaled_grad = (attended_grad * scale).astype(BF16)
        overlap[b] = scaled_grad.astype(F32) * whole
        for j in pairs:
            grads[b, j] = two_groups(scaled_grad, j)

    def regrade(b, j):
        prob_grads[b, j] = jnp.dot(values[b, j], grads[b, j], preferred_element_type=F32)

    def finish_pair(b, j):
        here = rows_at(b)
        heads = range(2 * GROUP * j, 2 * GROUP * (j + 1))
        row_dot = jnp.concatenate(
            [
                jnp.sum(overlap[b][h * HEAD_DIM : (h + 1) * HEAD_DIM], axis=0, keepdims=True)
                for h in heads
            ],
            axis=1,
        )
        expo = expo_scr[b, j]
        value_part = dot_nt(expo, grads[b, j])
        score_grad = (expo.astype(F32) * (prob_grads[b, j] - row_dot)).astype(BF16)
        query_grad = head_rows(dot_tn(keys[b, j], score_grad) * TEMPER).astype(BF16)
        qg_ref[heads.start * HEAD_DIM : heads.stop * HEAD_DIM, cols_at(b)] = query_grad
        key_part = dot_nt(score_grad, wide[b, j])
        parts_scr[here, j * PAIR : (j + 1) * PAIR] = key_part.astype(BF16)
        parts_scr[here, KV + j * PAIR : KV + (j + 1) * PAIR] = value_part.astype(BF16)

    for b in range(per_step):
        score(b)
    for j in pairs:
        soften(0, j)
    normalise(0)
    for b in range(per_step):
        for j in pairs:
            regrade(b, j)
            if b + 1 < per_step:
                soften(b + 1, j)
        for j in pairs:
            finish_pair(b, j)
            if b + 1 < per_step and j == 0:
                normalise(b + 1)
    start(give, len(back), put_ref, first, per_step * list_len)

    @pl.when(step == pl.num_programs(0) - 1)
    def _():
        for e in range(entries):
            give(e, 0, 0).wait()


def attention(gets, puts, queries, normed_grad, arrived, list_len, back_shapes):
    width, rows = queries.shape
    blocks = rows // BLK
    entries = blocks * list_len
    per_step = 2 if list_len <= 4 and blocks % 2 == 0 else 1
    row_spec = pl.BlockSpec((width, per_step * BLK), lambda r, g, p: (0, r))
    anywhere = pl.BlockSpec(memory_space=pl.ANY)
    keys = list_len * BLK
    pairs = HEADS * rows * keys
    return pl.pallas_call(
        functools.partial(attention_kernel, list_len, per_step, len(arrived)),
        grid_spec=pltpu.PrefetchScalarGridSpec(
            num_scalar_prefetch=2,
            grid=(blocks // per_step,),
            in_specs=[row_spec, row_spec] + [anywhere] * len(arrived),
            out_specs=[row_spec, row_spec] + [anywhere] * len(back_shapes),
            scratch_shapes=[
                pltpu.VMEM((per_step, KV // PAIR, keys, 2 * GROUP * BLK), BF16),
                pltpu.VMEM((entries * BLK, 2 * KV), BF16),
                pltpu.VMEM((entries * BLK, 2 * KV), BF16),
                pltpu.SemaphoreType.DMA((entries,)),
                pltpu.SemaphoreType.DMA((entries,)),
            ],
        ),
        out_shape=[jax.ShapeDtypeStruct((width, rows), BF16)] * 2
        + [jax.ShapeDtypeStruct(shape, BF16) for shape in back_shapes],
        compiler_params=params(56),
        cost_estimate=pl.CostEstimate(
            flops=12 * pairs * HEAD_DIM, bytes_accessed=16 * rows * width, transcendentals=pairs
        ),
        name="attention",
    )(gets, puts, queries, normed_grad, *arrived)


def project_kernel(tokens_hbm, wk_hbm, wv_hbm, out_ref, tokens, wk, wv, sems):
    copies = []
    for src, dst, pieces in ((wk_hbm, wk, 2), (tokens_hbm, tokens, 4), (wv_hbm, wv, 2)):
        size = src.shape[0] // pieces
        for i in range(pieces):
            part = pl.ds(i * size, size)
            copies.append(
                pltpu.make_async_copy(src.at[part], dst.at[part], sems.at[len(copies)])
            )
    for copy in copies:
        copy.start()
    for copy in copies[:6]:
        copy.wait()
    keys = jnp.dot(tokens[...], wk[...], preferred_element_type=F32)
    out_ref[:, :KV] = keys.astype(BF16)
    for copy in copies[6:]:
        copy.wait()
    values = jnp.dot(tokens[...], wv[...], preferred_element_type=F32)
    out_ref[:, KV:] = values.astype(BF16)


def project(tokens, w_key, w_value):
    args = (tokens, w_key, w_value)
    return pl.pallas_call(
        project_kernel,
        in_specs=[pl.BlockSpec(memory_space=pl.ANY)] * 3,
        out_specs=WHOLE,
        out_shape=jax.ShapeDtypeStruct((tokens.shape[0], 2 * KV), BF16),
        scratch_shapes=[pltpu.VMEM(x.shape, BF16) for x in args]
        + [pltpu.SemaphoreType.DMA((8,))],
        compiler_params=params(56),
        name="project",
    )(*args)


def pack_kernel(first, wanted_ref, tile_ref, *outs):
    for i, out in enumerate(outs):
        for s in range(CAP):
            out[s] = tile_ref[jnp.maximum(wanted_ref[first + (i + 1) * CAP + s], 0)]


def pack(group, plane, wanted, tile):
    shape = (CAP,) + tile.shape[1:]
    return pl.pallas_call(
        functools.partial(pack_kernel, group * plane * CAP),
        in_specs=[pl.BlockSpec(memory_space=pltpu.SMEM), WHOLE],
        out_specs=[WHOLE] * (plane - 1),
        out_shape=[jax.ShapeDtypeStruct(shape, BF16)] * (plane - 1),
        compiler_params=params(16),
        name="pack",
    )(wanted, tile)


def finish_kernel(parts, *refs):
    term_ref, wk_ref, wv_ref, out_ref = refs[parts:]
    grad = refs[0][...].astype(F32)
    for ref in refs[1:parts]:
        grad += ref[...].astype(F32)
    grad = grad.astype(BF16)
    total = dot_nt(grad[:, :KV], wk_ref[...]) + dot_nt(grad[:, KV:], wv_ref[...])
    out_ref[...] = (term_ref[...] + total).astype(out_ref.dtype)


def finish(parts, term, w_key, w_value, kind, flops):
    return pl.pallas_call(
        functools.partial(finish_kernel, len(parts)),
        in_specs=[WHOLE] * (len(parts) + 3),
        out_specs=WHOLE,
        out_shape=jax.ShapeDtypeStruct(term.shape, kind),
        compiler_params=params(24),
        cost_estimate=pl.CostEstimate(
            flops=flops, bytes_accessed=4 * term.size, transcendentals=0
        ),
        name="finish",
    )(*parts, term, w_key, w_value)


def owner_kernel(first, wanted_ref, *refs):
    parts, (out_ref, total) = refs[:-2], refs[-2:]
    total[...] = jnp.zeros_like(total)
    for p, part in enumerate(parts):
        for s in range(CAP):
            block = wanted_ref[first + p * CAP + s]

            @pl.when(block >= 0)
            def _():
                total[block] += part[s].astype(F32)

    out_ref[...] = total[...].astype(out_ref.dtype)


def owner_sum(group, wanted, parts, blocks, kind, flops):
    shape = (blocks,) + parts[0].shape[1:]
    return pl.pallas_call(
        functools.partial(owner_kernel, group * len(parts) * CAP),
        in_specs=[pl.BlockSpec(memory_space=pltpu.SMEM)] + [WHOLE] * len(parts),
        out_specs=WHOLE,
        out_shape=jax.ShapeDtypeStruct(shape, kind),
        scratch_shapes=[pltpu.VMEM(shape, F32)],
        compiler_params=params(16),
        cost_estimate=pl.CostEstimate(
            flops=flops, bytes_accessed=4 * parts[0].size, transcendentals=0
        ),
        name="owner_sum",
    )(wanted, *parts)


def shards(patches, out_grad, w_query, w_key, w_value, w_out, key_tiles, key_blocks):
    tokens = patches[0]
    rows = tokens.shape[0]
    tile_count = lax.axis_size("tile")
    plane = tile_count // MAJOR
    my_tile = lax.axis_index("tile")
    my_row, my_place = my_tile // plane, my_tile % plane
    block_count = rows // BLK
    list_len = key_tiles.shape[2]
    entry_count = block_count * list_len

    def swap(value, d, cross):
        pairs = [
            (v * tile_count + t, (v ^ cross) * tile_count + (t // plane ^ d) * plane + t % plane)
            for v in range(2)
            for t in range(tile_count)
        ]
        return lax.ppermute(value, ("vintage", "tile"), pairs)

    def after(value, earlier):
        return lax.optimization_barrier((value, earlier))[0]

    def spread(values, earlier=None):
        moved = []
        for i, value in enumerate(values):
            pairs = [(t, t // plane * plane + (t % plane ^ (i + 1))) for t in range(tile_count)]
            if earlier is not None:
                value = after(value, earlier[i])
            moved.append(lax.ppermute(value, "tile", pairs))
        return moved

    def plane_rows(table, row):
        table = table[0].reshape(MAJOR, plane, entry_count)
        return lax.dynamic_index_in_dim(table, row, 0, keepdims=False)

    def mine_of(table):
        return lax.dynamic_index_in_dim(table, my_place, 0, keepdims=False)

    earlier = jnp.arange(entry_count)[:, None] > jnp.arange(entry_count)[None, :]

    def ranked(tiles):
        same = (tiles[:, :, None] == tiles[:, None, :]) & earlier[None]
        return jnp.sum(same.astype(jnp.int32), axis=2)

    def asked(slots, count, picks, valid):
        ids = jnp.arange(count, dtype=jnp.int32)
        hits = (slots[:, None, :] == ids[None, :, None]) & valid[:, None, :]
        found = jnp.sum(jnp.where(hits, picks[:, None, :] + 1, 0), axis=2) - 1
        return found[jnp.arange(plane) ^ my_place]

    tiles, picks = plane_rows(key_tiles, my_row), plane_rows(key_blocks, my_row)
    ranks = ranked(tiles)
    groups, columns = (tiles // plane) ^ my_row, tiles % plane
    my_group, my_peer, my_rank = mine_of(groups), mine_of(columns) ^ my_place, mine_of(ranks)
    gets = (my_group * plane + my_peer) * CODE + jnp.where(my_peer == 0, mine_of(picks), my_rank)
    puts = jnp.where(
        my_group == 1,
        3 * plane * CODE + my_peer * CAP + my_rank,
        (jnp.maximum(my_group - 1, 0) * plane + my_peer) * CODE + my_rank,
    )
    wanted = asked(groups * CAP + ranks, MAJOR * CAP, picks, columns == my_place)
    wanted = wanted.reshape(plane, MAJOR, CAP).transpose(1, 0, 2).reshape(-1)
    tiles, picks = plane_rows(key_tiles, my_row ^ 1), plane_rows(key_blocks, my_row ^ 1)
    beside_wanted = asked(ranked(tiles), CAP, picks, tiles == my_tile).reshape(-1)
    own_wanted = jnp.concatenate([wanted[: plane * CAP], beside_wanted])

    mine = project(tokens, w_key, w_value).reshape(block_count, BLK, 2 * KV)
    next_tile = swap(mine, 1, 1)
    own_tile = swap(mine, 0, 1)
    far_tile = swap(after(mine, own_tile), 2, 1)
    own = spread(pack(0, plane, wanted, own_tile))
    beside = spread(pack(1, plane, wanted, next_tile), own)
    last_tile = swap(after(far_tile, own[-1]), 1, 0)
    far = spread(pack(2, plane, wanted, after(far_tile, own[-1])), beside)
    last = spread(pack(3, plane, wanted, last_tile), far)
    arrived = [own_tile, *own, next_tile, *beside, far_tile, *far, last_tile, *last]
    queries = lax.dot_general(
        w_query, tokens, (((0,), (1,)), ((), ())), preferred_element_type=F32
    ).astype(BF16)
    normed_grad = dot_nt(w_out, out_grad[0])
    slot_shape = (CAP, BLK, 2 * KV)
    back_shapes = [slot_shape] * (3 * plane) + [(plane * CAP, BLK, 2 * KV)]
    normed_low, query_grad, *back = attention(
        gets, puts, queries, normed_grad, arrived, list_len, back_shapes
    )
    hopped = swap(back[3 * plane], 1, 0)
    back = [back[d * plane : (d + 1) * plane] for d in range(3)]
    layer_out = dot_tn(normed_low, w_out).astype(BF16)
    query_term = lax.dot_general(
        query_grad, w_query, (((0,), (1,)), ((), ())), preferred_element_type=F32
    )
    last = spread(back[2][1:])
    last[0], query_term, layer_out = lax.optimization_barrier((last[0], query_term, layer_out))
    far = spread(back[1][1:], last)
    last_sum = owner_sum(3, wanted, [back[2][0], *last], block_count, BF16, 0)
    last_sum = swap(last_sum, 1, 0).astype(F32)
    far_sum = owner_sum(2, wanted, [back[1][0], *far], block_count, F32, FAR_SUM_FLOPS)
    far_sum = (far_sum + last_sum).astype(BF16)
    own = spread(back[0][1:], far)
    beside = [hopped[p * CAP : (p + 1) * CAP] for p in range(plane)]
    beside = [beside[0], *spread([after(x, far_sum) for x in beside[1:]], own)]
    own_sum = owner_sum(0, own_wanted, [back[0][0], *own, *beside], block_count, BF16, 0)
    far_grad, own_grad = swap(far_sum, 2, 1), swap(own_sum, 0, 1)
    query_term = finish(
        [far_grad.reshape(rows, 2 * KV)], query_term, w_key, w_value, F32, FAR_FLOPS
    )
    input_grad = finish(
        [own_grad.reshape(rows, 2 * KV)], query_term, w_key, w_value, BF16, 800_000_000
    )
    return (layer_out[None], input_grad[None])


def solution(mesh):
    in_specs = (
        P("vintage", "tile", None),
        P("vintage", "tile", None),
        P(),
        P(),
        P(),
        P(),
        P("vintage", None, None),
        P("vintage", None, None),
    )
    out_specs = (P("vintage", "tile", None), P("vintage", "tile", None))
    return jax.shard_map(shards, mesh=mesh, in_specs=in_specs, out_specs=out_specs, check_vma=False)
```

```python
import functools

import jax
import jax.numpy as jnp
from jax import lax
from jax.experimental import pallas as pl
from jax.experimental.pallas import tpu as pltpu
from jax.sharding import PartitionSpec as P

HEADS = 12
KV_HEADS = 4
HEAD_DIM = 64
BLK = 128
CAP = 2
GROUP = HEADS // KV_HEADS
KV = KV_HEADS * HEAD_DIM
PAIR = 2 * HEAD_DIM
CODE = 64
FAR_SUM_FLOPS = 5_000_000_000
FAR_FLOPS = 20_000_000_000
MAJOR = 4
TEMPER = HEAD_DIM ** (-0.5)
EPSILON = 1e-06
WHOLE = pl.BlockSpec(memory_space=pltpu.VMEM)
F32 = jnp.float32
BF16 = jnp.bfloat16


def params(mebibytes):
    return pltpu.CompilerParams(vmem_limit_bytes=mebibytes * 1024 * 1024)


def dot_nt(a, b):
    return lax.dot_general(a, b, (((1,), (1,)), ((), ())), preferred_element_type=F32)


def dot_tn(a, b):
    return lax.dot_general(a, b, (((0,), (0,)), ((), ())), preferred_element_type=F32)


def feature_heads(features, g):
    first = g * GROUP
    return jnp.concatenate(
        [features[(first + r) * HEAD_DIM : (first + r + 1) * HEAD_DIM] for r in range(GROUP)],
        axis=1,
    )


def two_groups(features, j):
    low, high = feature_heads(features, 2 * j), feature_heads(features, 2 * j + 1)
    zeros = jnp.zeros_like(low)
    return jnp.concatenate(
        [jnp.concatenate([low, zeros], axis=1), jnp.concatenate([zeros, high], axis=1)], axis=0
    )


def head_rows(pair_out):
    heads = []
    for i in range(2 * GROUP):
        top = i // GROUP * HEAD_DIM
        heads.append(pair_out[top : top + HEAD_DIM, i * BLK : (i + 1) * BLK])
    return jnp.concatenate(heads, axis=0)


def attention_kernel(list_len, per_step, sources, get_ref, put_ref, q_ref, ng_ref, *refs):
    expo_scr, kv_scr, parts_scr, in_sems, out_sems = refs[-5:]
    arrived, (normed_ref, qg_ref) = refs[:sources], refs[sources : sources + 2]
    back = refs[sources + 2 : -5]
    step = pl.program_id(0)
    entries = in_sems.shape[0]

    def rows_of(e):
        return pl.ds(pl.multiple_of(e * BLK, BLK), BLK)

    def fetch(e, source, slot):
        return pltpu.make_async_copy(
            arrived[source].at[slot], kv_scr.at[rows_of(e)], in_sems.at[e]
        )

    def give(e, source, slot):
        return pltpu.make_async_copy(
            parts_scr.at[rows_of(e)], back[source].at[slot], out_sems.at[e]
        )

    def start(copy, places, code_ref, begin, count):
        def one(i, carry):
            e = begin + i
            code = code_ref[e]
            for source in range(places):

                @pl.when(code // CODE == source)
                def _():
                    copy(e, source, code % CODE).start()

            return carry

        lax.fori_loop(0, count, one, 0)

    @pl.when(step == 0)
    def _():
        start(fetch, len(arrived), get_ref, 0, entries)

    first = step * per_step * list_len
    for i in range(per_step * list_len):
        fetch(first + i, 0, 0).wait()
    pairs = range(KV // PAIR)
    keys, values, wide, scores, exact, scales, grads, overlap, prob_grads = (
        {} for _ in range(9)
    )

    def rows_at(b):
        size = list_len * BLK
        return pl.ds(pl.multiple_of((step * per_step + b) * size, size), size)

    def cols_at(b):
        return slice(b * BLK, (b + 1) * BLK)

    def score(b):
        here = rows_at(b)
        queries = q_ref[:, cols_at(b)] * jnp.asarray(TEMPER, BF16)
        for j in pairs:
            keys[b, j] = kv_scr[here, j * PAIR : (j + 1) * PAIR]
            values[b, j] = kv_scr[here, KV + j * PAIR : KV + (j + 1) * PAIR]
            wide[b, j] = two_groups(queries, j)
            scores[b, j] = jnp.dot(keys[b, j], wide[b, j], preferred_element_type=F32)

    def soften(b, j):
        expo = jnp.exp(scores[b, j] - jnp.max(scores[b, j], axis=0, keepdims=True))
        scale = 1.0 / jnp.sum(expo, axis=0, keepdims=True)
        expo_scr[b, j] = expo.astype(BF16)
        exact[b, j] = head_rows(dot_tn(values[b, j], expo_scr[b, j]) * scale)
        scales[b, j] = jnp.concatenate(
            [
                jnp.broadcast_to(scale[:, i * BLK : (i + 1) * BLK], (HEAD_DIM, BLK))
                for i in range(2 * GROUP)
            ],
            axis=0,
        )

    def normalise(b):
        whole = jnp.concatenate([exact[b, j] for j in pairs], axis=0)
        attended = whole.astype(BF16).astype(F32)
        width = attended.shape[0]
        square = jnp.sum(attended * attended, axis=0, keepdims=True) / width
        inverse = lax.rsqrt(square + EPSILON)
        normed = attended * inverse
        normed_ref[:, cols_at(b)] = normed.astype(BF16)
        normed_grad = ng_ref[:, cols_at(b)]
        shared = jnp.sum(normed_grad * normed, axis=0, keepdims=True) / width
        attended_grad = (normed_grad - normed * shared) * inverse
        scale = jnp.concatenate([scales[b, j] for j in pairs], axis=0)
        scaled_grad = (attended_grad * scale).astype(BF16)
        overlap[b] = scaled_grad.astype(F32) * whole
        for j in pairs:
            grads[b, j] = two_groups(scaled_grad, j)

    def regrade(b, j):
        prob_grads[b, j] = jnp.dot(values[b, j], grads[b, j], preferred_element_type=F32)

    def finish_pair(b, j):
        here = rows_at(b)
        heads = range(2 * GROUP * j, 2 * GROUP * (j + 1))
        row_dot = jnp.concatenate(
            [
                jnp.sum(overlap[b][h * HEAD_DIM : (h + 1) * HEAD_DIM], axis=0, keepdims=True)
                for h in heads
            ],
            axis=1,
        )
        expo = expo_scr[b, j]
        value_part = dot_nt(expo, grads[b, j])
        score_grad = (expo.astype(F32) * (prob_grads[b, j] - row_dot)).astype(BF16)
        query_grad = head_rows(dot_tn(keys[b, j], score_grad) * TEMPER).astype(BF16)
        qg_ref[heads.start * HEAD_DIM : heads.stop * HEAD_DIM, cols_at(b)] = query_grad
        key_part = dot_nt(score_grad, wide[b, j])
        parts_scr[here, j * PAIR : (j + 1) * PAIR] = key_part.astype(BF16)
        parts_scr[here, KV + j * PAIR : KV + (j + 1) * PAIR] = value_part.astype(BF16)

    for b in range(per_step):
        score(b)
    for j in pairs:
        soften(0, j)
    normalise(0)
    for b in range(per_step):
        for j in pairs:
            regrade(b, j)
            if b + 1 < per_step:
                soften(b + 1, j)
        for j in pairs:
            finish_pair(b, j)
            if b + 1 < per_step and j == 0:
                normalise(b + 1)
    start(give, len(back), put_ref, first, per_step * list_len)

    @pl.when(step == pl.num_programs(0) - 1)
    def _():
        for e in range(entries):
            give(e, 0, 0).wait()


def attention(gets, puts, queries, normed_grad, arrived, list_len, back_shapes):
    width, rows = queries.shape
    blocks = rows // BLK
    entries = blocks * list_len
    per_step = 2 if list_len <= 4 and blocks % 2 == 0 else 1
    row_spec = pl.BlockSpec((width, per_step * BLK), lambda r, g, p: (0, r))
    anywhere = pl.BlockSpec(memory_space=pl.ANY)
    keys = list_len * BLK
    pairs = HEADS * rows * keys
    return pl.pallas_call(
        functools.partial(attention_kernel, list_len, per_step, len(arrived)),
        grid_spec=pltpu.PrefetchScalarGridSpec(
            num_scalar_prefetch=2,
            grid=(blocks // per_step,),
            in_specs=[row_spec, row_spec] + [anywhere] * len(arrived),
            out_specs=[row_spec, row_spec] + [anywhere] * len(back_shapes),
            scratch_shapes=[
                pltpu.VMEM((per_step, KV // PAIR, keys, 2 * GROUP * BLK), BF16),
                pltpu.VMEM((entries * BLK, 2 * KV), BF16),
                pltpu.VMEM((entries * BLK, 2 * KV), BF16),
                pltpu.SemaphoreType.DMA((entries,)),
                pltpu.SemaphoreType.DMA((entries,)),
            ],
        ),
        out_shape=[jax.ShapeDtypeStruct((width, rows), BF16)] * 2
        + [jax.ShapeDtypeStruct(shape, BF16) for shape in back_shapes],
        compiler_params=params(56),
        cost_estimate=pl.CostEstimate(
            flops=12 * pairs * HEAD_DIM, bytes_accessed=16 * rows * width, transcendentals=pairs
        ),
        name="attention",
    )(gets, puts, queries, normed_grad, *arrived)


def project_kernel(tokens_hbm, wk_hbm, wv_hbm, out_ref, tokens, wk, wv, sems):
    copies = []
    for src, dst, pieces in ((wk_hbm, wk, 2), (tokens_hbm, tokens, 4), (wv_hbm, wv, 2)):
        size = src.shape[0] // pieces
        for i in range(pieces):
            part = pl.ds(i * size, size)
            copies.append(
                pltpu.make_async_copy(src.at[part], dst.at[part], sems.at[len(copies)])
            )
    for copy in copies:
        copy.start()
    for copy in copies[:6]:
        copy.wait()
    keys = jnp.dot(tokens[...], wk[...], preferred_element_type=F32)
    out_ref[:, :KV] = keys.astype(BF16)
    for copy in copies[6:]:
        copy.wait()
    values = jnp.dot(tokens[...], wv[...], preferred_element_type=F32)
    out_ref[:, KV:] = values.astype(BF16)


def project(tokens, w_key, w_value):
    args = (tokens, w_key, w_value)
    return pl.pallas_call(
        project_kernel,
        in_specs=[pl.BlockSpec(memory_space=pl.ANY)] * 3,
        out_specs=WHOLE,
        out_shape=jax.ShapeDtypeStruct((tokens.shape[0], 2 * KV), BF16),
        scratch_shapes=[pltpu.VMEM(x.shape, BF16) for x in args]
        + [pltpu.SemaphoreType.DMA((8,))],
        compiler_params=params(56),
        name="project",
    )(*args)


def pack_kernel(first, wanted_ref, tile_ref, *outs):
    for i, out in enumerate(outs):
        for s in range(CAP):
            out[s] = tile_ref[jnp.maximum(wanted_ref[first + (i + 1) * CAP + s], 0)]


def pack(group, plane, wanted, tile):
    shape = (CAP,) + tile.shape[1:]
    return pl.pallas_call(
        functools.partial(pack_kernel, group * plane * CAP),
        in_specs=[pl.BlockSpec(memory_space=pltpu.SMEM), WHOLE],
        out_specs=[WHOLE] * (plane - 1),
        out_shape=[jax.ShapeDtypeStruct(shape, BF16)] * (plane - 1),
        compiler_params=params(16),
        name="pack",
    )(wanted, tile)


def finish_kernel(parts, *refs):
    term_ref, wk_ref, wv_ref, out_ref = refs[parts:]
    grad = refs[0][...].astype(F32)
    for ref in refs[1:parts]:
        grad += ref[...].astype(F32)
    grad = grad.astype(BF16)
    total = dot_nt(grad[:, :KV], wk_ref[...]) + dot_nt(grad[:, KV:], wv_ref[...])
    out_ref[...] = (term_ref[...] + total).astype(out_ref.dtype)


def finish(parts, term, w_key, w_value, kind, flops):
    return pl.pallas_call(
        functools.partial(finish_kernel, len(parts)),
        in_specs=[WHOLE] * (len(parts) + 3),
        out_specs=WHOLE,
        out_shape=jax.ShapeDtypeStruct(term.shape, kind),
        compiler_params=params(24),
        cost_estimate=pl.CostEstimate(
            flops=flops, bytes_accessed=4 * term.size, transcendentals=0
        ),
        name="finish",
    )(*parts, term, w_key, w_value)


def owner_kernel(first, wanted_ref, *refs):
    parts, (out_ref, total) = refs[:-2], refs[-2:]
    total[...] = jnp.zeros_like(total)
    for p, part in enumerate(parts):
        for s in range(CAP):
            block = wanted_ref[first + p * CAP + s]

            @pl.when(block >= 0)
            def _():
                total[block] += part[s].astype(F32)

    out_ref[...] = total[...].astype(out_ref.dtype)


def owner_sum(group, wanted, parts, blocks, kind, flops):
    shape = (blocks,) + parts[0].shape[1:]
    return pl.pallas_call(
        functools.partial(owner_kernel, group * len(parts) * CAP),
        in_specs=[pl.BlockSpec(memory_space=pltpu.SMEM)] + [WHOLE] * len(parts),
        out_specs=WHOLE,
        out_shape=jax.ShapeDtypeStruct(shape, kind),
        scratch_shapes=[pltpu.VMEM(shape, F32)],
        compiler_params=params(16),
        cost_estimate=pl.CostEstimate(
            flops=flops, bytes_accessed=4 * parts[0].size, transcendentals=0
        ),
        name="owner_sum",
    )(wanted, *parts)


def shards(patches, out_grad, w_query, w_key, w_value, w_out, key_tiles, key_blocks):
    tokens = patches[0]
    rows = tokens.shape[0]
    tile_count = lax.axis_size("tile")
    plane = tile_count // MAJOR
    my_tile = lax.axis_index("tile")
    my_row, my_place = my_tile // plane, my_tile % plane
    block_count = rows // BLK
    list_len = key_tiles.shape[2]
    entry_count = block_count * list_len

    def swap(value, d, cross):
        pairs = [
            (v * tile_count + t, (v ^ cross) * tile_count + (t // plane ^ d) * plane + t % plane)
            for v in range(2)
            for t in range(tile_count)
        ]
        return lax.ppermute(value, ("vintage", "tile"), pairs)

    def after(value, earlier):
        return lax.optimization_barrier((value, earlier))[0]

    def spread(values, earlier=None):
        moved = []
        for i, value in enumerate(values):
            pairs = [(t, t // plane * plane + (t % plane ^ (i + 1))) for t in range(tile_count)]
            if earlier is not None:
                value = after(value, earlier[i])
            moved.append(lax.ppermute(value, "tile", pairs))
        return moved

    def plane_rows(table, row):
        table = table[0].reshape(MAJOR, plane, entry_count)
        return lax.dynamic_index_in_dim(table, row, 0, keepdims=False)

    def mine_of(table):
        return lax.dynamic_index_in_dim(table, my_place, 0, keepdims=False)

    earlier = jnp.arange(entry_count)[:, None] > jnp.arange(entry_count)[None, :]

    def ranked(tiles):
        same = (tiles[:, :, None] == tiles[:, None, :]) & earlier[None]
        return jnp.sum(same.astype(jnp.int32), axis=2)

    def asked(slots, count, picks, valid):
        ids = jnp.arange(count, dtype=jnp.int32)
        hits = (slots[:, None, :] == ids[None, :, None]) & valid[:, None, :]
        found = jnp.sum(jnp.where(hits, picks[:, None, :] + 1, 0), axis=2) - 1
        return found[jnp.arange(plane) ^ my_place]

    tiles, picks = plane_rows(key_tiles, my_row), plane_rows(key_blocks, my_row)
    ranks = ranked(tiles)
    groups, columns = (tiles // plane) ^ my_row, tiles % plane
    my_group, my_peer, my_rank = mine_of(groups), mine_of(columns) ^ my_place, mine_of(ranks)
    gets = (my_group * plane + my_peer) * CODE + jnp.where(my_peer == 0, mine_of(picks), my_rank)
    puts = jnp.where(
        my_group == 1,
        3 * plane * CODE + my_peer * CAP + my_rank,
        (jnp.maximum(my_group - 1, 0) * plane + my_peer) * CODE + my_rank,
    )
    wanted = asked(groups * CAP + ranks, MAJOR * CAP, picks, columns == my_place)
    wanted = wanted.reshape(plane, MAJOR, CAP).transpose(1, 0, 2).reshape(-1)
    tiles, picks = plane_rows(key_tiles, my_row ^ 1), plane_rows(key_blocks, my_row ^ 1)
    beside_wanted = asked(ranked(tiles), CAP, picks, tiles == my_tile).reshape(-1)
    own_wanted = jnp.concatenate([wanted[: plane * CAP], beside_wanted])

    mine = project(tokens, w_key, w_value).reshape(block_count, BLK, 2 * KV)
    next_tile = swap(mine, 1, 1)
    own_tile = swap(mine, 0, 1)
    far_tile = swap(after(mine, own_tile), 2, 1)
    own = spread(pack(0, plane, wanted, own_tile))
    beside = spread(pack(1, plane, wanted, next_tile), own)
    last_tile = swap(after(far_tile, own[-1]), 1, 0)
    far = spread(pack(2, plane, wanted, after(far_tile, own[-1])), beside)
    last = spread(pack(3, plane, wanted, last_tile), far)
    arrived = [own_tile, *own, next_tile, *beside, far_tile, *far, last_tile, *last]
    queries = lax.dot_general(
        w_query, tokens, (((0,), (1,)), ((), ())), preferred_element_type=F32
    ).astype(BF16)
    normed_grad = dot_nt(w_out, out_grad[0])
    slot_shape = (CAP, BLK, 2 * KV)
    back_shapes = [slot_shape] * (3 * plane) + [(plane * CAP, BLK, 2 * KV)]
    normed_low, query_grad, *back = attention(
        gets, puts, queries, normed_grad, arrived, list_len, back_shapes
    )
    hopped = swap(back[3 * plane], 1, 0)
    back = [back[d * plane : (d + 1) * plane] for d in range(3)]
    layer_out = dot_tn(normed_low, w_out).astype(BF16)
    query_term = lax.dot_general(
        query_grad, w_query, (((0,), (1,)), ((), ())), preferred_element_type=F32
    )
    last = spread(back[2][1:])
    last[0], query_term, layer_out = lax.optimization_barrier((last[0], query_term, layer_out))
    far = spread(back[1][1:], last)
    last_sum = owner_sum(3, wanted, [back[2][0], *last], block_count, BF16, 0)
    last_sum = swap(last_sum, 1, 0).astype(F32)
    beside = [hopped[p * CAP : (p + 1) * CAP] for p in range(plane)]
    far[0], *beside = lax.optimization_barrier((far[0], *beside))
    far_sum = owner_sum(2, wanted, [back[1][0], *far], block_count, BF16, FAR_SUM_FLOPS)
    far_sum = (far_sum.astype(F32) + last_sum).astype(BF16)
    own = spread(back[0][1:], far)
    beside = [beside[0], *spread([after(x, far_sum) for x in beside[1:]], own)]
    own_sum = owner_sum(0, own_wanted, [back[0][0], *own, *beside], block_count, BF16, 0)
    far_grad, own_grad = swap(far_sum, 2, 1), swap(own_sum, 0, 1)
    query_term = finish(
        [far_grad.reshape(rows, 2 * KV)], query_term, w_key, w_value, F32, FAR_FLOPS
    )
    input_grad = finish(
        [own_grad.reshape(rows, 2 * KV)], query_term, w_key, w_value, BF16, 800_000_000
    )
    return (layer_out[None], input_grad[None])


def solution(mesh):
    in_specs = (
        P("vintage", "tile", None),
        P("vintage", "tile", None),
        P(),
        P(),
        P(),
        P(),
        P("vintage", None, None),
        P("vintage", None, None),
    )
    out_specs = (P("vintage", "tile", None), P("vintage", "tile", None))
    return jax.shard_map(shards, mesh=mesh, in_specs=in_specs, out_specs=out_specs, check_vma=False)
```

```python
import functools

import jax
import jax.numpy as jnp
from jax import lax
from jax.experimental import pallas as pl
from jax.experimental.pallas import tpu as pltpu
from jax.sharding import PartitionSpec as P

HEADS = 12
KV_HEADS = 4
HEAD_DIM = 64
BLK = 128
CAP = 2
GROUP = HEADS // KV_HEADS
KV = KV_HEADS * HEAD_DIM
PAIR = 2 * HEAD_DIM
CODE = 64
FAR_SUM_FLOPS = 5_000_000_000
FAR_FLOPS = 20_000_000_000
MAJOR = 4
TEMPER = HEAD_DIM ** (-0.5)
EPSILON = 1e-06
WHOLE = pl.BlockSpec(memory_space=pltpu.VMEM)
F32 = jnp.float32
BF16 = jnp.bfloat16


def params(mebibytes):
    return pltpu.CompilerParams(vmem_limit_bytes=mebibytes * 1024 * 1024)


def dot_nt(a, b):
    return lax.dot_general(a, b, (((1,), (1,)), ((), ())), preferred_element_type=F32)


def dot_tn(a, b):
    return lax.dot_general(a, b, (((0,), (0,)), ((), ())), preferred_element_type=F32)


def feature_heads(features, g):
    first = g * GROUP
    return jnp.concatenate(
        [features[(first + r) * HEAD_DIM : (first + r + 1) * HEAD_DIM] for r in range(GROUP)],
        axis=1,
    )


def two_groups(features, j):
    low, high = feature_heads(features, 2 * j), feature_heads(features, 2 * j + 1)
    zeros = jnp.zeros_like(low)
    return jnp.concatenate(
        [jnp.concatenate([low, zeros], axis=1), jnp.concatenate([zeros, high], axis=1)], axis=0
    )


def head_rows(pair_out):
    heads = []
    for i in range(2 * GROUP):
        top = i // GROUP * HEAD_DIM
        heads.append(pair_out[top : top + HEAD_DIM, i * BLK : (i + 1) * BLK])
    return jnp.concatenate(heads, axis=0)


def attention_kernel(list_len, per_step, sources, get_ref, put_ref, q_ref, ng_ref, *refs):
    expo_scr, kv_scr, parts_scr, in_sems, out_sems = refs[-5:]
    arrived, (normed_ref, qg_ref) = refs[:sources], refs[sources : sources + 2]
    back = refs[sources + 2 : -5]
    step = pl.program_id(0)
    entries = in_sems.shape[0]

    def rows_of(e):
        return pl.ds(pl.multiple_of(e * BLK, BLK), BLK)

    def fetch(e, source, slot):
        return pltpu.make_async_copy(
            arrived[source].at[slot], kv_scr.at[rows_of(e)], in_sems.at[e]
        )

    def give(e, source, slot):
        return pltpu.make_async_copy(
            parts_scr.at[rows_of(e)], back[source].at[slot], out_sems.at[e]
        )

    def start(copy, places, code_ref, begin, count):
        def one(i, carry):
            e = begin + i
            code = code_ref[e]
            for source in range(places):

                @pl.when(code // CODE == source)
                def _():
                    copy(e, source, code % CODE).start()

            return carry

        lax.fori_loop(0, count, one, 0)

    @pl.when(step == 0)
    def _():
        start(fetch, len(arrived), get_ref, 0, entries)

    first = step * per_step * list_len
    for i in range(per_step * list_len):
        fetch(first + i, 0, 0).wait()
    pairs = range(KV // PAIR)
    keys, values, wide, scores, exact, scales, grads, overlap, prob_grads = (
        {} for _ in range(9)
    )

    def rows_at(b):
        size = list_len * BLK
        return pl.ds(pl.multiple_of((step * per_step + b) * size, size), size)

    def cols_at(b):
        return slice(b * BLK, (b + 1) * BLK)

    def score(b):
        here = rows_at(b)
        queries = q_ref[:, cols_at(b)] * jnp.asarray(TEMPER, BF16)
        for j in pairs:
            keys[b, j] = kv_scr[here, j * PAIR : (j + 1) * PAIR]
            values[b, j] = kv_scr[here, KV + j * PAIR : KV + (j + 1) * PAIR]
            wide[b, j] = two_groups(queries, j)
            scores[b, j] = jnp.dot(keys[b, j], wide[b, j], preferred_element_type=F32)

    def soften(b, j):
        expo = jnp.exp(scores[b, j] - jnp.max(scores[b, j], axis=0, keepdims=True))
        scale = 1.0 / jnp.sum(expo, axis=0, keepdims=True)
        expo_scr[b, j] = expo.astype(BF16)
        exact[b, j] = head_rows(dot_tn(values[b, j], expo_scr[b, j]) * scale)
        scales[b, j] = jnp.concatenate(
            [
                jnp.broadcast_to(scale[:, i * BLK : (i + 1) * BLK], (HEAD_DIM, BLK))
                for i in range(2 * GROUP)
            ],
            axis=0,
        )

    def normalise(b):
        whole = jnp.concatenate([exact[b, j] for j in pairs], axis=0)
        attended = whole.astype(BF16).astype(F32)
        width = attended.shape[0]
        square = jnp.sum(attended * attended, axis=0, keepdims=True) / width
        inverse = lax.rsqrt(square + EPSILON)
        normed = attended * inverse
        normed_ref[:, cols_at(b)] = normed.astype(BF16)
        normed_grad = ng_ref[:, cols_at(b)]
        shared = jnp.sum(normed_grad * normed, axis=0, keepdims=True) / width
        attended_grad = (normed_grad - normed * shared) * inverse
        scale = jnp.concatenate([scales[b, j] for j in pairs], axis=0)
        scaled_grad = (attended_grad * scale).astype(BF16)
        overlap[b] = scaled_grad.astype(F32) * whole
        for j in pairs:
            grads[b, j] = two_groups(scaled_grad, j)

    def regrade(b, j):
        prob_grads[b, j] = jnp.dot(values[b, j], grads[b, j], preferred_element_type=F32)

    def finish_pair(b, j):
        here = rows_at(b)
        heads = range(2 * GROUP * j, 2 * GROUP * (j + 1))
        row_dot = jnp.concatenate(
            [
                jnp.sum(overlap[b][h * HEAD_DIM : (h + 1) * HEAD_DIM], axis=0, keepdims=True)
                for h in heads
            ],
            axis=1,
        )
        expo = expo_scr[b, j]
        value_part = dot_nt(expo, grads[b, j])
        score_grad = (expo.astype(F32) * (prob_grads[b, j] - row_dot)).astype(BF16)
        query_grad = head_rows(dot_tn(keys[b, j], score_grad) * TEMPER).astype(BF16)
        qg_ref[heads.start * HEAD_DIM : heads.stop * HEAD_DIM, cols_at(b)] = query_grad
        key_part = dot_nt(score_grad, wide[b, j])
        parts_scr[here, j * PAIR : (j + 1) * PAIR] = key_part.astype(BF16)
        parts_scr[here, KV + j * PAIR : KV + (j + 1) * PAIR] = value_part.astype(BF16)

    for b in range(per_step):
        score(b)
    for j in pairs:
        soften(0, j)
    normalise(0)
    for b in range(per_step):
        for j in pairs:
            regrade(b, j)
            if b + 1 < per_step:
                soften(b + 1, j)
        for j in pairs:
            finish_pair(b, j)
            if b + 1 < per_step and j == 0:
                normalise(b + 1)
    start(give, len(back), put_ref, first, per_step * list_len)

    @pl.when(step == pl.num_programs(0) - 1)
    def _():
        for e in range(entries):
            give(e, 0, 0).wait()


def attention(gets, puts, queries, normed_grad, arrived, list_len, back_shapes):
    width, rows = queries.shape
    blocks = rows // BLK
    entries = blocks * list_len
    per_step = 2 if list_len <= 4 and blocks % 2 == 0 else 1
    row_spec = pl.BlockSpec((width, per_step * BLK), lambda r, g, p: (0, r))
    anywhere = pl.BlockSpec(memory_space=pl.ANY)
    keys = list_len * BLK
    pairs = HEADS * rows * keys
    return pl.pallas_call(
        functools.partial(attention_kernel, list_len, per_step, len(arrived)),
        grid_spec=pltpu.PrefetchScalarGridSpec(
            num_scalar_prefetch=2,
            grid=(blocks // per_step,),
            in_specs=[row_spec, row_spec] + [anywhere] * len(arrived),
            out_specs=[row_spec, row_spec] + [anywhere] * len(back_shapes),
            scratch_shapes=[
                pltpu.VMEM((per_step, KV // PAIR, keys, 2 * GROUP * BLK), BF16),
                pltpu.VMEM((entries * BLK, 2 * KV), BF16),
                pltpu.VMEM((entries * BLK, 2 * KV), BF16),
                pltpu.SemaphoreType.DMA((entries,)),
                pltpu.SemaphoreType.DMA((entries,)),
            ],
        ),
        out_shape=[jax.ShapeDtypeStruct((width, rows), BF16)] * 2
        + [jax.ShapeDtypeStruct(shape, BF16) for shape in back_shapes],
        compiler_params=params(56),
        cost_estimate=pl.CostEstimate(
            flops=12 * pairs * HEAD_DIM, bytes_accessed=16 * rows * width, transcendentals=pairs
        ),
        name="attention",
    )(gets, puts, queries, normed_grad, *arrived)


def project_kernel(tokens_hbm, wk_hbm, wv_hbm, out_ref, tokens, wk, wv, sems):
    copies = []
    for src, dst, pieces in ((wk_hbm, wk, 2), (tokens_hbm, tokens, 4), (wv_hbm, wv, 2)):
        size = src.shape[0] // pieces
        for i in range(pieces):
            part = pl.ds(i * size, size)
            copies.append(
                pltpu.make_async_copy(src.at[part], dst.at[part], sems.at[len(copies)])
            )
    for copy in copies:
        copy.start()
    for copy in copies[:6]:
        copy.wait()
    keys = jnp.dot(tokens[...], wk[...], preferred_element_type=F32)
    out_ref[:, :KV] = keys.astype(BF16)
    for copy in copies[6:]:
        copy.wait()
    values = jnp.dot(tokens[...], wv[...], preferred_element_type=F32)
    out_ref[:, KV:] = values.astype(BF16)


def project(tokens, w_key, w_value):
    args = (tokens, w_key, w_value)
    return pl.pallas_call(
        project_kernel,
        in_specs=[pl.BlockSpec(memory_space=pl.ANY)] * 3,
        out_specs=WHOLE,
        out_shape=jax.ShapeDtypeStruct((tokens.shape[0], 2 * KV), BF16),
        scratch_shapes=[pltpu.VMEM(x.shape, BF16) for x in args]
        + [pltpu.SemaphoreType.DMA((8,))],
        compiler_params=params(56),
        name="project",
    )(*args)


def pack_kernel(first, wanted_ref, tile_ref, *outs):
    for i, out in enumerate(outs):
        for s in range(CAP):
            out[s] = tile_ref[jnp.maximum(wanted_ref[first + (i + 1) * CAP + s], 0)]


def pack(group, plane, wanted, tile):
    shape = (CAP,) + tile.shape[1:]
    return pl.pallas_call(
        functools.partial(pack_kernel, group * plane * CAP),
        in_specs=[pl.BlockSpec(memory_space=pltpu.SMEM), WHOLE],
        out_specs=[WHOLE] * (plane - 1),
        out_shape=[jax.ShapeDtypeStruct(shape, BF16)] * (plane - 1),
        compiler_params=params(16),
        name="pack",
    )(wanted, tile)


def finish_kernel(parts, *refs):
    term_ref, wk_ref, wv_ref, out_ref = refs[parts:]
    grad = refs[0][...].astype(F32)
    for ref in refs[1:parts]:
        grad += ref[...].astype(F32)
    grad = grad.astype(BF16)
    total = dot_nt(grad[:, :KV], wk_ref[...]) + dot_nt(grad[:, KV:], wv_ref[...])
    out_ref[...] = (term_ref[...] + total).astype(out_ref.dtype)


def finish(parts, term, w_key, w_value, kind, flops):
    return pl.pallas_call(
        functools.partial(finish_kernel, len(parts)),
        in_specs=[WHOLE] * (len(parts) + 3),
        out_specs=WHOLE,
        out_shape=jax.ShapeDtypeStruct(term.shape, kind),
        compiler_params=params(24),
        cost_estimate=pl.CostEstimate(
            flops=flops, bytes_accessed=4 * term.size, transcendentals=0
        ),
        name="finish",
    )(*parts, term, w_key, w_value)


def owner_kernel(first, wanted_ref, *refs):
    parts, (out_ref, total) = refs[:-2], refs[-2:]
    total[...] = jnp.zeros_like(total)
    for p, part in enumerate(parts):
        for s in range(CAP):
            block = wanted_ref[first + p * CAP + s]

            @pl.when(block >= 0)
            def _():
                total[block] += part[s].astype(F32)

    out_ref[...] = total[...].astype(out_ref.dtype)


def owner_sum(group, wanted, parts, blocks, kind, flops):
    shape = (blocks,) + parts[0].shape[1:]
    return pl.pallas_call(
        functools.partial(owner_kernel, group * len(parts) * CAP),
        in_specs=[pl.BlockSpec(memory_space=pltpu.SMEM)] + [WHOLE] * len(parts),
        out_specs=WHOLE,
        out_shape=jax.ShapeDtypeStruct(shape, kind),
        scratch_shapes=[pltpu.VMEM(shape, F32)],
        compiler_params=params(16),
        cost_estimate=pl.CostEstimate(
            flops=flops, bytes_accessed=4 * parts[0].size, transcendentals=0
        ),
        name="owner_sum",
    )(wanted, *parts)


def shards(patches, out_grad, w_query, w_key, w_value, w_out, key_tiles, key_blocks):
    tokens = patches[0]
    rows = tokens.shape[0]
    tile_count = lax.axis_size("tile")
    plane = tile_count // MAJOR
    my_tile = lax.axis_index("tile")
    my_row, my_place = my_tile // plane, my_tile % plane
    block_count = rows // BLK
    list_len = key_tiles.shape[2]
    entry_count = block_count * list_len

    def swap(value, d, cross):
        pairs = [
            (v * tile_count + t, (v ^ cross) * tile_count + (t // plane ^ d) * plane + t % plane)
            for v in range(2)
            for t in range(tile_count)
        ]
        return lax.ppermute(value, ("vintage", "tile"), pairs)

    def after(value, earlier):
        return lax.optimization_barrier((value, earlier))[0]

    def spread(values, earlier=None):
        moved = []
        for i, value in enumerate(values):
            pairs = [(t, t // plane * plane + (t % plane ^ (i + 1))) for t in range(tile_count)]
            if earlier is not None:
                value = after(value, earlier[i])
            moved.append(lax.ppermute(value, "tile", pairs))
        return moved

    def plane_rows(table, row):
        table = table[0].reshape(MAJOR, plane, entry_count)
        return lax.dynamic_index_in_dim(table, row, 0, keepdims=False)

    def mine_of(table):
        return lax.dynamic_index_in_dim(table, my_place, 0, keepdims=False)

    earlier = jnp.arange(entry_count)[:, None] > jnp.arange(entry_count)[None, :]

    def ranked(tiles):
        same = (tiles[:, :, None] == tiles[:, None, :]) & earlier[None]
        return jnp.sum(same.astype(jnp.int32), axis=2)

    def asked(slots, count, picks, valid):
        ids = jnp.arange(count, dtype=jnp.int32)
        hits = (slots[:, None, :] == ids[None, :, None]) & valid[:, None, :]
        found = jnp.sum(jnp.where(hits, picks[:, None, :] + 1, 0), axis=2) - 1
        return found[jnp.arange(plane) ^ my_place]

    tiles, picks = plane_rows(key_tiles, my_row), plane_rows(key_blocks, my_row)
    ranks = ranked(tiles)
    groups, columns = (tiles // plane) ^ my_row, tiles % plane
    my_group, my_peer, my_rank = mine_of(groups), mine_of(columns) ^ my_place, mine_of(ranks)
    gets = (my_group * plane + my_peer) * CODE + jnp.where(my_peer == 0, mine_of(picks), my_rank)
    puts = jnp.where(
        my_group == 1,
        3 * plane * CODE + my_peer * CAP + my_rank,
        (jnp.maximum(my_group - 1, 0) * plane + my_peer) * CODE + my_rank,
    )
    wanted = asked(groups * CAP + ranks, MAJOR * CAP, picks, columns == my_place)
    wanted = wanted.reshape(plane, MAJOR, CAP).transpose(1, 0, 2).reshape(-1)
    tiles, picks = plane_rows(key_tiles, my_row ^ 1), plane_rows(key_blocks, my_row ^ 1)
    beside_wanted = asked(ranked(tiles), CAP, picks, tiles == my_tile).reshape(-1)
    own_wanted = jnp.concatenate([wanted[: plane * CAP], beside_wanted])

    mine = project(tokens, w_key, w_value).reshape(block_count, BLK, 2 * KV)
    next_tile = swap(mine, 1, 1)
    own_tile = swap(mine, 0, 1)
    far_tile = swap(after(mine, own_tile), 2, 1)
    own = spread(pack(0, plane, wanted, own_tile))
    beside = spread(pack(1, plane, wanted, next_tile), own)
    last_tile = swap(after(far_tile, own[-1]), 1, 0)
    far = spread(pack(2, plane, wanted, after(far_tile, own[-1])), beside)
    last = spread(pack(3, plane, wanted, last_tile), far)
    arrived = [own_tile, *own, next_tile, *beside, far_tile, *far, last_tile, *last]
    queries = lax.dot_general(
        w_query, tokens, (((0,), (1,)), ((), ())), preferred_element_type=F32
    ).astype(BF16)
    normed_grad = dot_nt(w_out, out_grad[0])
    slot_shape = (CAP, BLK, 2 * KV)
    back_shapes = [slot_shape] * (3 * plane) + [(plane * CAP, BLK, 2 * KV)]
    normed_low, query_grad, *back = attention(
        gets, puts, queries, normed_grad, arrived, list_len, back_shapes
    )
    hopped = swap(back[3 * plane], 1, 0)
    back = [back[d * plane : (d + 1) * plane] for d in range(3)]
    layer_out = dot_tn(normed_low, w_out).astype(BF16)
    query_term = lax.dot_general(
        query_grad, w_query, (((0,), (1,)), ((), ())), preferred_element_type=F32
    )
    last = spread(back[2][1:])
    last[1], query_term, layer_out = lax.optimization_barrier((last[1], query_term, layer_out))
    far = spread(back[1][1:], last)
    last_sum = owner_sum(3, wanted, [back[2][0], *last], block_count, BF16, 0)
    last_sum = swap(last_sum, 1, 0).astype(F32)
    beside = [hopped[p * CAP : (p + 1) * CAP] for p in range(plane)]
    far[0], *beside = lax.optimization_barrier((far[0], *beside))
    far_sum = owner_sum(2, wanted, [back[1][0], *far], block_count, BF16, FAR_SUM_FLOPS)
    far_sum = (far_sum.astype(F32) + last_sum).astype(BF16)
    own = spread(back[0][1:], far)
    beside = [beside[0], *spread([after(x, far_sum) for x in beside[1:]], own)]
    own_sum = owner_sum(0, own_wanted, [back[0][0], *own, *beside], block_count, BF16, 0)
    far_grad, own_grad = swap(far_sum, 2, 1), swap(own_sum, 0, 1)
    query_term = finish(
        [far_grad.reshape(rows, 2 * KV)], query_term, w_key, w_value, F32, FAR_FLOPS
    )
    input_grad = finish(
        [own_grad.reshape(rows, 2 * KV)], query_term, w_key, w_value, BF16, 800_000_000
    )
    return (layer_out[None], input_grad[None])


def solution(mesh):
    in_specs = (
        P("vintage", "tile", None),
        P("vintage", "tile", None),
        P(),
        P(),
        P(),
        P(),
        P("vintage", None, None),
        P("vintage", None, None),
    )
    out_specs = (P("vintage", "tile", None), P("vintage", "tile", None))
    return jax.shard_map(shards, mesh=mesh, in_specs=in_specs, out_specs=out_specs, check_vma=False)
```

```python
import functools

import jax
import jax.numpy as jnp
from jax import lax
from jax.experimental import pallas as pl
from jax.experimental.pallas import tpu as pltpu
from jax.sharding import PartitionSpec as P

HEADS = 12
KV_HEADS = 4
HEAD_DIM = 64
BLK = 128
CAP = 2
GROUP = HEADS // KV_HEADS
KV = KV_HEADS * HEAD_DIM
PAIR = 2 * HEAD_DIM
CODE = 64
FAR_SUM_FLOPS = 5_000_000_000
FAR_FLOPS = 20_000_000_000
MAJOR = 4
TEMPER = HEAD_DIM ** (-0.5)
EPSILON = 1e-06
WHOLE = pl.BlockSpec(memory_space=pltpu.VMEM)
F32 = jnp.float32
BF16 = jnp.bfloat16


def params(mebibytes):
    return pltpu.CompilerParams(vmem_limit_bytes=mebibytes * 1024 * 1024)


def dot_nt(a, b):
    return lax.dot_general(a, b, (((1,), (1,)), ((), ())), preferred_element_type=F32)


def dot_tn(a, b):
    return lax.dot_general(a, b, (((0,), (0,)), ((), ())), preferred_element_type=F32)


def feature_heads(features, g):
    first = g * GROUP
    return jnp.concatenate(
        [features[(first + r) * HEAD_DIM : (first + r + 1) * HEAD_DIM] for r in range(GROUP)],
        axis=1,
    )


def two_groups(features, j):
    low, high = feature_heads(features, 2 * j), feature_heads(features, 2 * j + 1)
    zeros = jnp.zeros_like(low)
    return jnp.concatenate(
        [jnp.concatenate([low, zeros], axis=1), jnp.concatenate([zeros, high], axis=1)], axis=0
    )


def head_rows(pair_out):
    heads = []
    for i in range(2 * GROUP):
        top = i // GROUP * HEAD_DIM
        heads.append(pair_out[top : top + HEAD_DIM, i * BLK : (i + 1) * BLK])
    return jnp.concatenate(heads, axis=0)


def attention_kernel(list_len, per_step, sources, get_ref, put_ref, q_ref, ng_ref, *refs):
    expo_scr, kv_scr, parts_scr, in_sems, out_sems = refs[-5:]
    arrived, (normed_ref, qg_ref) = refs[:sources], refs[sources : sources + 2]
    back = refs[sources + 2 : -5]
    step = pl.program_id(0)
    entries = in_sems.shape[0]

    def rows_of(e):
        return pl.ds(pl.multiple_of(e * BLK, BLK), BLK)

    def fetch(e, source, slot):
        return pltpu.make_async_copy(
            arrived[source].at[slot], kv_scr.at[rows_of(e)], in_sems.at[e]
        )

    def give(e, source, slot):
        return pltpu.make_async_copy(
            parts_scr.at[rows_of(e)], back[source].at[slot], out_sems.at[e]
        )

    def start(copy, places, code_ref, begin, count):
        def one(i, carry):
            e = begin + i
            code = code_ref[e]
            for source in range(places):

                @pl.when(code // CODE == source)
                def _():
                    copy(e, source, code % CODE).start()

            return carry

        lax.fori_loop(0, count, one, 0)

    @pl.when(step == 0)
    def _():
        start(fetch, len(arrived), get_ref, 0, entries)

    first = step * per_step * list_len
    for i in range(per_step * list_len):
        fetch(first + i, 0, 0).wait()
    pairs = range(KV // PAIR)
    keys, values, wide, scores, exact, scales, grads, overlap, prob_grads = (
        {} for _ in range(9)
    )

    def rows_at(b):
        size = list_len * BLK
        return pl.ds(pl.multiple_of((step * per_step + b) * size, size), size)

    def cols_at(b):
        return slice(b * BLK, (b + 1) * BLK)

    def score(b):
        here = rows_at(b)
        queries = q_ref[:, cols_at(b)] * jnp.asarray(TEMPER, BF16)
        for j in pairs:
            keys[b, j] = kv_scr[here, j * PAIR : (j + 1) * PAIR]
            values[b, j] = kv_scr[here, KV + j * PAIR : KV + (j + 1) * PAIR]
            wide[b, j] = two_groups(queries, j)
            scores[b, j] = jnp.dot(keys[b, j], wide[b, j], preferred_element_type=F32)

    def soften(b, j):
        expo = jnp.exp(scores[b, j] - jnp.max(scores[b, j], axis=0, keepdims=True))
        scale = 1.0 / jnp.sum(expo, axis=0, keepdims=True)
        expo_scr[b, j] = expo.astype(BF16)
        exact[b, j] = head_rows(dot_tn(values[b, j], expo_scr[b, j]) * scale)
        scales[b, j] = jnp.concatenate(
            [
                jnp.broadcast_to(scale[:, i * BLK : (i + 1) * BLK], (HEAD_DIM, BLK))
                for i in range(2 * GROUP)
            ],
            axis=0,
        )

    def normalise(b):
        whole = jnp.concatenate([exact[b, j] for j in pairs], axis=0)
        attended = whole.astype(BF16).astype(F32)
        width = attended.shape[0]
        square = jnp.sum(attended * attended, axis=0, keepdims=True) / width
        inverse = lax.rsqrt(square + EPSILON)
        normed = attended * inverse
        normed_ref[:, cols_at(b)] = normed.astype(BF16)
        normed_grad = ng_ref[:, cols_at(b)]
        shared = jnp.sum(normed_grad * normed, axis=0, keepdims=True) / width
        attended_grad = (normed_grad - normed * shared) * inverse
        scale = jnp.concatenate([scales[b, j] for j in pairs], axis=0)
        scaled_grad = (attended_grad * scale).astype(BF16)
        overlap[b] = scaled_grad.astype(F32) * whole
        for j in pairs:
            grads[b, j] = two_groups(scaled_grad, j)

    def regrade(b, j):
        prob_grads[b, j] = jnp.dot(values[b, j], grads[b, j], preferred_element_type=F32)

    def finish_pair(b, j):
        here = rows_at(b)
        heads = range(2 * GROUP * j, 2 * GROUP * (j + 1))
        row_dot = jnp.concatenate(
            [
                jnp.sum(overlap[b][h * HEAD_DIM : (h + 1) * HEAD_DIM], axis=0, keepdims=True)
                for h in heads
            ],
            axis=1,
        )
        expo = expo_scr[b, j]
        value_part = dot_nt(expo, grads[b, j])
        score_grad = (expo.astype(F32) * (prob_grads[b, j] - row_dot)).astype(BF16)
        query_grad = head_rows(dot_tn(keys[b, j], score_grad) * TEMPER).astype(BF16)
        qg_ref[heads.start * HEAD_DIM : heads.stop * HEAD_DIM, cols_at(b)] = query_grad
        key_part = dot_nt(score_grad, wide[b, j])
        parts_scr[here, j * PAIR : (j + 1) * PAIR] = key_part.astype(BF16)
        parts_scr[here, KV + j * PAIR : KV + (j + 1) * PAIR] = value_part.astype(BF16)

    for b in range(per_step):
        score(b)
    for j in pairs:
        soften(0, j)
    normalise(0)
    for b in range(per_step):
        for j in pairs:
            regrade(b, j)
            if b + 1 < per_step:
                soften(b + 1, j)
        for j in pairs:
            finish_pair(b, j)
            if b + 1 < per_step and j == 0:
                normalise(b + 1)
    start(give, len(back), put_ref, first, per_step * list_len)

    @pl.when(step == pl.num_programs(0) - 1)
    def _():
        for e in range(entries):
            give(e, 0, 0).wait()


def attention(gets, puts, queries, normed_grad, arrived, list_len, back_shapes):
    width, rows = queries.shape
    blocks = rows // BLK
    entries = blocks * list_len
    per_step = 2 if list_len <= 4 and blocks % 2 == 0 else 1
    row_spec = pl.BlockSpec((width, per_step * BLK), lambda r, g, p: (0, r))
    anywhere = pl.BlockSpec(memory_space=pl.ANY)
    keys = list_len * BLK
    pairs = HEADS * rows * keys
    return pl.pallas_call(
        functools.partial(attention_kernel, list_len, per_step, len(arrived)),
        grid_spec=pltpu.PrefetchScalarGridSpec(
            num_scalar_prefetch=2,
            grid=(blocks // per_step,),
            in_specs=[row_spec, row_spec] + [anywhere] * len(arrived),
            out_specs=[row_spec, row_spec] + [anywhere] * len(back_shapes),
            scratch_shapes=[
                pltpu.VMEM((per_step, KV // PAIR, keys, 2 * GROUP * BLK), BF16),
                pltpu.VMEM((entries * BLK, 2 * KV), BF16),
                pltpu.VMEM((entries * BLK, 2 * KV), BF16),
                pltpu.SemaphoreType.DMA((entries,)),
                pltpu.SemaphoreType.DMA((entries,)),
            ],
        ),
        out_shape=[jax.ShapeDtypeStruct((width, rows), BF16)] * 2
        + [jax.ShapeDtypeStruct(shape, BF16) for shape in back_shapes],
        compiler_params=params(56),
        cost_estimate=pl.CostEstimate(
            flops=12 * pairs * HEAD_DIM, bytes_accessed=16 * rows * width, transcendentals=pairs
        ),
        name="attention",
    )(gets, puts, queries, normed_grad, *arrived)


def pack_kernel(first, wanted_ref, tile_ref, *outs):
    for i, out in enumerate(outs):
        for s in range(CAP):
            out[s] = tile_ref[jnp.maximum(wanted_ref[first + (i + 1) * CAP + s], 0)]


def pack(group, plane, wanted, tile):
    shape = (CAP,) + tile.shape[1:]
    return pl.pallas_call(
        functools.partial(pack_kernel, group * plane * CAP),
        in_specs=[pl.BlockSpec(memory_space=pltpu.SMEM), WHOLE],
        out_specs=[WHOLE] * (plane - 1),
        out_shape=[jax.ShapeDtypeStruct(shape, BF16)] * (plane - 1),
        compiler_params=params(16),
        name="pack",
    )(wanted, tile)


def finish_kernel(parts, *refs):
    term_ref, wk_ref, wv_ref, out_ref = refs[parts:]
    grad = refs[0][...].astype(F32)
    for ref in refs[1:parts]:
        grad += ref[...].astype(F32)
    grad = grad.astype(BF16)
    total = dot_nt(grad[:, :KV], wk_ref[...]) + dot_nt(grad[:, KV:], wv_ref[...])
    out_ref[...] = (term_ref[...] + total).astype(out_ref.dtype)


def finish(parts, term, w_key, w_value, kind, flops):
    return pl.pallas_call(
        functools.partial(finish_kernel, len(parts)),
        in_specs=[WHOLE] * (len(parts) + 3),
        out_specs=WHOLE,
        out_shape=jax.ShapeDtypeStruct(term.shape, kind),
        compiler_params=params(24),
        cost_estimate=pl.CostEstimate(
            flops=flops, bytes_accessed=4 * term.size, transcendentals=0
        ),
        name="finish",
    )(*parts, term, w_key, w_value)


def owner_kernel(first, wanted_ref, *refs):
    parts, (out_ref, total) = refs[:-2], refs[-2:]
    total[...] = jnp.zeros_like(total)
    for p, part in enumerate(parts):
        for s in range(CAP):
            block = wanted_ref[first + p * CAP + s]

            @pl.when(block >= 0)
            def _():
                total[block] += part[s].astype(F32)

    out_ref[...] = total[...].astype(out_ref.dtype)


def owner_sum(group, wanted, parts, blocks, kind, flops):
    shape = (blocks,) + parts[0].shape[1:]
    return pl.pallas_call(
        functools.partial(owner_kernel, group * len(parts) * CAP),
        in_specs=[pl.BlockSpec(memory_space=pltpu.SMEM)] + [WHOLE] * len(parts),
        out_specs=WHOLE,
        out_shape=jax.ShapeDtypeStruct(shape, kind),
        scratch_shapes=[pltpu.VMEM(shape, F32)],
        compiler_params=params(16),
        cost_estimate=pl.CostEstimate(
            flops=flops, bytes_accessed=4 * parts[0].size, transcendentals=0
        ),
        name="owner_sum",
    )(wanted, *parts)


def shards(patches, out_grad, w_query, w_key, w_value, w_out, key_tiles, key_blocks):
    tokens = patches[0]
    rows = tokens.shape[0]
    tile_count = lax.axis_size("tile")
    plane = tile_count // MAJOR
    my_tile = lax.axis_index("tile")
    my_row, my_place = my_tile // plane, my_tile % plane
    block_count = rows // BLK
    list_len = key_tiles.shape[2]
    entry_count = block_count * list_len

    def swap(value, d, cross):
        pairs = [
            (v * tile_count + t, (v ^ cross) * tile_count + (t // plane ^ d) * plane + t % plane)
            for v in range(2)
            for t in range(tile_count)
        ]
        return lax.ppermute(value, ("vintage", "tile"), pairs)

    def after(value, earlier):
        return lax.optimization_barrier((value, earlier))[0]

    def spread(values, earlier=None):
        moved = []
        for i, value in enumerate(values):
            pairs = [(t, t // plane * plane + (t % plane ^ (i + 1))) for t in range(tile_count)]
            if earlier is not None:
                value = after(value, earlier[i])
            moved.append(lax.ppermute(value, "tile", pairs))
        return moved

    def plane_rows(table, row):
        table = table[0].reshape(MAJOR, plane, entry_count)
        return lax.dynamic_index_in_dim(table, row, 0, keepdims=False)

    def mine_of(table):
        return lax.dynamic_index_in_dim(table, my_place, 0, keepdims=False)

    earlier = jnp.arange(entry_count)[:, None] > jnp.arange(entry_count)[None, :]

    def ranked(tiles):
        same = (tiles[:, :, None] == tiles[:, None, :]) & earlier[None]
        return jnp.sum(same.astype(jnp.int32), axis=2)

    def asked(slots, count, picks, valid):
        ids = jnp.arange(count, dtype=jnp.int32)
        hits = (slots[:, None, :] == ids[None, :, None]) & valid[:, None, :]
        found = jnp.sum(jnp.where(hits, picks[:, None, :] + 1, 0), axis=2) - 1
        return found[jnp.arange(plane) ^ my_place]

    tiles, picks = plane_rows(key_tiles, my_row), plane_rows(key_blocks, my_row)
    ranks = ranked(tiles)
    groups, columns = (tiles // plane) ^ my_row, tiles % plane
    my_group, my_peer, my_rank = mine_of(groups), mine_of(columns) ^ my_place, mine_of(ranks)
    gets = (my_group * plane + my_peer) * CODE + jnp.where(my_peer == 0, mine_of(picks), my_rank)
    puts = jnp.where(
        my_group == 1,
        3 * plane * CODE + my_peer * CAP + my_rank,
        (jnp.maximum(my_group - 1, 0) * plane + my_peer) * CODE + my_rank,
    )
    wanted = asked(groups * CAP + ranks, MAJOR * CAP, picks, columns == my_place)
    wanted = wanted.reshape(plane, MAJOR, CAP).transpose(1, 0, 2).reshape(-1)
    tiles, picks = plane_rows(key_tiles, my_row ^ 1), plane_rows(key_blocks, my_row ^ 1)
    beside_wanted = asked(ranked(tiles), CAP, picks, tiles == my_tile).reshape(-1)
    own_wanted = jnp.concatenate([wanted[: plane * CAP], beside_wanted])

    keys = jnp.dot(tokens, w_key, preferred_element_type=F32).astype(BF16)
    values = jnp.dot(tokens, w_value, preferred_element_type=F32).astype(BF16)
    mine = jnp.concatenate([keys, values], axis=-1).reshape(block_count, BLK, 2 * KV)
    next_tile = swap(mine, 1, 1)
    own_tile = swap(mine, 0, 1)
    far_tile = swap(after(mine, own_tile), 2, 1)
    own = spread(pack(0, plane, wanted, own_tile))
    beside = spread(pack(1, plane, wanted, next_tile), own)
    last_tile = swap(after(far_tile, own[-1]), 1, 0)
    far = spread(pack(2, plane, wanted, after(far_tile, own[-1])), beside)
    last = spread(pack(3, plane, wanted, last_tile), far)
    arrived = [own_tile, *own, next_tile, *beside, far_tile, *far, last_tile, *last]
    queries = lax.dot_general(
        w_query, tokens, (((0,), (1,)), ((), ())), preferred_element_type=F32
    ).astype(BF16)
    normed_grad = dot_nt(w_out, out_grad[0])
    slot_shape = (CAP, BLK, 2 * KV)
    back_shapes = [slot_shape] * (3 * plane) + [(plane * CAP, BLK, 2 * KV)]
    normed_low, query_grad, *back = attention(
        gets, puts, queries, normed_grad, arrived, list_len, back_shapes
    )
    hopped = swap(back[3 * plane], 1, 0)
    back = [back[d * plane : (d + 1) * plane] for d in range(3)]
    layer_out = dot_tn(normed_low, w_out).astype(BF16)
    query_term = lax.dot_general(
        query_grad, w_query, (((0,), (1,)), ((), ())), preferred_element_type=F32
    )
    last = spread(back[2][1:])
    last[1], query_term, layer_out = lax.optimization_barrier((last[1], query_term, layer_out))
    far = spread(back[1][1:], last)
    last_sum = owner_sum(3, wanted, [back[2][0], *last], block_count, BF16, 0)
    last_sum = swap(last_sum, 1, 0).astype(F32)
    beside = [hopped[p * CAP : (p + 1) * CAP] for p in range(plane)]
    far[0], *beside = lax.optimization_barrier((far[0], *beside))
    far_sum = owner_sum(2, wanted, [back[1][0], *far], block_count, BF16, FAR_SUM_FLOPS)
    far_sum = (far_sum.astype(F32) + last_sum).astype(BF16)
    own = spread(back[0][1:], far)
    beside = [beside[0], *spread([after(x, far_sum) for x in beside[1:]], own)]
    own_sum = owner_sum(0, own_wanted, [back[0][0], *own, *beside], block_count, BF16, 0)
    far_grad, own_grad = swap(far_sum, 2, 1), swap(own_sum, 0, 1)
    query_term = finish(
        [far_grad.reshape(rows, 2 * KV)], query_term, w_key, w_value, F32, FAR_FLOPS
    )
    input_grad = finish(
        [own_grad.reshape(rows, 2 * KV)], query_term, w_key, w_value, BF16, 800_000_000
    )
    return (layer_out[None], input_grad[None])


def solution(mesh):
    in_specs = (
        P("vintage", "tile", None),
        P("vintage", "tile", None),
        P(),
        P(),
        P(),
        P(),
        P("vintage", None, None),
        P("vintage", None, None),
    )
    out_specs = (P("vintage", "tile", None), P("vintage", "tile", None))
    return jax.shard_map(shards, mesh=mesh, in_specs=in_specs, out_specs=out_specs, check_vma=False)
```
